32 devices in a mesh: wide: 16 (over z, y, x), narrow: 2 (over core).
Axes of the slice: x: 2, y: 2, z: 4, core: 2. Of those that a mesh axis runs over, the one named last changes fastest.
Arguments:
- layer_input: bfloat16 [8192, 2048], P(('wide', 'narrow')), may hold values from -6 to 6
- doc_lengths: int32 [16, 4], P('wide'), may hold values from 1 to 256, 512 in all within a row
- w_query: bfloat16 [2048, 2048], P('wide', 'narrow'), may hold values from -0.125 to 0.125
- w_key: bfloat16 [2048, 2048], P('wide', 'narrow'), may hold values from -0.125 to 0.125
- w_value: bfloat16 [2048, 2048], P('wide', 'narrow'), may hold values from -0.125 to 0.125
- w_gate: bfloat16 [2048, 2048], P('wide', 'narrow'), may hold values from -0.125 to 0.125
- w_output: bfloat16 [2048, 2048], P('wide', 'narrow'), may hold values from -0.125 to 0.125
- w_left: bfloat16 [2048, 5632], P('wide', 'narrow'), may hold values from -0.125 to 0.125
- w_right: bfloat16 [2048, 5632], P('wide', 'narrow'), may hold values from -0.125 to 0.125
- w_down: bfloat16 [2048, 5632], P('wide', 'narrow'), may hold values from -0.078125 to 0.078125
- cotangent: bfloat16 [8192, 2048], P(('wide', 'narrow')), may hold values from -6 to 6
Outputs:
- layer_output: bfloat16 [8192, 2048], P(('wide', 'narrow'))
- input_grad: float32 [8192, 2048], P(('wide', 'narrow'))
- grad_query: float32 [2048, 2048], P('wide', 'narrow')
- grad_key: float32 [2048, 2048], P('wide', 'narrow')
- grad_value: float32 [2048, 2048], P('wide', 'narrow')
- grad_gate: float32 [2048, 2048], P('wide', 'narrow')
- grad_output: float32 [2048, 2048], P('wide', 'narrow')
- grad_left: float32 [2048, 5632], P('wide', 'narrow')
- grad_right: float32 [2048, 5632], P('wide', 'narrow')
- grad_down: float32 [2048, 5632], P('wide', 'narrow')
The draws below stay inside these ranges and needn't reach their ends.
Inputs may be any that keep to these rules, and one draw needn't show every extreme that they name: `doc_lengths`: in each packed row the 4 lengths add up to 512, the documents lying along the row in this order; the longest of every row has 256 tokens.
All inputs are finite; a program needn't handle non-finite values.
Results may differ from the reference program's by a relative error of at most 0.014.
Values may be sent and summed in bfloat16 or wider, within the bound.
A program may use at most 256 MiB of HBM per device.

```python
import math
import jax
import jax.numpy as jnp
import numpy as np
from jax import lax

D = 2048
HEADS = 16
HEAD_DIM = 128
FF = 5632
ROW_LEN = 512
NDOCS = 4
DOC_MOST = 256
ROWS = 16
TOKENS = 8192


def spiked(drawn, stream_key, source, target, parts, factor):
    def block_of(position):
        return (jnp.arange(drawn.shape[position]) // (drawn.shape[position] // parts)).reshape((-1,) + (1,) * (drawn.ndim - 1 - position))

    near = jax.random.permutation(stream_key, parts)[block_of(target)]
    other_side = (block_of(target) + parts // 2) % parts
    return jnp.where((block_of(source) == near) | (block_of(source) == other_side), factor * drawn, drawn)


def block_scale(rng, extent, cuts, least, top_value):
    level, own = 1.0, jax.random.fold_in(rng, 6)
    for axis_at, shards_of in cuts:
        steps = jnp.exp(jax.random.uniform(jax.random.fold_in(own, axis_at), (shards_of,), jnp.float32, least / len(cuts), top_value / len(cuts)))
        level = level * jnp.repeat(steps, extent[axis_at] // shards_of).reshape([-1 if axis == axis_at else 1 for axis in range(len(extent))])
    return level


def split_up(count, total, limit, lean):
    portions = [(1 << 20) // math.isqrt(standing ** lean) + 1 for standing in range(2, count + 1)]
    surplus, holding = total - limit - (count - 1), [1] * (count - 1)
    while surplus > 0:
        movable = [i for i in range(count - 1) if holding[i] < limit]
        mass, left = sum([portions[i] for i in movable]), surplus
        for i in movable:
            more = min(limit - holding[i], max(1, left * portions[i] // mass), surplus)
            holding[i] = holding[i] + more
            surplus = surplus - more
    return np.array([limit] + holding)


def ragged(key, number_of, total, most, skew):
    if number_of == 2:
        one = jax.random.randint(key, (), max(1, total - most), min(most, total - 1) + 1)
        return jnp.stack([one, total - one])
    sizes = jnp.asarray(split_up(number_of, total, most, skew), jnp.int32)
    pairs = (number_of - 1) // 2
    source_of, sink = sizes[1:1 + 2 * pairs:2], sizes[2:2 + 2 * pairs:2]
    slack = jnp.minimum(source_of - 1, most - sink)
    shifted = jax.random.randint(jax.random.fold_in(key, 1), (pairs,), 0, 1 << 20) % (slack + 1)
    sizes = sizes.at[1:1 + 2 * pairs:2].set(source_of - shifted).at[2:2 + 2 * pairs:2].set(sink + shifted)
    return sizes[jax.random.permutation(jax.random.fold_in(key, 2), number_of)]


def normal_values(own_key, dims, width, most, cuts=(), kind=jnp.bfloat16):
    values = jax.random.normal(own_key, dims, jnp.float32) * width
    if len(cuts) > 0:
        values = block_scale(own_key, dims, cuts, -0.22, 0.18) * values
    return jnp.clip(values, min=-most, max=most).astype(kind)


def bell_draw_with(stream_key, shape, scale, bound, pieces, heavy, held_as=jnp.bfloat16):
    values = scale * jax.random.normal(stream_key, shape, jnp.float32)
    if pieces:
        values = values * block_scale(stream_key, shape, pieces, -0.22, 0.18)
    return jnp.clip(spiked(values, jax.random.fold_in(stream_key, 3), *heavy), -bound, bound).astype(held_as)


def setup_inputs(seed: int = 0) -> dict:
    key_of = jax.random.split(jax.random.key(seed), 12)
    return {
        "layer_input": bell_draw_with(key_of[0], (TOKENS, D), 1.0, 6.0, ((0, 32),), (0, 1, 32, 2.75)),
        "doc_lengths": jax.vmap(lambda own: ragged(own, NDOCS, ROW_LEN, DOC_MOST, 2))(jax.random.split(key_of[1], ROWS)).reshape((ROWS, NDOCS)).astype(jnp.int32),
        "w_query": normal_values(key_of[2], (D, D), D ** -0.5, 0.125, ((0, 16), (1, 2))),
        "w_key": normal_values(key_of[3], (D, D), D ** -0.5, 0.125, ((0, 16), (1, 2))),
        "w_value": normal_values(key_of[4], (D, D), D ** -0.5, 0.125, ((0, 16), (1, 2))),
        "w_gate": normal_values(key_of[5], (D, D), D ** -0.5, 0.125, ((0, 16), (1, 2))),
        "w_output": normal_values(key_of[6], (D, D), D ** -0.5, 0.125, ((0, 16), (1, 2))),
        "w_left": normal_values(key_of[7], (D, FF), D ** -0.5, 0.125, ((0, 16), (1, 2))),
        "w_right": normal_values(key_of[8], (D, FF), D ** -0.5, 0.125, ((0, 16), (1, 2))),
        "w_down": normal_values(key_of[9], (D, FF), FF ** -0.5, 0.078125, ((0, 16), (1, 2))),
        "cotangent": bell_draw_with(key_of[10], (TOKENS, D), 1.0, 6.0, ((0, 32),), (0, 1, 32, 2.75)),
    }


epsilon = 1e-06
decay_scale = 2.0
highest = lax.Precision.HIGHEST

@jax.custom_vjp
def low(v):
    return lax.optimization_barrier(v.astype(jnp.bfloat16)).astype(jnp.float32)

@jax.custom_vjp
def low_back(v):
    return v

def low_keep(v):
    return (low(v), None)

def low_pass(kept, grad):
    return (grad,)

def back_keep(v):
    return (v, None)

def back_low(kept, grad):
    return (low(grad),)
low.defvjp(low_keep, low_pass)
low_back.defvjp(back_keep, back_low)

def simple_norm(values):
    return values * lax.rsqrt(lax.optimization_barrier(jnp.mean(values * values, axis=-1, keepdims=True)) + epsilon)

def decay_mask(lengths, head_ids):
    starts = jnp.cumsum(lengths) - lengths
    places = jnp.arange(ROW_LEN, dtype=jnp.int32)
    doc_ids = lax.optimization_barrier(jnp.sum((places[:, None] >= starts[None, :]).astype(jnp.int32), axis=1))
    causal = places[:, None] >= places[None, :]
    allowed = causal & (doc_ids[:, None] == doc_ids[None, :])
    spread = jnp.where(causal, (places[:, None] - places[None, :]).astype(jnp.float32), jnp.float32(0.0))
    head_rates = decay_scale * head_ids.astype(jnp.float32) / HEADS
    weights = jnp.exp(-head_rates[:, None, None] * spread[None, :, :])
    return jnp.where(allowed[None, :, :], weights, jnp.float32(0.0))

def attend_row(row_parts):
    queries, keys_row, values_row, lengths = row_parts
    decay_masks = decay_mask(lengths, jnp.arange(HEADS, dtype=jnp.int32))
    scores = low_back(jnp.einsum('ihd,jhd->hij', queries, keys_row, precision=highest))
    attn_probs = low(scores * decay_masks)
    return low_back(jnp.einsum('hij,jhd->ihd', attn_probs, values_row, precision=highest))

def layer_forward(inputs, w_query, w_key, w_value, w_gate, w_output, w_left, w_right, w_down, lengths):
    normed = low(simple_norm(inputs))
    queries = low(jax.nn.silu(low_back(jnp.dot(normed, w_query, precision=highest))))
    keys_all = low(jax.nn.silu(low_back(jnp.dot(normed, w_key, precision=highest))))
    values_all = low(low_back(jnp.dot(normed, w_value, precision=highest)))
    gate_all = low_back(jnp.dot(normed, w_gate, precision=highest))
    split_shape = (ROWS, ROW_LEN, HEADS, HEAD_DIM)
    mixed_out = lax.map(jax.checkpoint(attend_row), (queries.reshape(split_shape), keys_all.reshape(split_shape), values_all.reshape(split_shape), lengths))
    mixed_out = mixed_out.reshape(TOKENS, D)
    blended = low(gate_all * simple_norm(mixed_out))
    middle = inputs + low_back(jnp.dot(blended, w_output.T, precision=highest))
    mid_normed = low(simple_norm(middle))
    left_all = low_back(jnp.dot(mid_normed, w_left, precision=highest))
    right_all = low_back(jnp.dot(mid_normed, w_right, precision=highest))
    product = low(left_all * right_all)
    return middle + low_back(jnp.dot(product, w_down.T, precision=highest))

def reference(layer_input, doc_lengths, w_query, w_key, w_value, w_gate, w_output, w_left, w_right, w_down, cotangent):
    floats = [item.astype(jnp.float32) for item in (layer_input, w_query, w_key, w_value, w_gate, w_output, w_left, w_right, w_down)]

    def forward_only(inputs, query_w, key_w, value_w, gate_w, output_w, left_w, right_w, down_w):
        return layer_forward(inputs, query_w, key_w, value_w, gate_w, output_w, left_w, right_w, down_w, doc_lengths)
    result, pullback = jax.vjp(forward_only, floats[0], floats[1], floats[2], floats[3], floats[4], floats[5], floats[6], floats[7], floats[8])
    gradients = pullback(cotangent.astype(jnp.float32))
    return (result.astype(jnp.bfloat16), gradients[0], gradients[1], gradients[2], gradients[3], gradients[4], gradients[5], gradients[6], gradients[7], gradients[8])
```

```python
import jax
import jax.numpy as jnp
from jax import lax
from jax.sharding import PartitionSpec as P

HEAD_DIM = 128
LINE = 4
EPS = 1e-06
DECAY = 2.0
F32 = jnp.float32
BF16 = jnp.bfloat16


def mm(a, b, out=F32):
    return lax.dot_general(a, b, (((1,), (0,)), ((), ())), preferred_element_type=F32).astype(out)


def mm_t(a, b, out=F32):
    return lax.dot_general(a, b, (((1,), (1,)), ((), ())), preferred_element_type=F32).astype(out)


def t_mm(a, b, out=F32):
    return lax.dot_general(a, b, (((0,), (0,)), ((), ())), preferred_element_type=F32).astype(out)


def norm_scale_of(values):
    return lax.rsqrt(jnp.mean(values * values, axis=-1, keepdims=True) + EPS)


def norm_back(values, scale, gradient):
    inner = jnp.mean(gradient * values, axis=-1, keepdims=True)
    return scale * gradient - values * (scale * scale * scale) * inner


def after(value, *deps):
    return lax.optimization_barrier((value,) + deps)[0]


class Net:
    def __init__(self, wide):
        self.wide = wide
        self.me = lax.axis_index("wide")
        bits = wide.bit_length() - 1
        self.plane = [0, 1] + list(range(4, bits))
        self.n_plane = wide // LINE
        self.lines = [
            [base + 4 * k for k in range(LINE)] for base in range(wide) if not base & 12
        ]

    def flip(self, value, bit):
        return lax.ppermute(value, "wide", [(w, w ^ (1 << bit)) for w in range(self.wide)])

    def core(self, value):
        return lax.ppermute(value, "narrow", [(0, 1), (1, 0)])

    def line(self, value):
        return lax.all_to_all(
            value, "wide", 0, 0, axis_index_groups=self.lines, tiled=True
        )

    def permute(self, value):
        size = value.shape[1] // self.wide
        blocks = [value[:, i * size : (i + 1) * size] for i in range(self.wide)]
        blocks = self.swap(blocks)
        order = [self.index(m, z) for m in range(self.n_plane) for z in range(LINE)]
        return jnp.concatenate([blocks[i] for i in order], axis=1)

    def restore(self, value):
        size = value.shape[1] // self.wide
        blocks = [None] * self.wide
        for m in range(self.n_plane):
            for z in range(LINE):
                at = (m * LINE + z) * size
                blocks[self.index(m, z)] = value[:, at : at + size]
        return jnp.concatenate(self.swap(blocks), axis=1)

    def index(self, m, z):
        return z * 4 + sum(((m >> j) & 1) << bit for j, bit in enumerate(self.plane))

    def swap(self, blocks):
        for bit in self.plane:
            mine = ((self.me >> bit) & 1) == 1
            blocks = [
                jnp.where(mine, blocks[i ^ (1 << bit)], blocks[i])
                for i in range(len(blocks))
            ]
        return blocks

    def scatter_line(self, weight):
        rows, cols = weight.shape
        halves = [weight[:, : cols // 2], weight[:, cols // 2 :]]
        return self.line(jnp.stack([halves[z & 1] for z in range(LINE)]))

    def spread(self, block, turn):
        order = list(range(len(self.plane)))
        if turn:
            order = [1, 0] + order[2:]
        held = {0: block}
        for j in order:
            held.update({m | (1 << j): self.flip(b, self.plane[j]) for m, b in held.items()})
        return [held[m] for m in range(self.n_plane)]

    def gather(self, lined, turn, split):
        _, size, cols = lined.shape
        if split:
            cut = [self.spread(lined[:2], turn), self.spread(lined[2:], not turn)]
            parts = [p for pair in zip(*cut) for p in pair]
        else:
            parts = self.spread(lined, turn)
        return jnp.concatenate([p.reshape(-1, cols) for p in parts], axis=0)

    def fold(self, blocks, turn):
        order = list(range(len(self.plane)))
        if turn:
            order = [1, 0] + order[2:]
        held = {m: blocks[m] for m in range(self.n_plane)}
        for j in reversed(order):
            keep = [m for m in held if not (m >> j) & 1]
            sent = jnp.stack([held[m | (1 << j)] for m in keep])
            got = self.flip(sent, self.plane[j])
            held = {
                m: (held[m].astype(F32) + got[i].astype(F32)).astype(BF16)
                for i, m in enumerate(keep)
            }
        return held[0]

    def reduce(self, grad, turn, split):
        rows, cols = grad.shape
        size = rows // self.wide
        blocks = grad.reshape(self.n_plane, LINE, size, cols)
        if split:
            lined = jnp.concatenate(
                [self.fold(blocks[:, :2], turn), self.fold(blocks[:, 2:], not turn)]
            )
        else:
            lined = self.fold(blocks, turn)
        got = self.line(lined).astype(F32)
        return jnp.concatenate([got[0] + got[2], got[1] + got[3]], axis=1)

    def group_gather(self, value):
        near = self.core(value)
        far = self.flip(value, 2)
        return jnp.concatenate([value, near, far, self.core(far)], axis=0)

    def group_sum(self, value):
        quarter = value.shape[0] // 4
        b = value.reshape(4, quarter)
        got = self.core(b)
        b = b + jnp.concatenate([got[1:2], got[0:1], got[3:4], got[2:3]])
        got = self.flip(b, 2)
        return (b + jnp.concatenate([got[2:], got[:2]])).reshape(-1)

    def group_scatter(self, value):
        quarter = value.shape[0] // 4
        b = [value[i * quarter : (i + 1) * quarter] for i in range(4)]
        got = self.core(jnp.concatenate([b[1], b[3]]))
        far = (b[2].astype(F32) + got[quarter:].astype(F32)).astype(BF16)
        own = b[0].astype(F32) + got[:quarter].astype(F32)
        return own + self.flip(far, 2).astype(F32)


def masks(lengths, places, rates):
    starts, total = [], 0
    for c in range(lengths.shape[1] - 1):
        total = total + lengths[:, c]
        starts.append(total)
    starts = jnp.stack(starts, axis=1)
    docs = jnp.sum((places[None, :, None] >= starts[:, None, :]).astype(jnp.int32), axis=2)
    gap = places[:, None] - places[None, :]
    allowed = (gap >= 0)[None] & (docs[:, :, None] == docs[:, None, :])
    spread = jnp.maximum(gap, 0).astype(F32)
    weights = jnp.exp(-rates[:, None, None] * spread[None])
    return jnp.where(allowed[:, None], weights[None], 0.0)


def sigmoid(z):
    return 1.0 / (1.0 + jnp.exp(-z))


def on_device(
    layer_input, doc_lengths, w_query, w_key, w_value, w_gate, w_output, w_left, w_right, w_down, cotangent, *, wide
):
    net = Net(wide)
    core = lax.axis_index("narrow")
    half = (net.me >> 2) & 1
    features = layer_input.shape[1]

    weights = [w_query, w_key, w_value, w_gate, w_output, w_left, w_right, w_down]
    turns = [0, 1, 0, 1, 0, 0, 1, 0]
    splits = [0, 0, 0, 0, 0, 1, 1, 1]
    lined = []
    for i, w in enumerate(weights):
        if i >= 2:
            w = after(w, lined[i - 2])
        lined.append(net.scatter_line(w))
    full = [net.gather(x, t, s) for x, t, s in zip(lined, turns, splits)]
    query_w, key_w, value_w, gate_w, output_w, left_w, right_w, down_w = full

    inputs = net.permute(layer_input).astype(F32)
    norm_one = norm_scale_of(inputs)
    normed = net.group_gather((inputs * norm_one).astype(BF16))
    cot = net.permute(cotangent)
    cot_all = net.group_gather(cot)

    quarter = inputs.shape[0]
    tokens = 4 * quarter
    row_len = 2 * quarter
    width = query_w.shape[1]
    heads = width // HEAD_DIM
    all_heads = features // HEAD_DIM
    head_ids = (core * 2 + half) * heads + jnp.arange(heads, dtype=jnp.int32)
    rates = DECAY * head_ids.astype(F32) / all_heads
    own = jnp.arange(quarter, dtype=jnp.int32)
    places = jnp.concatenate([own + core * quarter, own + (1 - core) * quarter])
    lengths = jnp.concatenate([doc_lengths, net.flip(doc_lengths, 2)])
    decay = masks(lengths, places, rates)

    query_pre = mm(normed, query_w)
    key_pre = mm(normed, key_w)
    values = mm(normed, value_w, BF16)
    gate = mm(normed, gate_w)
    query_sig, key_sig = sigmoid(query_pre), sigmoid(key_pre)
    queries = (query_pre * query_sig).astype(BF16)
    keys = (key_pre * key_sig).astype(BF16)
    shape = (2, row_len, heads, HEAD_DIM)
    q4, k4, v4 = (a.reshape(shape) for a in (queries, keys, values))
    scores = jnp.einsum("rihd,rjhd->rhij", q4, k4, preferred_element_type=F32)
    probs = (scores * decay).astype(BF16)
    mixed = jnp.einsum("rhij,rjhd->rihd", probs, v4, preferred_element_type=F32)
    mixed = mixed.reshape(tokens, width)
    squares = net.group_sum(jnp.sum(mixed * mixed, axis=1))
    attn_scale = lax.rsqrt(squares / features + EPS)[:, None]
    scaled = mixed * attn_scale
    blended = (gate * scaled).astype(BF16)
    middle = inputs + net.group_scatter(mm_t(blended, output_w, BF16))
    norm_two = norm_scale_of(middle)
    mid = net.group_gather((middle * norm_two).astype(BF16))
    left = mm(mid, left_w)
    right = mm(mid, right_w)
    product = (left * right).astype(BF16)
    grad_down = net.reduce(t_mm(cot_all, product, BF16), 0, 1)

    layer_output = middle + net.group_scatter(mm_t(product, down_w, BF16))
    layer_output = net.restore(layer_output.astype(BF16))

    grad_product = mm(cot_all, down_w)
    grad_left_pre = (grad_product * right).astype(BF16)
    grad_right_pre = (grad_product * left).astype(BF16)
    grad_mid = net.group_scatter(
        (mm_t(grad_left_pre, left_w) + mm_t(grad_right_pre, right_w)).astype(BF16)
    )
    grad_left = net.reduce(t_mm(mid, grad_left_pre, BF16), 0, 1)
    grad_right = net.reduce(t_mm(mid, grad_right_pre, BF16), 1, 1)
    grad_middle = cot.astype(F32) + norm_back(middle, norm_two, grad_mid)
    branch = net.group_gather(grad_middle.astype(BF16))
    grad_blended = mm(branch, output_w)
    grad_output = net.reduce(t_mm(branch, blended, BF16), 0, 0)
    grad_gate_pre = (grad_blended * scaled).astype(BF16)
    grad_gate = net.reduce(t_mm(normed, grad_gate_pre, BF16), 1, 0)
    grad_scaled = grad_blended * gate
    inner = net.group_sum(jnp.sum(grad_scaled * mixed, axis=1)) / features
    grad_mixed = (
        attn_scale * grad_scaled - mixed * (attn_scale * attn_scale * attn_scale) * inner[:, None]
    ).astype(BF16)
    g4 = grad_mixed.reshape(shape)
    grad_probs = jnp.einsum("rihd,rjhd->rhij", g4, v4, preferred_element_type=F32)
    grad_values = jnp.einsum("rhij,rihd->rjhd", probs, g4, preferred_element_type=F32)
    grad_value_pre = grad_values.astype(BF16).reshape(tokens, width)
    grad_value = net.reduce(t_mm(normed, grad_value_pre, BF16), 0, 0)
    grad_scores = (grad_probs * decay).astype(BF16)
    grad_queries = jnp.einsum("rhij,rjhd->rihd", grad_scores, k4, preferred_element_type=F32)
    grad_keys = jnp.einsum("rhij,rihd->rjhd", grad_scores, q4, preferred_element_type=F32)
    grad_query_pre = (
        grad_queries.reshape(tokens, width) * (query_sig * (1.0 + query_pre * (1.0 - query_sig)))
    ).astype(BF16)
    grad_key_pre = (
        grad_keys.reshape(tokens, width) * (key_sig * (1.0 + key_pre * (1.0 - key_sig)))
    ).astype(BF16)
    grad_query = net.reduce(t_mm(normed, grad_query_pre, BF16), 1, 0)
    grad_key = net.reduce(t_mm(normed, grad_key_pre, BF16), 0, 0)
    total = mm_t(grad_gate_pre, gate_w) + mm_t(grad_value_pre, value_w)
    total = total + mm_t(grad_query_pre, query_w) + mm_t(grad_key_pre, key_w)
    grad_normed = net.group_scatter(total.astype(BF16))
    input_grad = net.restore(grad_middle + norm_back(inputs, norm_one, grad_normed))
    return (
        layer_output,
        input_grad,
        grad_query,
        grad_key,
        grad_value,
        grad_gate,
        grad_output,
        grad_left,
        grad_right,
        grad_down,
    )


def solution(mesh):
    both, weight = P(("wide", "narrow"), None), P("wide", "narrow")
    wide = mesh.shape["wide"]

    def body(*args):
        return on_device(*args, wide=wide)

    return jax.shard_map(
        body,
        mesh=mesh,
        in_specs=(both, P("wide", None)) + (weight,) * 8 + (both,),
        out_specs=(both, both) + (weight,) * 8,
        check_vma=False,
    )
```

```python
import functools

import jax
import jax.numpy as jnp
from jax import lax
from jax.experimental import pallas as pl
from jax.experimental.pallas import tpu as pltpu
from jax.sharding import PartitionSpec as P

HEAD_DIM = 128
LINE = 4
EPS = 1e-06
DECAY = 2.0
F32 = jnp.float32
BF16 = jnp.bfloat16


def mm(a, b, out=F32):
    return lax.dot_general(a, b, (((1,), (0,)), ((), ())), preferred_element_type=F32).astype(out)


def mm_t(a, b, out=F32):
    return lax.dot_general(a, b, (((1,), (1,)), ((), ())), preferred_element_type=F32).astype(out)


def t_mm(a, b, out=F32):
    return lax.dot_general(a, b, (((0,), (0,)), ((), ())), preferred_element_type=F32).astype(out)


def norm_scale_of(values):
    return lax.rsqrt(jnp.mean(values * values, axis=-1, keepdims=True) + EPS)


def norm_back(values, scale, gradient):
    inner = jnp.mean(gradient * values, axis=-1, keepdims=True)
    return scale * gradient - values * (scale * scale * scale) * inner


def after(value, *deps):
    return lax.optimization_barrier((value,) + deps)[0]


class Net:
    def __init__(self, wide):
        self.wide = wide
        self.me = lax.axis_index("wide")
        self.n_plane = wide // LINE
        self.lines = [
            [base + 4 * k for k in range(LINE)] for base in range(wide) if not base & 12
        ]
        self.planes = [[w for w in range(wide) if (w >> 2) % LINE == z] for z in range(LINE)]

    def flip(self, value, bit):
        return lax.ppermute(value, "wide", [(w, w ^ (1 << bit)) for w in range(self.wide)])

    def core(self, value):
        return lax.ppermute(value, "narrow", [(0, 1), (1, 0)])

    def line(self, value):
        return lax.all_to_all(
            value, "wide", 0, 0, axis_index_groups=self.lines, tiled=True
        )

    def permute(self, value):
        tokens, cols = value.shape
        value = value.reshape(tokens, self.n_plane // 4, LINE, 4, cols // self.wide)
        return value.transpose(0, 1, 3, 2, 4).reshape(tokens, cols)

    def restore(self, value):
        tokens, cols = value.shape
        value = value.reshape(tokens, self.n_plane // 4, 4, LINE, cols // self.wide)
        return value.transpose(0, 1, 3, 2, 4).reshape(tokens, cols)

    def gather(self, lined):
        return lax.all_gather(lined, "wide", axis=0, axis_index_groups=self.planes, tiled=True)

    def reduce(self, grad):
        lined = lax.psum_scatter(
            grad, "wide", scatter_dimension=0, axis_index_groups=self.planes, tiled=True
        )
        got = self.line(lined.reshape(LINE, -1, grad.shape[1])).astype(F32)
        return jnp.concatenate([got[0] + got[2], got[1] + got[3]], axis=1)

    def group_gather(self, value):
        near = self.core(value)
        far = self.flip(value, 2)
        return jnp.concatenate([value, near, far, self.core(far)], axis=0)

    def group_sum(self, value):
        quarter = value.shape[0] // 4
        b = value.reshape(4, quarter)
        got = self.core(b)
        b = b + jnp.concatenate([got[1:2], got[0:1], got[3:4], got[2:3]])
        got = self.flip(b, 2)
        return (b + jnp.concatenate([got[2:], got[:2]])).reshape(-1)

    def group_scatter(self, value):
        quarter = value.shape[0] // 4
        b = [value[i * quarter : (i + 1) * quarter] for i in range(4)]
        got = self.core(jnp.concatenate([b[1], b[3]]))
        far = (b[2].astype(F32) + got[quarter:].astype(F32)).astype(BF16)
        own = b[0].astype(F32) + got[:quarter].astype(F32)
        return own + self.flip(far, 2).astype(F32)


def place_of(wide):
    me = lax.axis_index("wide")
    z = (me // 4) % LINE

    def on_line(k):
        there = (z + k) % LINE
        return me + (there - z) * 4, there

    def flip(bit):
        return me + (1 - 2 * ((me >> bit) & 1)) * (1 << bit)

    return me, lax.axis_index("narrow"), z, on_line, flip


def meet(devices):
    barrier = pltpu.get_barrier_semaphore()
    for device in devices:
        pl.semaphore_signal(
            barrier, inc=1, device_id=device, device_id_type=pl.DeviceIdType.MESH
        )
    pl.semaphore_wait(barrier, len(devices))


def gather_kernel(wide, chunks, n_in, n_out, *refs):
    ins, outs = refs[: n_in + 2], refs[n_in + 2 : n_in + n_out + 4]
    line_send, line_recv, own_sem, plane_send, plane_recv, token_sem, token_send, token_recv = refs[
        n_in + n_out + 4 :
    ]
    me, core, z, on_line, flip = place_of(wide)
    extra = list(range(4, wide.bit_length() - 1))
    plane_at = (me // 16) * 4 + me % 4
    others = [on_line(k)[0] for k in (1, 2, 3)] + [flip(b) for b in [0, 1] + extra]
    meet([(other, core) for other in others] + [(me, 1 - core)])
    rb = ins[0].shape[0]

    def token_copies(i):
        source, out = ins[n_in + i], outs[n_out + i]
        size = source.shape[0]

        def send(j, source, device):
            return pltpu.make_async_remote_copy(
                src_ref=source, dst_ref=out.at[pl.ds((j + 1) * size, size)],
                send_sem=token_send.at[i, j], recv_sem=token_recv.at[i, j],
                device_id=device, device_id_type=pl.DeviceIdType.MESH,
            )

        return (
            pltpu.make_async_copy(source, out.at[pl.ds(0, size)], token_sem.at[i]),
            send(0, source, (me, 1 - core)),
            send(1, source, (flip(2), core)),
            send(2, out.at[pl.ds(2 * size, size)], (me, 1 - core)),
        )

    def part(i, start, size):
        source, out, col, _ = chunks[i]
        width = ins[source].shape[1] // 2
        return outs[out].at[pl.ds(pl.multiple_of(start, min(size, rb)), size), pl.ds(col, width)]

    def block(m):
        return (plane_at ^ m) * (LINE * rb)

    def mine(i, there):
        source = chunks[i][0]
        width = ins[source].shape[1] // 2
        return ins[source].at[:, pl.ds(pl.multiple_of((there % 2) * width, HEAD_DIM), width)]

    def landing(i):
        return part(i, (block(0) if chunks[i][3] else 0) + z * rb, rb)

    def line_copy(i, k):
        device, there = on_line(k)
        return pltpu.make_async_remote_copy(
            src_ref=mine(i, there), dst_ref=landing(i),
            send_sem=line_send.at[i, k - 1], recv_sem=line_recv.at[i, k - 1],
            device_id=(device, core), device_id_type=pl.DeviceIdType.MESH,
        )

    def own_copy(i):
        return pltpu.make_async_copy(mine(i, z), landing(i), own_sem.at[i])

    def plane(i, j, start, size, bit):
        return pltpu.make_async_remote_copy(
            src_ref=part(i, start, size), dst_ref=part(i, start, size),
            send_sem=plane_send.at[i, j], recv_sem=plane_recv.at[i, j],
            device_id=(flip(bit), core), device_id_type=pl.DeviceIdType.MESH,
        )

    q = LINE * rb
    h = q // 2

    def first(i):
        return plane(i, 0, block(0), q, 0), plane(i, 1, block(0), q, 1)

    def second(i):
        return plane(i, 2, block(1), h, 1), plane(i, 3, block(2) + h, h, 0)

    def start_line(i):
        own_copy(i).start()
        for k in (1, 2, 3):
            line_copy(i, k).start()

    count = len(chunks)
    spread = [c[3] for c in chunks]
    tokens = [token_copies(0), token_copies(1)]
    for copy in tokens[0][:3]:
        copy.start()
    for i in range(2):
        start_line(i)
    for i in range(count + 1):
        if i == 2:
            for copy in tokens[1][:3]:
                copy.start()
            tokens[0][2].wait_recv()
            tokens[0][3].start()
        if i < count:
            own_copy(i).wait()
            for k in (1, 2, 3):
                line_copy(i, k).wait_recv()
            if spread[i]:
                for copy in first(i):
                    copy.start()
            if i + 2 < count:
                start_line(i + 2)
        if i > 0 and spread[i - 1]:
            for got, onward in zip(first(i - 1), second(i - 1)):
                got.wait_recv()
                onward.start()
    tokens[1][2].wait_recv()
    tokens[1][3].start()
    for own, near, far, onward in tokens:
        own.wait()
        near.wait()
        far.wait_send()
        onward.wait()
    for i in range(count):
        for k in (1, 2, 3):
            line_copy(i, k).wait_send()
        if spread[i]:
            for copy in first(i):
                copy.wait_send()
            for copy in second(i):
                copy.wait()
    for e, bit in enumerate(extra):
        size = q << (2 + e)
        start = (plane_at >> (2 + e)) * size
        copies = [plane(i, 4 + e, start, size, bit) for i in range(count) if spread[i]]
        for copy in copies:
            copy.start()
        for copy in copies:
            copy.wait()


def gather_weights(wide, weights, chunks, outs, tokens):
    count = len(chunks)
    steps = wide.bit_length() - 1
    anywhere = pl.BlockSpec(memory_space=pl.ANY)
    dma = pltpu.SemaphoreType.DMA
    return pl.pallas_call(
        functools.partial(gather_kernel, wide, chunks, len(weights), len(outs)),
        out_shape=[jax.ShapeDtypeStruct(o, BF16) for o in outs]
        + [jax.ShapeDtypeStruct((4 * t.shape[0], t.shape[1]), BF16) for t in tokens],
        in_specs=[anywhere] * (len(weights) + 2),
        out_specs=[anywhere] * (len(outs) + 2),
        scratch_shapes=[dma((count, 3)), dma((count, 3)), dma((count,)), dma((count, steps)), dma((count, steps))]
        + [dma((2,)), dma((2, 3)), dma((2, 3))],
        compiler_params=pltpu.CompilerParams(
            has_side_effects=True, collective_id=1, vmem_limit_bytes=1 << 20
        ),
        cost_estimate=pl.CostEstimate(flops=0, bytes_accessed=300 << 20, transcendentals=0),
    )(*weights, *tokens)


def reduce_kernel(wide, count, *refs):
    grads, outs = refs[:count], refs[count : 2 * count]
    held, near, far, line, more, load_sem, send, recv, line_send, line_recv, more_send, more_recv = refs[2 * count :]
    me, core, z, on_line, flip = place_of(wide)
    extra = list(range(4, wide.bit_length() - 1))
    plane_at = (me // 16) * 4 + me % 4
    others = [on_line(k)[0] for k in (1, 2, 3)] + [flip(b) for b in [0, 1] + extra]
    rows, cols = grads[0].shape
    rb = rows // wide
    q = LINE * rb
    h = q // 2

    def rows_at(i, start, size):
        return held.at[i, pl.ds(pl.multiple_of(start, min(size, h)), size)]

    def block(m):
        return (plane_at ^ m) * q

    def remote(source, target, send_sem, recv_sem, device):
        return pltpu.make_async_remote_copy(
            src_ref=source, dst_ref=target, send_sem=send_sem, recv_sem=recv_sem,
            device_id=(device, core), device_id_type=pl.DeviceIdType.MESH,
        )

    def step(i, j, start, size, target, bit):
        return remote(rows_at(i, start, size), target, send.at[i, j], recv.at[i, j], flip(bit))

    def copies(i):
        return (
            step(i, 0, block(3), h, near.at[i, 0], 1),
            step(i, 1, block(3) + h, h, near.at[i, 1], 0),
            step(i, 2, block(1) + h, h, far.at[i, 0, pl.ds(h, h)], 0),
            step(i, 3, block(2), h, far.at[i, 1, pl.ds(0, h)], 1),
            step(i, 4, block(1), h, far.at[i, 0, pl.ds(0, h)], 0),
            step(i, 5, block(2) + h, h, far.at[i, 1, pl.ds(h, h)], 1),
        )

    def line_copy(i, k):
        device, there = on_line(k)
        return remote(
            rows_at(i, block(0) + there * rb, rb), line.at[i, k - 1],
            line_send.at[i, k - 1], line_recv.at[i, k - 1], device,
        )

    def load(i):
        return pltpu.make_async_copy(grads[i], held.at[i], load_sem.at[i])

    def add(i, start, size, *sources):
        tile = min(64, size)

        def body(n, carry):
            at = pl.ds(pl.multiple_of(start + n * tile, tile), tile)
            total = held[i, at].astype(F32)
            for source in sources:
                total = total + source[pl.ds(n * tile, tile)].astype(F32)
            held[i, at] = total.astype(BF16)
            return carry

        lax.fori_loop(0, size // tile, body, 0)

    for i in range(count):
        load(i).start()
    meet([(other, core) for other in others])

    def begin(i):
        load(i).wait()
        for e in reversed(range(len(extra))):
            size = q << (2 + e)
            half = plane_at >> (2 + e)
            copy = remote(
                rows_at(i, (half ^ 1) * size, size), more.at[i, e, pl.ds(0, size)],
                more_send.at[i, e], more_recv.at[i, e], flip(extra[e]),
            )
            copy.start()
            copy.wait()
            add(i, half * size, size, more.at[i, e])
        for copy in copies(i)[:4]:
            copy.start()

    def fold(i):
        c = copies(i)
        c[0].wait_recv()
        add(i, block(1), h, near.at[i, 0])
        c[4].start()
        c[1].wait_recv()
        add(i, block(2) + h, h, near.at[i, 1])
        c[5].start()

    def to_line(i):
        for copy in copies(i)[2:]:
            copy.wait_recv()
        add(i, block(0), q, far.at[i, 0], far.at[i, 1])
        for k in (1, 2, 3):
            line_copy(i, k).start()

    def finish(i):
        for k in (1, 2, 3):
            line_copy(i, k).wait_recv()
        own = held[i, pl.ds(pl.multiple_of(block(0) + z * rb, rb), rb)].astype(F32) + line[i, 1].astype(F32)
        other = line[i, 0].astype(F32) + line[i, 2].astype(F32)
        lower = z % 2 == 0

        @pl.when(lower)
        def _():
            outs[i][:, pl.ds(0, cols)] = own
            outs[i][:, pl.ds(cols, cols)] = other

        @pl.when(jnp.logical_not(lower))
        def _():
            outs[i][:, pl.ds(0, cols)] = other
            outs[i][:, pl.ds(cols, cols)] = own

    for n in range(count + 3):
        if n < count:
            begin(n)
        if 0 <= n - 1 < count:
            fold(n - 1)
        if 0 <= n - 2 < count:
            to_line(n - 2)
        if 0 <= n - 3 < count:
            finish(n - 3)
    for i in range(count):
        for copy in copies(i):
            copy.wait_send()
        for k in (1, 2, 3):
            line_copy(i, k).wait_send()


def reduce_weights(wide, grads):
    count = len(grads)
    rows, cols = grads[0].shape
    rb = rows // wide
    q = LINE * rb
    extra = max(1, wide.bit_length() - 5)
    dma = pltpu.SemaphoreType.DMA
    return pl.pallas_call(
        functools.partial(reduce_kernel, wide, count),
        out_shape=[jax.ShapeDtypeStruct((rb, 2 * cols), F32)] * count,
        in_specs=[pl.BlockSpec(memory_space=pl.ANY)] * count,
        out_specs=[pl.BlockSpec(memory_space=pltpu.VMEM)] * count,
        scratch_shapes=[
            pltpu.VMEM((count, rows, cols), BF16),
            pltpu.VMEM((count, 2, q // 2, cols), BF16),
            pltpu.VMEM((count, 2, q, cols), BF16),
            pltpu.VMEM((count, 3, rb, cols), BF16),
            pltpu.VMEM((count, extra, rows // 2 if wide > 16 else 16, cols), BF16),
            dma((count,)),
            dma((count, 6)),
            dma((count, 6)),
            dma((count, 3)),
            dma((count, 3)),
            dma((count, extra)),
            dma((count, extra)),
        ],
        compiler_params=pltpu.CompilerParams(
            has_side_effects=True, collective_id=2, vmem_limit_bytes=48 << 20
        ),
        cost_estimate=pl.CostEstimate(flops=0, bytes_accessed=300 << 20, transcendentals=0),
    )(*grads)


def masks(lengths, places, rates):
    starts, total = [], 0
    for c in range(lengths.shape[1] - 1):
        total = total + lengths[:, c]
        starts.append(total)
    starts = jnp.stack(starts, axis=1)
    docs = jnp.sum((places[None, :, None] >= starts[:, None, :]).astype(jnp.int32), axis=2)
    gap = places[:, None] - places[None, :]
    allowed = (gap >= 0)[None] & (docs[:, :, None] == docs[:, None, :])
    spread = jnp.maximum(gap, 0).astype(F32)
    weights = jnp.exp(-rates[:, None, None] * spread[None])
    return jnp.where(allowed[:, None], weights[None], 0.0)


def sigmoid(z):
    return 1.0 / (1.0 + jnp.exp(-z))


def on_device(
    layer_input, doc_lengths, w_query, w_key, w_value, w_gate, w_output, w_left, w_right, w_down, cotangent, *, wide
):
    net = Net(wide)
    core = lax.axis_index("narrow")
    half = (net.me >> 2) & 1
    features = layer_input.shape[1]

    inputs = net.permute(layer_input).astype(F32)
    norm_one = norm_scale_of(inputs)
    cot = net.permute(cotangent)
    rows, small, large = features, w_query.shape[1] // 2, w_left.shape[1] // 2
    qk_w, vg_w, output_w, left_lined, right_lined, down_lined, normed, cot_all = gather_weights(
        wide,
        [w_query, w_key, w_value, w_gate, w_output, w_left, w_right, w_down],
        [(0, 0, 0, 1), (1, 0, small, 1), (2, 1, 0, 1), (3, 1, small, 1), (4, 2, 0, 1), (5, 3, 0, 0), (6, 4, 0, 0), (7, 5, 0, 0)],
        [(rows, 2 * small), (rows, 2 * small), (rows, small), *[(LINE * w_left.shape[0], large)] * 3],
        [(inputs * norm_one).astype(BF16), cot],
    )
    left_w = net.gather(left_lined)
    right_w = net.gather(right_lined)
    down_w = net.gather(down_lined)

    quarter = inputs.shape[0]
    tokens = 4 * quarter
    row_len = 2 * quarter
    width = output_w.shape[1]
    heads = width // HEAD_DIM
    all_heads = features // HEAD_DIM
    head_ids = (core * 2 + half) * heads + jnp.arange(heads, dtype=jnp.int32)
    rates = DECAY * head_ids.astype(F32) / all_heads
    own = jnp.arange(quarter, dtype=jnp.int32)
    places = jnp.concatenate([own + core * quarter, own + (1 - core) * quarter])
    lengths = jnp.concatenate([doc_lengths, net.flip(doc_lengths, 2)])
    decay = masks(lengths, places, rates)

    qk_pre = mm(normed, qk_w)
    query_pre, key_pre = qk_pre[:, :width], qk_pre[:, width:]
    vg = mm(normed, vg_w)
    values, gate = vg[:, :width].astype(BF16), vg[:, width:]
    query_sig, key_sig = sigmoid(query_pre), sigmoid(key_pre)
    queries = (query_pre * query_sig).astype(BF16)
    keys = (key_pre * key_sig).astype(BF16)
    shape = (2, row_len, heads, HEAD_DIM)
    q4, k4, v4 = (a.reshape(shape) for a in (queries, keys, values))
    scores = jnp.einsum("rihd,rjhd->rhij", q4, k4, preferred_element_type=F32)
    probs = (scores * decay).astype(BF16)
    mixed = jnp.einsum("rhij,rjhd->rihd", probs, v4, preferred_element_type=F32)
    mixed = mixed.reshape(tokens, width)
    squares = net.group_sum(jnp.sum(mixed * mixed, axis=1))
    attn_scale = lax.rsqrt(squares / features + EPS)[:, None]
    scaled = mixed * attn_scale
    blended = (gate * scaled).astype(BF16)
    middle = inputs + net.group_scatter(mm_t(blended, output_w, BF16))
    norm_two = norm_scale_of(middle)
    mid = net.group_gather((middle * norm_two).astype(BF16))
    left = mm(mid, left_w)
    right = mm(mid, right_w)
    product = (left * right).astype(BF16)
    grad_down = t_mm(cot_all, product, BF16)
    output_part = mm_t(product, down_w, BF16)
    layer_output = middle + net.group_scatter(output_part)
    layer_output = net.restore(layer_output.astype(BF16))

    grad_product = mm(cot_all, down_w)
    grad_left_pre = (grad_product * right).astype(BF16)
    grad_right_pre = (grad_product * left).astype(BF16)
    grad_mid = net.group_scatter(
        (mm_t(grad_left_pre, left_w) + mm_t(grad_right_pre, right_w)).astype(BF16)
    )
    grad_left = t_mm(mid, grad_left_pre, BF16)
    grad_right = t_mm(mid, grad_right_pre, BF16)
    grad_mid = after(grad_mid, grad_left, grad_right)
    grad_middle = cot.astype(F32) + norm_back(middle, norm_two, grad_mid)
    branch = net.group_gather(grad_middle.astype(BF16))
    branch = after(branch, output_part, grad_down)
    grad_left, grad_right, grad_down = (net.reduce(g) for g in (grad_left, grad_right, grad_down))
    grad_blended = mm(branch, output_w)
    grad_output = t_mm(branch, blended, BF16)
    grad_gate_pre = (grad_blended * scaled).astype(BF16)
    grad_gate = t_mm(normed, grad_gate_pre, BF16)
    grad_scaled = grad_blended * gate
    inner = net.group_sum(jnp.sum(grad_scaled * mixed, axis=1)) / features
    grad_mixed = (
        attn_scale * grad_scaled - mixed * (attn_scale * attn_scale * attn_scale) * inner[:, None]
    ).astype(BF16)
    g4 = grad_mixed.reshape(shape)
    grad_probs = jnp.einsum("rihd,rjhd->rhij", g4, v4, preferred_element_type=F32)
    grad_values = jnp.einsum("rhij,rihd->rjhd", probs, g4, preferred_element_type=F32)
    grad_value_pre = grad_values.astype(BF16).reshape(tokens, width)
    grad_value = t_mm(normed, grad_value_pre, BF16)
    grad_scores = (grad_probs * decay).astype(BF16)
    grad_queries = jnp.einsum("rhij,rjhd->rihd", grad_scores, k4, preferred_element_type=F32)
    grad_keys = jnp.einsum("rhij,rihd->rjhd", grad_scores, q4, preferred_element_type=F32)
    grad_query_pre = (
        grad_queries.reshape(tokens, width) * (query_sig * (1.0 + query_pre * (1.0 - query_sig)))
    ).astype(BF16)
    grad_key_pre = (
        grad_keys.reshape(tokens, width) * (key_sig * (1.0 + key_pre * (1.0 - key_sig)))
    ).astype(BF16)
    grad_query = t_mm(normed, grad_query_pre, BF16)
    grad_key = t_mm(normed, grad_key_pre, BF16)
    grad_output, grad_gate, grad_value, grad_query, grad_key = reduce_weights(
        wide, [grad_output, grad_gate, grad_value, grad_query, grad_key]
    )
    total = mm_t(jnp.concatenate([grad_value_pre, grad_gate_pre], axis=1), vg_w)
    total = total + mm_t(jnp.concatenate([grad_query_pre, grad_key_pre], axis=1), qk_w)
    grad_normed = net.group_scatter(total.astype(BF16))
    input_grad = net.restore(grad_middle + norm_back(inputs, norm_one, grad_normed))
    return (
        layer_output,
        input_grad,
        grad_query,
        grad_key,
        grad_value,
        grad_gate,
        grad_output,
        grad_left,
        grad_right,
        grad_down,
    )


def solution(mesh):
    both, weight = P(("wide", "narrow"), None), P("wide", "narrow")
    wide = mesh.shape["wide"]

    def body(*args):
        return on_device(*args, wide=wide)

    return jax.shard_map(
        body,
        mesh=mesh,
        in_specs=(both, P("wide", None)) + (weight,) * 8 + (both,),
        out_specs=(both, both) + (weight,) * 8,
        check_vma=False,
    )
```

```python
import functools

import jax
import jax.numpy as jnp
from jax import lax
from jax.experimental import pallas as pl
from jax.experimental.pallas import tpu as pltpu
from jax.sharding import PartitionSpec as P

HEAD_DIM = 128
LINE = 4
EPS = 1e-06
DECAY = 2.0
F32 = jnp.float32
BF16 = jnp.bfloat16


def mm(a, b, out=F32):
    return lax.dot_general(a, b, (((1,), (0,)), ((), ())), preferred_element_type=F32).astype(out)


def mm_t(a, b, out=F32):
    return lax.dot_general(a, b, (((1,), (1,)), ((), ())), preferred_element_type=F32).astype(out)


def t_mm(a, b, out=F32):
    return lax.dot_general(a, b, (((0,), (0,)), ((), ())), preferred_element_type=F32).astype(out)


def norm_scale_of(values):
    return lax.rsqrt(jnp.mean(values * values, axis=-1, keepdims=True) + EPS)


def norm_back(values, scale, gradient):
    inner = jnp.mean(gradient * values, axis=-1, keepdims=True)
    return scale * gradient - values * (scale * scale * scale) * inner


def after(value, *deps):
    return lax.optimization_barrier((value,) + deps)[0]


class Net:
    def __init__(self, wide):
        self.wide = wide
        self.me = lax.axis_index("wide")
        self.n_plane = wide // LINE
        self.lines = [
            [base + 4 * k for k in range(LINE)] for base in range(wide) if not base & 12
        ]
        self.planes = [[w for w in range(wide) if (w >> 2) % LINE == z] for z in range(LINE)]

    def flip(self, value, bit):
        return lax.ppermute(value, "wide", [(w, w ^ (1 << bit)) for w in range(self.wide)])

    def core(self, value):
        return lax.ppermute(value, "narrow", [(0, 1), (1, 0)])

    def line(self, value):
        return lax.all_to_all(
            value, "wide", 0, 0, axis_index_groups=self.lines, tiled=True
        )

    def permute(self, value):
        tokens, cols = value.shape
        value = value.reshape(tokens, self.n_plane // 4, LINE, 4, cols // self.wide)
        return value.transpose(0, 1, 3, 2, 4).reshape(tokens, cols)

    def restore(self, value):
        tokens, cols = value.shape
        value = value.reshape(tokens, self.n_plane // 4, 4, LINE, cols // self.wide)
        return value.transpose(0, 1, 3, 2, 4).reshape(tokens, cols)

    def gather(self, lined):
        return lax.all_gather(lined, "wide", axis=0, axis_index_groups=self.planes, tiled=True)

    def plane_sum(self, grad):
        return lax.psum_scatter(
            grad, "wide", scatter_dimension=0, axis_index_groups=self.planes, tiled=True
        )

    def line_sum(self, lined):
        got = self.line(lined.reshape(LINE, -1, lined.shape[1])).astype(F32)
        return jnp.concatenate([got[0] + got[2], got[1] + got[3]], axis=1)

    def group_gather(self, value):
        near = self.core(value)
        far = self.flip(value, 2)
        return jnp.concatenate([value, near, far, self.core(far)], axis=0)

    def group_sum(self, value):
        quarter = value.shape[0] // 4
        b = value.reshape(4, quarter)
        got = self.core(b)
        b = b + jnp.concatenate([got[1:2], got[0:1], got[3:4], got[2:3]])
        got = self.flip(b, 2)
        return (b + jnp.concatenate([got[2:], got[:2]])).reshape(-1)

    def group_scatter(self, value):
        quarter = value.shape[0] // 4
        b = [value[i * quarter : (i + 1) * quarter] for i in range(4)]
        got = self.core(jnp.concatenate([b[1], b[3]]))
        far = (b[2].astype(F32) + got[quarter:].astype(F32)).astype(BF16)
        own = b[0].astype(F32) + got[:quarter].astype(F32)
        return own + self.flip(far, 2).astype(F32)


def place_of(wide):
    me = lax.axis_index("wide")
    z = (me // 4) % LINE

    def on_line(k):
        there = (z + k) % LINE
        return me + (there - z) * 4, there

    def flip(bit):
        return me + (1 - 2 * ((me >> bit) & 1)) * (1 << bit)

    return me, lax.axis_index("narrow"), z, on_line, flip


def meet(devices):
    barrier = pltpu.get_barrier_semaphore()
    for device in devices:
        pl.semaphore_signal(
            barrier, inc=1, device_id=device, device_id_type=pl.DeviceIdType.MESH
        )
    pl.semaphore_wait(barrier, len(devices))


def forward_kernel(wide, small, large, *refs):
    (
        w_in, (normed_own, cot_own, x_own, ends_own),
        w_out, (normed_out, cot_out, query_pre_out, key_pre_out, gate_out, query_out, key_out, value_out, mixed_out,
                probs_out, middle_out, mid_out, left_out, right_out, product_out),
        (normed, wide_w, query_pre, key_pre, gate, query, key, value, mixed, probs, blended, part, part_core, part_far,
         square, square_core, square_far, ends_far, mid, middle, large_w, left, right, product),
        (line_send, line_recv, own_sem, plane_send, plane_recv, load_sem, save_sem, token_sem, token_send, token_recv,
         small_send, small_recv),
    ) = split_refs(refs, (8, 4, 6, 15, 24, 12))
    me, core, z, on_line, flip = place_of(wide)
    extra = list(range(4, wide.bit_length() - 1))
    plane_at = (me // 16) * 4 + me % 4
    others = [on_line(k)[0] for k in (1, 2, 3)] + [flip(b) for b in [0, 1] + extra]
    meet([(other, core) for other in others] + [(me, 1 - core)])
    rb = w_in[0].shape[0]
    q = LINE * rb
    h = q // 2
    quarter, features = x_own.shape
    row_len = 2 * quarter
    chunks = [(0, 0), (0, small), (1, 0), (1, small), (2, 0), (3, 0), (4, 0), (5, 0)]
    near_device, far_device = (me, 1 - core), (flip(2), core)


    def part_of(i, start, size):
        out, col = chunks[i]
        cols = w_in[i].shape[1] // 2
        return w_out[out].at[pl.ds(pl.multiple_of(start, min(size, rb)), size), pl.ds(col, cols)]

    def block(m):
        return (plane_at ^ m) * q

    def remote(source, target, send_sem, recv_sem, device):
        return pltpu.make_async_remote_copy(
            src_ref=source, dst_ref=target, send_sem=send_sem, recv_sem=recv_sem,
            device_id=device, device_id_type=pl.DeviceIdType.MESH,
        )

    def mine(i, there):
        cols = w_in[i].shape[1] // 2
        return w_in[i].at[:, pl.ds(pl.multiple_of((there % 2) * cols, HEAD_DIM), cols)]

    def line_copy(i, k):
        device, there = on_line(k)
        return remote(
            mine(i, there), part_of(i, block(0) + z * rb, rb),
            line_send.at[i, k - 1], line_recv.at[i, k - 1], (device, core),
        )

    def own_copy(i):
        return pltpu.make_async_copy(mine(i, z), part_of(i, block(0) + z * rb, rb), own_sem.at[i])

    def plane(i, j, start, size, bit):
        place = part_of(i, start, size)
        return remote(place, place, plane_send.at[i, j], plane_recv.at[i, j], (flip(bit), core))

    def first(i):
        return plane(i, 0, block(0), q, 0), plane(i, 1, block(0), q, 1)

    def second(i):
        return plane(i, 2, block(1), h, 1), plane(i, 3, block(2) + h, h, 0)

    def start_line(i):
        own_copy(i).start()
        for k in (1, 2, 3):
            line_copy(i, k).start()

    def start_plane(i):
        own_copy(i).wait()
        for k in (1, 2, 3):
            line_copy(i, k).wait_recv()
        for copy in first(i):
            copy.start()

    def forward_plane(i):
        for got, onward in zip(first(i), second(i)):
            got.wait_recv()
            onward.start()

    def complete(i):
        for copy in second(i):
            copy.wait_recv()
        for e, bit in enumerate(extra):
            size = q << (2 + e)
            copy = plane(i, 4 + e, (plane_at >> (2 + e)) * size, size, bit)
            copy.start()
            copy.wait()


    def rows(b):
        return pl.ds(b * quarter, quarter)

    def token_copies(n, source, out):
        send = lambda j, source, device: remote(
            source, out.at[rows(j + 1)], token_send.at[n, j], token_recv.at[n, j], device
        )
        return send(0, source, near_device), send(1, source, far_device), send(2, out.at[rows(2)], near_device)

    def start_tokens(copies):
        copies[0].start()
        copies[1].start()

    def pass_tokens(copies):
        copies[1].wait_recv()
        copies[2].start()

    def end_tokens(copies):
        copies[0].wait_recv()
        copies[2].wait_recv()

    def sent_tokens(copies):
        for copy in copies:
            copy.wait_send()

    saves = []

    def save(source, target):
        copy = pltpu.make_async_copy(source, target, save_sem.at[len(saves)])
        copy.start()
        saves.append(copy)

    normed_copies = token_copies(0, normed_own, normed)
    cot_copies = token_copies(1, cot_own, cot_out)
    mid_copies = token_copies(2, mid.at[rows(0)], mid)
    normed_local = pltpu.make_async_copy(normed_own, normed.at[rows(0)], token_sem.at[0])
    cot_local = pltpu.make_async_copy(cot_own, cot_out.at[rows(0)], token_sem.at[1])
    ends_copy = remote(ends_own, ends_far, small_send.at[0], small_recv.at[0], far_device)


    def load(i, slot):
        return pltpu.make_async_copy(
            part_of(i, 0, features), wide_w.at[slot] if i < 5 else large_w, load_sem.at[i]
        )

    def project(i, slot, keep):
        copy = load(i, slot)
        copy.start()
        copy.wait()

        def body(n, carry):
            at = pl.ds(pl.multiple_of(n * row_len, row_len), row_len)
            keep(at, jnp.dot(normed[at], wide_w[slot], preferred_element_type=F32))
            return carry

        lax.fori_loop(0, 2, body, 0)

    def keep_query(at, total):
        query_pre[at] = total
        query[at] = (total * sigmoid(total)).astype(BF16)

    def keep_key(at, total):
        key_pre[at] = total
        key[at] = (total * sigmoid(total)).astype(BF16)

    def keep_value(at, total):
        value[at] = total.astype(BF16)

    def keep_gate(at, total):
        gate[at] = total

    heads = small // HEAD_DIM
    first_head = (core * 2 + z % 2) * heads

    def attend(row, ends):
        at = pl.ds(row * row_len, row_len)

        def place(dim):
            index = lax.broadcasted_iota(jnp.int32, (row_len, row_len), dim) + core * quarter
            return jnp.where(index >= row_len, index - row_len, index).astype(F32)

        def body(head, carry):
            cols = pl.ds(pl.multiple_of(head * HEAD_DIM, HEAD_DIM), HEAD_DIM)
            scores = lax.dot_general(
                query[at, cols], key[at, cols], (((1,), (1,)), ((), ())), preferred_element_type=F32
            )
            to, source = place(0), place(1)
            allowed = (to >= source) & (to < ends[0:1, :])
            rate = (first_head + head).astype(F32) * (DECAY * HEAD_DIM / features)
            decay = jnp.where(allowed, jnp.exp(-rate * jnp.maximum(to - source, 0.0)), 0.0)
            weights = (scores * decay).astype(BF16)
            probs[row, head] = weights
            mixed[at, cols] = jnp.dot(weights, value[at, cols], preferred_element_type=F32)
            return carry

        lax.fori_loop(0, heads, body, 0)
        for b in (2 * row, 2 * row + 1):
            m = mixed[rows(b)]
            total = jnp.sum(m * m, axis=1, keepdims=True)
            square[rows(b)] = jnp.broadcast_to(total, (quarter, HEAD_DIM))
            blended[rows(b)] = (gate[rows(b)] * m).astype(BF16)

    def output_part(row, slot):
        at = pl.ds(row * row_len, row_len)

        def body(n, carry):
            cols = pl.ds(pl.multiple_of(n * row_len, row_len), row_len)
            part[at, cols] = lax.dot_general(
                blended[at], wide_w[slot, cols], (((1,), (1,)), ((), ())), preferred_element_type=F32
            ).astype(BF16)
            return carry

        lax.fori_loop(0, features // row_len, body, 0)

    tile = 32

    def tiles(body):
        def step(n, carry):
            body(pl.multiple_of(n * tile, tile))
            return carry

        lax.fori_loop(0, quarter // tile, step, 0)


    normed_local.start()
    start_tokens(normed_copies)
    ends_copy.start()
    start_line(0)
    start_line(1)
    start_plane(0)
    start_line(2)
    start_plane(1)
    start_line(3)
    pass_tokens(normed_copies)
    forward_plane(0)
    start_plane(2)
    start_line(4)
    forward_plane(1)
    normed_local.wait()
    end_tokens(normed_copies)
    save(normed, normed_out)
    complete(0)
    project(0, 0, keep_query)
    save(query_pre, query_pre_out)
    save(query, query_out)
    start_plane(3)
    start_line(5)
    forward_plane(2)
    complete(1)
    project(1, 1, keep_key)
    save(key_pre, key_pre_out)
    save(key, key_out)
    start_plane(4)
    start_line(6)
    forward_plane(3)
    complete(2)
    project(2, 0, keep_value)
    save(value, value_out)
    forward_plane(4)
    complete(3)
    project(3, 1, keep_gate)
    save(gate, gate_out)
    ends_copy.wait()
    attend(1, ends_far)
    square_near = remote(
        square.at[rows(1)], square_core.at[rows(0)], small_send.at[1], small_recv.at[1], near_device
    )
    square_diag = remote(
        square.at[rows(3)], square_core.at[rows(1)], small_send.at[2], small_recv.at[2], near_device
    )
    square_pair = remote(square.at[rows(2)], square_far, small_send.at[3], small_recv.at[3], far_device)
    square_diag.start()
    start_plane(5)
    attend(0, ends_own)
    save(mixed, mixed_out)
    save(probs, probs_out)
    square_near.start()
    square_diag.wait_recv()
    square[rows(2)] += square_core[rows(1)]
    square_pair.start()
    complete(4)
    copy = load(4, 0)
    copy.start()
    copy.wait()
    output_part(1, 0)
    part_near = remote(part.at[rows(1)], part_core.at[rows(0)], small_send.at[4], small_recv.at[4], near_device)
    part_diag = remote(part.at[rows(3)], part_core.at[rows(1)], small_send.at[5], small_recv.at[5], near_device)
    part_pair = remote(part.at[rows(2)], part_far, small_send.at[6], small_recv.at[6], far_device)
    part_diag.start()
    part_diag.wait_recv()

    @tiles
    def _(start):
        here = pl.ds(start + 2 * quarter, tile)
        part[here] = (part[here].astype(F32) + part_core[pl.ds(start + quarter, tile)].astype(F32)).astype(BF16)

    part_pair.start()
    output_part(0, 0)
    part_near.start()
    forward_plane(5)
    start_plane(6)
    square_near.wait_recv()
    square_pair.wait_recv()
    part_near.wait_recv()
    part_pair.wait_recv()

    @tiles
    def _(start):
        here = pl.ds(start, tile)
        total = part[here].astype(F32) + part_core[here].astype(F32) + part_far[here].astype(F32)
        squares = square[here, 0:1] + square_core[here, 0:1] + square_far[here, 0:1]
        total = x_own[here].astype(F32) + total * lax.rsqrt(squares / features + EPS)
        middle[here] = total
        mid[here] = (total * lax.rsqrt(jnp.mean(total * total, axis=1, keepdims=True) + EPS)).astype(BF16)

    start_tokens(mid_copies)
    save(middle, middle_out)
    complete(5)
    copy = load(5, 0)
    copy.start()
    copy.wait()
    mid_copies[0].wait_recv()

    def left_rows(row):
        at = pl.ds(row * row_len, row_len)
        left[at] = jnp.dot(mid[at], large_w[...], preferred_element_type=F32).astype(BF16)

    left_rows(0)
    pass_tokens(mid_copies)
    start_line(7)
    cot_local.start()
    start_tokens(cot_copies)
    forward_plane(6)
    mid_copies[2].wait_recv()
    left_rows(1)
    save(mid, mid_out)
    save(left, left_out)
    complete(6)
    copy = load(6, 0)
    copy.start()
    copy.wait()

    def right_rows(n, carry):
        at = pl.ds(pl.multiple_of(n * row_len, row_len), row_len)
        total = jnp.dot(mid[at], large_w[...], preferred_element_type=F32)
        right[at] = total.astype(BF16)
        product[at] = (left[at].astype(F32) * total).astype(BF16)
        return carry

    start_plane(7)
    lax.fori_loop(0, 2, right_rows, 0)
    save(right, right_out)
    save(product, product_out)
    pass_tokens(cot_copies)
    forward_plane(7)
    complete(7)
    cot_local.wait()
    end_tokens(cot_copies)
    for copies in (normed_copies, cot_copies, mid_copies):
        sent_tokens(copies)
    for copy in (square_near, square_diag, square_pair, part_near, part_diag, part_pair):
        copy.wait_send()
    for i in range(8):
        for k in (1, 2, 3):
            line_copy(i, k).wait_send()
        for copy in first(i) + second(i):
            copy.wait_send()
    for copy in saves:
        copy.wait()


def split_refs(refs, counts):
    parts, at = [], 0
    for count in counts:
        parts.append(refs[at : at + count])
        at += count
    return parts


def forward(wide, weights, normed, cot, x, ends):
    small, large = weights[0].shape[1] // 2, weights[5].shape[1] // 2
    quarter, features = x.shape
    tokens, row_len, heads = 4 * quarter, 2 * quarter, small // HEAD_DIM
    steps = wide.bit_length() - 1
    anywhere, vmem = pl.BlockSpec(memory_space=pl.ANY), pl.BlockSpec(memory_space=pltpu.VMEM)
    dma = pltpu.SemaphoreType.DMA
    outs = [
        ((features, 2 * small), BF16),
        ((features, 2 * small), BF16),
        ((features, small), BF16),
        ((features, large), BF16),
        ((features, large), BF16),
        ((features, large), BF16),
        ((tokens, features), BF16),
        ((tokens, features), BF16),
        ((tokens, small), F32),
        ((tokens, small), F32),
        ((tokens, small), F32),
        ((tokens, small), BF16),
        ((tokens, small), BF16),
        ((tokens, small), BF16),
        ((tokens, small), F32),
        ((2, heads, row_len, row_len), BF16),
        ((quarter, features), F32),
        ((tokens, features), BF16),
        ((tokens, large), BF16),
        ((tokens, large), BF16),
        ((tokens, large), BF16),
    ]
    held = [
        ((tokens, features), BF16),
        ((2, features, small), BF16),
        ((tokens, small), F32),
        ((tokens, small), F32),
        ((tokens, small), F32),
        ((tokens, small), BF16),
        ((tokens, small), BF16),
        ((tokens, small), BF16),
        ((tokens, small), F32),
        ((2, heads, row_len, row_len), BF16),
        ((tokens, small), BF16),
        ((tokens, features), BF16),
        ((row_len, features), BF16),
        ((quarter, features), BF16),
        ((tokens, HEAD_DIM), F32),
        ((row_len, HEAD_DIM), F32),
        ((quarter, HEAD_DIM), F32),
        (ends.shape, F32),
        ((tokens, features), BF16),
        ((quarter, features), F32),
        ((features, large), BF16),
        ((tokens, large), BF16),
        ((tokens, large), BF16),
        ((tokens, large), BF16),
    ]
    sems = [(8, 3), (8, 3), (8,), (8, steps), (8, steps), (8,), (14,), (2,), (3, 3), (3, 3), (7,), (7,)]
    return pl.pallas_call(
        functools.partial(forward_kernel, wide, small, large),
        out_shape=[jax.ShapeDtypeStruct(s, t) for s, t in outs],
        in_specs=[anywhere] * 10 + [vmem] * 2,
        out_specs=[anywhere] * len(outs),
        scratch_shapes=[pltpu.VMEM(s, t) for s, t in held] + [dma(s) for s in sems],
        compiler_params=pltpu.CompilerParams(
            has_side_effects=True, collective_id=1, vmem_limit_bytes=60 << 20
        ),
        cost_estimate=pl.CostEstimate(flops=0, bytes_accessed=300 << 20, transcendentals=0),
    )(*weights, normed, cot, x, ends)


def reduce_kernel(wide, count, *refs):
    grads, outs = refs[:count], refs[count : 2 * count]
    held, near, far, line, more, load_sem, send, recv, line_send, line_recv, more_send, more_recv = refs[2 * count :]
    me, core, z, on_line, flip = place_of(wide)
    extra = list(range(4, wide.bit_length() - 1))
    plane_at = (me // 16) * 4 + me % 4
    others = [on_line(k)[0] for k in (1, 2, 3)] + [flip(b) for b in [0, 1] + extra]
    rows, cols = grads[0].shape
    rb = rows // wide
    q = LINE * rb
    h = q // 2

    def rows_at(i, start, size):
        return held.at[i, pl.ds(pl.multiple_of(start, min(size, h)), size)]

    def block(m):
        return (plane_at ^ m) * q

    def remote(source, target, send_sem, recv_sem, device):
        return pltpu.make_async_remote_copy(
            src_ref=source, dst_ref=target, send_sem=send_sem, recv_sem=recv_sem,
            device_id=(device, core), device_id_type=pl.DeviceIdType.MESH,
        )

    def step(i, j, start, size, target, bit):
        return remote(rows_at(i, start, size), target, send.at[i, j], recv.at[i, j], flip(bit))

    def copies(i):
        return (
            step(i, 0, block(3), h, near.at[i, 0], 1),
            step(i, 1, block(3) + h, h, near.at[i, 1], 0),
            step(i, 2, block(1) + h, h, far.at[i, 0, pl.ds(h, h)], 0),
            step(i, 3, block(2), h, far.at[i, 1, pl.ds(0, h)], 1),
            step(i, 4, block(1), h, far.at[i, 0, pl.ds(0, h)], 0),
            step(i, 5, block(2) + h, h, far.at[i, 1, pl.ds(h, h)], 1),
        )

    def line_copy(i, k):
        device, there = on_line(k)
        return remote(
            rows_at(i, block(0) + there * rb, rb), line.at[i, k - 1],
            line_send.at[i, k - 1], line_recv.at[i, k - 1], device,
        )

    def load(i):
        return pltpu.make_async_copy(grads[i], held.at[i], load_sem.at[i])

    def add(i, start, size, *sources):
        tile = min(64, size)

        def body(n, carry):
            at = pl.ds(pl.multiple_of(start + n * tile, tile), tile)
            total = held[i, at].astype(F32)
            for source in sources:
                total = total + source[pl.ds(n * tile, tile)].astype(F32)
            held[i, at] = total.astype(BF16)
            return carry

        lax.fori_loop(0, size // tile, body, 0)

    for i in range(count):
        load(i).start()
    meet([(other, core) for other in others])

    def begin(i):
        load(i).wait()
        for e in reversed(range(len(extra))):
            size = q << (2 + e)
            half = plane_at >> (2 + e)
            copy = remote(
                rows_at(i, (half ^ 1) * size, size), more.at[i, e, pl.ds(0, size)],
                more_send.at[i, e], more_recv.at[i, e], flip(extra[e]),
            )
            copy.start()
            copy.wait()
            add(i, half * size, size, more.at[i, e])
        for copy in copies(i)[:4]:
            copy.start()

    def fold(i):
        c = copies(i)
        c[0].wait_recv()
        add(i, block(1), h, near.at[i, 0])
        c[4].start()
        c[1].wait_recv()
        add(i, block(2) + h, h, near.at[i, 1])
        c[5].start()

    def to_line(i):
        for copy in copies(i)[2:]:
            copy.wait_recv()
        add(i, block(0), q, far.at[i, 0], far.at[i, 1])
        for k in (1, 2, 3):
            line_copy(i, k).start()

    def finish(i):
        for k in (1, 2, 3):
            line_copy(i, k).wait_recv()
        own = held[i, pl.ds(pl.multiple_of(block(0) + z * rb, rb), rb)].astype(F32) + line[i, 1].astype(F32)
        other = line[i, 0].astype(F32) + line[i, 2].astype(F32)
        lower = z % 2 == 0

        @pl.when(lower)
        def _():
            outs[i][:, pl.ds(0, cols)] = own
            outs[i][:, pl.ds(cols, cols)] = other

        @pl.when(jnp.logical_not(lower))
        def _():
            outs[i][:, pl.ds(0, cols)] = other
            outs[i][:, pl.ds(cols, cols)] = own

    for n in range(count + 3):
        if n < count:
            begin(n)
        if 0 <= n - 1 < count:
            fold(n - 1)
        if 0 <= n - 2 < count:
            to_line(n - 2)
        if 0 <= n - 3 < count:
            finish(n - 3)
    for i in range(count):
        for copy in copies(i):
            copy.wait_send()
        for k in (1, 2, 3):
            line_copy(i, k).wait_send()


def reduce_weights(wide, grads):
    count = len(grads)
    rows, cols = grads[0].shape
    rb = rows // wide
    q = LINE * rb
    extra = max(1, wide.bit_length() - 5)
    dma = pltpu.SemaphoreType.DMA
    return pl.pallas_call(
        functools.partial(reduce_kernel, wide, count),
        out_shape=[jax.ShapeDtypeStruct((rb, 2 * cols), F32)] * count,
        in_specs=[pl.BlockSpec(memory_space=pl.ANY)] * count,
        out_specs=[pl.BlockSpec(memory_space=pltpu.VMEM)] * count,
        scratch_shapes=[
            pltpu.VMEM((count, rows, cols), BF16),
            pltpu.VMEM((count, 2, q // 2, cols), BF16),
            pltpu.VMEM((count, 2, q, cols), BF16),
            pltpu.VMEM((count, 3, rb, cols), BF16),
            pltpu.VMEM((count, extra, rows // 2 if wide > 16 else 16, cols), BF16),
            dma((count,)),
            dma((count, 6)),
            dma((count, 6)),
            dma((count, 3)),
            dma((count, 3)),
            dma((count, extra)),
            dma((count, extra)),
        ],
        compiler_params=pltpu.CompilerParams(
            has_side_effects=True, collective_id=2, vmem_limit_bytes=48 << 20
        ),
        cost_estimate=pl.CostEstimate(flops=0, bytes_accessed=300 << 20, transcendentals=0),
    )(*grads)


def masks(lengths, places, rates):
    starts, total = [], 0
    for c in range(lengths.shape[1] - 1):
        total = total + lengths[:, c]
        starts.append(total)
    starts = jnp.stack(starts, axis=1)
    docs = jnp.sum((places[None, :, None] >= starts[:, None, :]).astype(jnp.int32), axis=2)
    gap = places[:, None] - places[None, :]
    allowed = (gap >= 0)[None] & (docs[:, :, None] == docs[:, None, :])
    spread = jnp.maximum(gap, 0).astype(F32)
    weights = jnp.exp(-rates[:, None, None] * spread[None])
    return jnp.where(allowed[:, None], weights[None], 0.0)


def ends_of(lengths, places):
    total, ends = 0, 0
    for c in range(lengths.shape[1]):
        ends = ends + jnp.where(places >= total, lengths[0, c], 0)
        total = total + lengths[0, c]
    return jnp.broadcast_to(ends.astype(F32)[None], (8, places.shape[0]))


def sigmoid(z):
    return 1.0 / (1.0 + jnp.exp(-z))


def on_device(
    layer_input, doc_lengths, w_query, w_key, w_value, w_gate, w_output, w_left, w_right, w_down, cotangent, *, wide
):
    net = Net(wide)
    core = lax.axis_index("narrow")
    half = (net.me >> 2) & 1
    features = layer_input.shape[1]

    x = net.permute(layer_input)
    inputs = x.astype(F32)
    norm_one = norm_scale_of(inputs)
    cot = net.permute(cotangent)
    quarter = inputs.shape[0]
    tokens = 4 * quarter
    row_len = 2 * quarter
    own = jnp.arange(quarter, dtype=jnp.int32)
    places = jnp.concatenate([own + core * quarter, own + (1 - core) * quarter])
    (
        qk_w, vg_w, output_w, left_w, right_w, down_w, normed, cot_all, query_pre, key_pre, gate, queries, keys, values,
        mixed, probs, middle, mid, left, right, product,
    ) = forward(
        wide,
        [w_query, w_key, w_value, w_gate, w_output, w_left, w_right, w_down],
        (inputs * norm_one).astype(BF16),
        cot,
        x,
        ends_of(doc_lengths, places),
    )

    width = output_w.shape[1]
    heads = width // HEAD_DIM
    all_heads = features // HEAD_DIM
    head_ids = (core * 2 + half) * heads + jnp.arange(heads, dtype=jnp.int32)
    rates = DECAY * head_ids.astype(F32) / all_heads
    lengths = jnp.concatenate([doc_lengths, net.flip(doc_lengths, 2)])
    decay = masks(lengths, places, rates)
    query_sig, key_sig = sigmoid(query_pre), sigmoid(key_pre)
    shape = (2, row_len, heads, HEAD_DIM)
    q4, k4, v4 = (a.reshape(shape) for a in (queries, keys, values))
    squares = net.group_sum(jnp.sum(mixed * mixed, axis=1))
    attn_scale = lax.rsqrt(squares / features + EPS)[:, None]
    scaled = mixed * attn_scale
    blended = (gate * scaled).astype(BF16)
    norm_two = norm_scale_of(middle)
    grad_down = t_mm(cot_all, product, BF16)
    output_part = mm_t(product, down_w, BF16)
    layer_output = middle + net.group_scatter(output_part)
    layer_output = net.restore(layer_output.astype(BF16))

    grad_product = mm(cot_all, down_w)
    grad_left_pre = (grad_product * right.astype(F32)).astype(BF16)
    grad_right_pre = (grad_product * left.astype(F32)).astype(BF16)
    grad_mid = net.group_scatter(
        (mm_t(grad_left_pre, left_w) + mm_t(grad_right_pre, right_w)).astype(BF16)
    )
    grad_left = t_mm(mid, grad_left_pre, BF16)
    grad_right = t_mm(mid, grad_right_pre, BF16)
    grad_mid = after(grad_mid, grad_left, grad_right)
    grad_middle = cot.astype(F32) + norm_back(middle, norm_two, grad_mid)
    branch = net.group_gather(grad_middle.astype(BF16))
    branch = after(branch, output_part, grad_down)
    grad_down, grad_left, grad_right = (net.plane_sum(g) for g in (grad_down, grad_left, grad_right))
    grad_down = net.line_sum(after(grad_down, branch))
    grad_blended = mm(branch, output_w)
    grad_output = t_mm(branch, blended, BF16)
    grad_gate_pre = (grad_blended * scaled).astype(BF16)
    grad_gate = t_mm(normed, grad_gate_pre, BF16)
    grad_scaled = grad_blended * gate
    inner = net.group_sum(jnp.sum(grad_scaled * mixed, axis=1)) / features
    grad_mixed = (
        attn_scale * grad_scaled - mixed * (attn_scale * attn_scale * attn_scale) * inner[:, None]
    ).astype(BF16)
    g4 = grad_mixed.reshape(shape)
    grad_probs = jnp.einsum("rihd,rjhd->rhij", g4, v4, preferred_element_type=F32)
    grad_values = jnp.einsum("rhij,rihd->rjhd", probs, g4, preferred_element_type=F32)
    grad_value_pre = grad_values.astype(BF16).reshape(tokens, width)
    grad_value = t_mm(normed, grad_value_pre, BF16)
    grad_scores = (grad_probs * decay).astype(BF16)
    grad_queries = jnp.einsum("rhij,rjhd->rihd", grad_scores, k4, preferred_element_type=F32)
    grad_keys = jnp.einsum("rhij,rihd->rjhd", grad_scores, q4, preferred_element_type=F32)
    grad_queries, grad_keys = (after(g, grad_down) for g in (grad_queries, grad_keys))
    grad_left = net.line_sum(after(grad_left, grad_queries))
    grad_query_pre = (
        grad_queries.reshape(tokens, width) * (query_sig * (1.0 + query_pre * (1.0 - query_sig)))
    ).astype(BF16)
    grad_key_pre = (
        grad_keys.reshape(tokens, width) * (key_sig * (1.0 + key_pre * (1.0 - key_sig)))
    ).astype(BF16)
    grad_query = t_mm(normed, grad_query_pre, BF16)
    grad_key = t_mm(normed, grad_key_pre, BF16)
    grad_key = after(grad_key, grad_left)
    grad_right = net.line_sum(after(grad_right, grad_left))
    grad_output, grad_gate, grad_value, grad_query, grad_key = reduce_weights(
        wide, [grad_output, grad_gate, grad_value, grad_query, grad_key]
    )
    total = mm_t(jnp.concatenate([grad_value_pre, grad_gate_pre], axis=1), vg_w)
    total = total + mm_t(jnp.concatenate([grad_query_pre, grad_key_pre], axis=1), qk_w)
    grad_normed = net.group_scatter(total.astype(BF16))
    input_grad = net.restore(grad_middle + norm_back(inputs, norm_one, grad_normed))
    return (
        layer_output,
        input_grad,
        grad_query,
        grad_key,
        grad_value,
        grad_gate,
        grad_output,
        grad_left,
        grad_right,
        grad_down,
    )


def solution(mesh):
    both, weight = P(("wide", "narrow"), None), P("wide", "narrow")
    wide = mesh.shape["wide"]

    def body(*args):
        return on_device(*args, wide=wide)

    return jax.shard_map(
        body,
        mesh=mesh,
        in_specs=(both, P("wide", None)) + (weight,) * 8 + (both,),
        out_specs=(both, both) + (weight,) * 8,
        check_vma=False,
    )
```

```python
import functools

import jax
import jax.numpy as jnp
from jax import lax
from jax.experimental import pallas as pl
from jax.experimental.pallas import tpu as pltpu
from jax.sharding import PartitionSpec as P

HEAD_DIM = 128
LINE = 4
EPS = 1e-06
DECAY = 2.0
F32 = jnp.float32
BF16 = jnp.bfloat16


def mm(a, b, out=F32):
    return lax.dot_general(a, b, (((1,), (0,)), ((), ())), preferred_element_type=F32).astype(out)


def mm_t(a, b, out=F32):
    return lax.dot_general(a, b, (((1,), (1,)), ((), ())), preferred_element_type=F32).astype(out)


def t_mm(a, b, out=F32):
    return lax.dot_general(a, b, (((0,), (0,)), ((), ())), preferred_element_type=F32).astype(out)


def norm_scale_of(values):
    return lax.rsqrt(jnp.mean(values * values, axis=-1, keepdims=True) + EPS)


def norm_back(values, scale, gradient):
    inner = jnp.mean(gradient * values, axis=-1, keepdims=True)
    return scale * gradient - values * (scale * scale * scale) * inner


def after(value, *deps):
    return lax.optimization_barrier((value,) + deps)[0]


class Net:
    def __init__(self, wide):
        self.wide = wide
        self.me = lax.axis_index("wide")
        self.n_plane = wide // LINE
        self.lines = [
            [base + 4 * k for k in range(LINE)] for base in range(wide) if not base & 12
        ]
        self.planes = [[w for w in range(wide) if (w >> 2) % LINE == z] for z in range(LINE)]

    def flip(self, value, bit):
        return lax.ppermute(value, "wide", [(w, w ^ (1 << bit)) for w in range(self.wide)])

    def core(self, value):
        return lax.ppermute(value, "narrow", [(0, 1), (1, 0)])

    def line(self, value):
        return lax.all_to_all(
            value, "wide", 0, 0, axis_index_groups=self.lines, tiled=True
        )

    def permute(self, value):
        tokens, cols = value.shape
        value = value.reshape(tokens, self.n_plane // 4, LINE, 4, cols // self.wide)
        return value.transpose(0, 1, 3, 2, 4).reshape(tokens, cols)

    def restore(self, value):
        tokens, cols = value.shape
        value = value.reshape(tokens, self.n_plane // 4, 4, LINE, cols // self.wide)
        return value.transpose(0, 1, 3, 2, 4).reshape(tokens, cols)

    def gather(self, lined):
        return lax.all_gather(lined, "wide", axis=0, axis_index_groups=self.planes, tiled=True)

    def plane_sum(self, grad):
        return lax.psum_scatter(
            grad, "wide", scatter_dimension=0, axis_index_groups=self.planes, tiled=True
        )

    def line_sum(self, lined):
        got = self.line(lined.reshape(LINE, -1, lined.shape[1])).astype(F32)
        return jnp.concatenate([got[0] + got[2], got[1] + got[3]], axis=1)

    def group_gather(self, value):
        near = self.core(value)
        far = self.flip(value, 2)
        return jnp.concatenate([value, near, far, self.core(far)], axis=0)

    def group_sum(self, value):
        quarter = value.shape[0] // 4
        b = value.reshape(4, quarter)
        got = self.core(b)
        b = b + jnp.concatenate([got[1:2], got[0:1], got[3:4], got[2:3]])
        got = self.flip(b, 2)
        return (b + jnp.concatenate([got[2:], got[:2]])).reshape(-1)

    def group_scatter(self, value):
        quarter = value.shape[0] // 4
        b = [value[i * quarter : (i + 1) * quarter] for i in range(4)]
        got = self.core(jnp.concatenate([b[1], b[3]]))
        far = (b[2].astype(F32) + got[quarter:].astype(F32)).astype(BF16)
        own = b[0].astype(F32) + got[:quarter].astype(F32)
        return own + self.flip(far, 2).astype(F32)


def place_of(wide):
    me = lax.axis_index("wide")
    z = (me // 4) % LINE

    def on_line(k):
        there = (z + k) % LINE
        return me + (there - z) * 4, there

    def flip(bit):
        return me + (1 - 2 * ((me >> bit) & 1)) * (1 << bit)

    return me, lax.axis_index("narrow"), z, on_line, flip


def meet(devices):
    barrier = pltpu.get_barrier_semaphore()
    for device in devices:
        pl.semaphore_signal(
            barrier, inc=1, device_id=device, device_id_type=pl.DeviceIdType.MESH
        )
    pl.semaphore_wait(barrier, len(devices))


def forward_kernel(wide, small, large, *refs):
    (
        w_in, (normed_own, cot_own, x_own, ends_own),
        w_out, (normed_out, cot_out, query_pre_out, key_pre_out, gate_out, query_out, key_out, value_out, mixed_out,
                probs_out, middle_out, mid_out, left_out, right_out, product_out),
        (normed, wide_w, query_pre, key_pre, gate, query, key, value, mixed, probs, blended, part, part_core, part_far,
         square, square_core, square_far, ends_far, mid, middle, large_w, left, right, product),
        (line_send, line_recv, own_sem, plane_send, plane_recv, load_sem, save_sem, token_sem, token_send, token_recv,
         small_send, small_recv),
    ) = split_refs(refs, (8, 4, 6, 15, 24, 12))
    me, core, z, on_line, flip = place_of(wide)
    extra = list(range(4, wide.bit_length() - 1))
    plane_at = (me // 16) * 4 + me % 4
    others = [on_line(k)[0] for k in (1, 2, 3)] + [flip(b) for b in [0, 1] + extra]
    meet([(other, core) for other in others] + [(me, 1 - core)])
    rb = w_in[0].shape[0]
    q = LINE * rb
    h = q // 2
    quarter, features = x_own.shape
    row_len = 2 * quarter
    chunks = [(0, 0), (0, small), (1, 0), (1, small), (2, 0), (3, 0), (4, 0), (5, 0)]
    near_device, far_device = (me, 1 - core), (flip(2), core)


    def part_of(i, start, size):
        out, col = chunks[i]
        cols = w_in[i].shape[1] // 2
        return w_out[out].at[pl.ds(pl.multiple_of(start, min(size, rb)), size), pl.ds(col, cols)]

    def block(m):
        return (plane_at ^ m) * q

    def remote(source, target, send_sem, recv_sem, device):
        return pltpu.make_async_remote_copy(
            src_ref=source, dst_ref=target, send_sem=send_sem, recv_sem=recv_sem,
            device_id=device, device_id_type=pl.DeviceIdType.MESH,
        )

    def mine(i, there):
        cols = w_in[i].shape[1] // 2
        return w_in[i].at[:, pl.ds(pl.multiple_of((there % 2) * cols, HEAD_DIM), cols)]

    def line_copy(i, k):
        device, there = on_line(k)
        return remote(
            mine(i, there), part_of(i, block(0) + z * rb, rb),
            line_send.at[i, k - 1], line_recv.at[i, k - 1], (device, core),
        )

    def own_copy(i):
        return pltpu.make_async_copy(mine(i, z), part_of(i, block(0) + z * rb, rb), own_sem.at[i])

    def plane(i, j, start, size, bit):
        place = part_of(i, start, size)
        return remote(place, place, plane_send.at[i, j], plane_recv.at[i, j], (flip(bit), core))

    def first(i):
        return plane(i, 0, block(0), q, 0), plane(i, 1, block(0), q, 1)

    def second(i):
        return plane(i, 2, block(1), h, 1), plane(i, 3, block(2) + h, h, 0)

    def start_line(i):
        own_copy(i).start()
        for k in (1, 2, 3):
            line_copy(i, k).start()

    def start_plane(i):
        own_copy(i).wait()
        for k in (1, 2, 3):
            line_copy(i, k).wait_recv()
        for copy in first(i):
            copy.start()

    def forward_plane(i):
        for got, onward in zip(first(i), second(i)):
            got.wait_recv()
            onward.start()

    def complete(i):
        for copy in second(i):
            copy.wait_recv()
        for e, bit in enumerate(extra):
            size = q << (2 + e)
            copy = plane(i, 4 + e, (plane_at >> (2 + e)) * size, size, bit)
            copy.start()
            copy.wait()


    def rows(b):
        return pl.ds(b * quarter, quarter)

    def token_copies(n, source, out):
        send = lambda j, source, device: remote(
            source, out.at[rows(j + 1)], token_send.at[n, j], token_recv.at[n, j], device
        )
        return send(0, source, near_device), send(1, source, far_device), send(2, out.at[rows(2)], near_device)

    def start_tokens(copies):
        copies[0].start()
        copies[1].start()

    def pass_tokens(copies):
        copies[1].wait_recv()
        copies[2].start()

    def end_tokens(copies):
        copies[0].wait_recv()
        copies[2].wait_recv()

    def sent_tokens(copies):
        for copy in copies:
            copy.wait_send()

    saves = []

    def save(source, target):
        copy = pltpu.make_async_copy(source, target, save_sem.at[len(saves)])
        copy.start()
        saves.append(copy)

    normed_copies = token_copies(0, normed_own, normed)
    cot_copies = token_copies(1, cot_own, cot_out)
    mid_copies = token_copies(2, mid.at[rows(0)], mid)
    normed_local = pltpu.make_async_copy(normed_own, normed.at[rows(0)], token_sem.at[0])
    cot_local = pltpu.make_async_copy(cot_own, cot_out.at[rows(0)], token_sem.at[1])
    ends_copy = remote(ends_own, ends_far, small_send.at[0], small_recv.at[0], far_device)


    def load(i, slot):
        return pltpu.make_async_copy(
            part_of(i, 0, features), wide_w.at[slot] if i < 5 else large_w, load_sem.at[i]
        )

    def project(i, slot, keep):
        copy = load(i, slot)
        copy.start()
        copy.wait()

        def body(n, carry):
            at = pl.ds(pl.multiple_of(n * row_len, row_len), row_len)
            keep(at, jnp.dot(normed[at], wide_w[slot], preferred_element_type=F32))
            return carry

        lax.fori_loop(0, 2, body, 0)

    def keep_query(at, total):
        query_pre[at] = total.astype(BF16)
        query[at] = (total * sigmoid(total)).astype(BF16)

    def keep_key(at, total):
        key_pre[at] = total.astype(BF16)
        key[at] = (total * sigmoid(total)).astype(BF16)

    def keep_value(at, total):
        value[at] = total.astype(BF16)

    def keep_gate(at, total):
        gate[at] = total.astype(BF16)

    heads = small // HEAD_DIM
    first_head = (core * 2 + z % 2) * heads

    def attend(row, ends):
        at = pl.ds(row * row_len, row_len)

        def place(dim):
            index = lax.broadcasted_iota(jnp.int32, (row_len, row_len), dim) + core * quarter
            return jnp.where(index >= row_len, index - row_len, index).astype(F32)

        def body(head, carry):
            cols = pl.ds(pl.multiple_of(head * HEAD_DIM, HEAD_DIM), HEAD_DIM)
            scores = lax.dot_general(
                query[at, cols], key[at, cols], (((1,), (1,)), ((), ())), preferred_element_type=F32
            )
            to, source = place(0), place(1)
            allowed = (to >= source) & (to < ends[0:1, :])
            rate = (first_head + head).astype(F32) * (DECAY * HEAD_DIM / features)
            decay = jnp.where(allowed, jnp.exp(-rate * jnp.maximum(to - source, 0.0)), 0.0)
            weights = (scores * decay).astype(BF16)
            probs[row, head] = weights
            mixed[at, cols] = jnp.dot(weights, value[at, cols], preferred_element_type=F32).astype(BF16)
            return carry

        lax.fori_loop(0, heads, body, 0)
        for b in (2 * row, 2 * row + 1):
            m = mixed[rows(b)].astype(F32)
            total = jnp.sum(m * m, axis=1, keepdims=True)
            square[rows(b)] = jnp.broadcast_to(total, (quarter, HEAD_DIM))
            blended[rows(b)] = (gate[rows(b)].astype(F32) * m).astype(BF16)

    def output_part(row, slot):
        at = pl.ds(row * row_len, row_len)

        def body(n, carry):
            cols = pl.ds(pl.multiple_of(n * row_len, row_len), row_len)
            part[at, cols] = lax.dot_general(
                blended[at], wide_w[slot, cols], (((1,), (1,)), ((), ())), preferred_element_type=F32
            ).astype(BF16)
            return carry

        lax.fori_loop(0, features // row_len, body, 0)

    tile = 32

    def tiles(body):
        def step(n, carry):
            body(pl.multiple_of(n * tile, tile))
            return carry

        lax.fori_loop(0, quarter // tile, step, 0)


    normed_local.start()
    start_tokens(normed_copies)
    ends_copy.start()
    start_line(0)
    start_line(1)
    start_plane(0)
    start_line(2)
    start_plane(1)
    start_line(3)
    pass_tokens(normed_copies)
    forward_plane(0)
    start_plane(2)
    start_line(4)
    forward_plane(1)
    normed_local.wait()
    end_tokens(normed_copies)
    save(normed, normed_out)
    complete(0)
    project(0, 0, keep_query)
    save(query_pre, query_pre_out)
    save(query, query_out)
    start_plane(3)
    start_line(5)
    forward_plane(2)
    complete(1)
    project(1, 1, keep_key)
    save(key_pre, key_pre_out)
    save(key, key_out)
    start_plane(4)
    start_line(6)
    forward_plane(3)
    complete(2)
    project(2, 0, keep_value)
    save(value, value_out)
    forward_plane(4)
    complete(3)
    project(3, 1, keep_gate)
    save(gate, gate_out)
    ends_copy.wait()
    attend(1, ends_far)
    square_near = remote(
        square.at[rows(1)], square_core.at[rows(0)], small_send.at[1], small_recv.at[1], near_device
    )
    square_diag = remote(
        square.at[rows(3)], square_core.at[rows(1)], small_send.at[2], small_recv.at[2], near_device
    )
    square_pair = remote(square.at[rows(2)], square_far, small_send.at[3], small_recv.at[3], far_device)
    square_diag.start()
    start_plane(5)
    attend(0, ends_own)
    save(mixed, mixed_out)
    save(probs, probs_out)
    square_near.start()
    square_diag.wait_recv()
    square[rows(2)] += square_core[rows(1)]
    square_pair.start()
    complete(4)
    copy = load(4, 0)
    copy.start()
    copy.wait()
    output_part(1, 0)
    part_near = remote(part.at[rows(1)], part_core.at[rows(0)], small_send.at[4], small_recv.at[4], near_device)
    part_diag = remote(part.at[rows(3)], part_core.at[rows(1)], small_send.at[5], small_recv.at[5], near_device)
    part_pair = remote(part.at[rows(2)], part_far, small_send.at[6], small_recv.at[6], far_device)
    part_diag.start()
    part_diag.wait_recv()

    @tiles
    def _(start):
        here = pl.ds(start + 2 * quarter, tile)
        part[here] = (part[here].astype(F32) + part_core[pl.ds(start + quarter, tile)].astype(F32)).astype(BF16)

    part_pair.start()
    output_part(0, 0)
    part_near.start()
    forward_plane(5)
    start_plane(6)
    square_near.wait_recv()
    square_pair.wait_recv()
    part_near.wait_recv()
    part_pair.wait_recv()

    @tiles
    def _(start):
        here = pl.ds(start, tile)
        total = part[here].astype(F32) + part_core[here].astype(F32) + part_far[here].astype(F32)
        squares = square[here, 0:1] + square_core[here, 0:1] + square_far[here, 0:1]
        total = x_own[here].astype(F32) + total * lax.rsqrt(squares / features + EPS)
        middle[here] = total
        mid[here] = (total * lax.rsqrt(jnp.mean(total * total, axis=1, keepdims=True) + EPS)).astype(BF16)

    start_tokens(mid_copies)
    save(middle, middle_out)
    complete(5)
    copy = load(5, 0)
    copy.start()
    copy.wait()
    mid_copies[0].wait_recv()

    def left_rows(row):
        at = pl.ds(row * row_len, row_len)
        left[at] = jnp.dot(mid[at], large_w[...], preferred_element_type=F32).astype(BF16)

    left_rows(0)
    pass_tokens(mid_copies)
    start_line(7)
    cot_local.start()
    start_tokens(cot_copies)
    forward_plane(6)
    mid_copies[2].wait_recv()
    left_rows(1)
    save(mid, mid_out)
    save(left, left_out)
    complete(6)
    copy = load(6, 0)
    copy.start()
    copy.wait()

    def right_rows(n, carry):
        at = pl.ds(pl.multiple_of(n * row_len, row_len), row_len)
        total = jnp.dot(mid[at], large_w[...], preferred_element_type=F32)
        right[at] = total.astype(BF16)
        product[at] = (left[at].astype(F32) * total).astype(BF16)
        return carry

    start_plane(7)
    lax.fori_loop(0, 2, right_rows, 0)
    save(right, right_out)
    save(product, product_out)
    pass_tokens(cot_copies)
    forward_plane(7)
    complete(7)
    cot_local.wait()
    end_tokens(cot_copies)
    for copies in (normed_copies, cot_copies, mid_copies):
        sent_tokens(copies)
    for copy in (square_near, square_diag, square_pair, part_near, part_diag, part_pair):
        copy.wait_send()
    for i in range(8):
        for k in (1, 2, 3):
            line_copy(i, k).wait_send()
        for copy in first(i) + second(i):
            copy.wait_send()
    for copy in saves:
        copy.wait()


def split_refs(refs, counts):
    parts, at = [], 0
    for count in counts:
        parts.append(refs[at : at + count])
        at += count
    return parts


def forward(wide, weights, normed, cot, x, ends):
    small, large = weights[0].shape[1] // 2, weights[5].shape[1] // 2
    quarter, features = x.shape
    tokens, row_len, heads = 4 * quarter, 2 * quarter, small // HEAD_DIM
    steps = wide.bit_length() - 1
    anywhere, vmem = pl.BlockSpec(memory_space=pl.ANY), pl.BlockSpec(memory_space=pltpu.VMEM)
    dma = pltpu.SemaphoreType.DMA
    outs = [
        ((features, 2 * small), BF16),
        ((features, 2 * small), BF16),
        ((features, small), BF16),
        ((features, large), BF16),
        ((features, large), BF16),
        ((features, large), BF16),
        ((tokens, features), BF16),
        ((tokens, features), BF16),
        ((tokens, small), BF16),
        ((tokens, small), BF16),
        ((tokens, small), BF16),
        ((tokens, small), BF16),
        ((tokens, small), BF16),
        ((tokens, small), BF16),
        ((tokens, small), BF16),
        ((2, heads, row_len, row_len), BF16),
        ((quarter, features), F32),
        ((tokens, features), BF16),
        ((tokens, large), BF16),
        ((tokens, large), BF16),
        ((tokens, large), BF16),
    ]
    held = [
        ((tokens, features), BF16),
        ((2, features, small), BF16),
        ((tokens, small), BF16),
        ((tokens, small), BF16),
        ((tokens, small), BF16),
        ((tokens, small), BF16),
        ((tokens, small), BF16),
        ((tokens, small), BF16),
        ((tokens, small), BF16),
        ((2, heads, row_len, row_len), BF16),
        ((tokens, small), BF16),
        ((tokens, features), BF16),
        ((row_len, features), BF16),
        ((quarter, features), BF16),
        ((tokens, HEAD_DIM), F32),
        ((row_len, HEAD_DIM), F32),
        ((quarter, HEAD_DIM), F32),
        (ends.shape, F32),
        ((tokens, features), BF16),
        ((quarter, features), F32),
        ((features, large), BF16),
        ((tokens, large), BF16),
        ((tokens, large), BF16),
        ((tokens, large), BF16),
    ]
    sems = [(8, 3), (8, 3), (8,), (8, steps), (8, steps), (8,), (14,), (2,), (3, 3), (3, 3), (7,), (7,)]
    return pl.pallas_call(
        functools.partial(forward_kernel, wide, small, large),
        out_shape=[jax.ShapeDtypeStruct(s, t) for s, t in outs],
        in_specs=[anywhere] * 10 + [vmem] * 2,
        out_specs=[anywhere] * len(outs),
        scratch_shapes=[pltpu.VMEM(s, t) for s, t in held] + [dma(s) for s in sems],
        compiler_params=pltpu.CompilerParams(
            has_side_effects=True, collective_id=1, vmem_limit_bytes=60 << 20
        ),
        cost_estimate=pl.CostEstimate(flops=0, bytes_accessed=300 << 20, transcendentals=0),
    )(*weights, normed, cot, x, ends)


def backward_kernel(wide, small, large, *refs):
    (
        (branch_in, normed_in, gate_in, mixed_in, query_pre_in, key_pre_in, query_in, key_in, value_in, probs_in,
         blended_in, output_w, vg_w, qk_w, right_in, left_in, down_in, scale, ends),
        (output_out, gate_out, value_out, query_out, key_out, right_out, left_out, down_out, normed_grad_out,
         big_near, big_far, big_line),
        (branch, normed, weights, gate, mixed, query_pre, key_pre, query, key, value, grad_blended, grad_mixed, blended,
         vg_grad, qk_grad, inner, inner_core, inner_sum, inner_far, inner_col, part_core, part_far, held, near, far,
         line, stage, added, small_result, big_result),
        (load_sem, send, recv, line_send, line_recv, big_send, big_recv, big_line_send, big_line_recv, small_send,
         small_recv, stage_sem, result_sem, more_send, more_recv),
    ) = split_refs(refs, (19, 12, 30, 15))
    me, core, z, on_line, flip = place_of(wide)
    extra = list(range(4, wide.bit_length() - 1))
    plane_at = (me // 16) * 4 + me % 4
    others = [on_line(k)[0] for k in (1, 2, 3)] + [flip(b) for b in [0, 1] + extra]
    tokens, features = branch.shape
    quarter, row_len = tokens // 4, tokens // 2
    rb = features // wide
    q = LINE * rb
    h = q // 2
    heads = small // HEAD_DIM
    near_device, far_device = (me, 1 - core), (flip(2), core)
    lower = z % 2 == 0

    def remote(source, target, send_sem, recv_sem, device):
        return pltpu.make_async_remote_copy(
            src_ref=source, dst_ref=target, send_sem=send_sem, recv_sem=recv_sem,
            device_id=device, device_id_type=pl.DeviceIdType.MESH,
        )

    def block(m):
        return pl.multiple_of((plane_at ^ m) * q, q)

    def rows(b):
        return pl.ds(b * quarter, quarter)

    def loops(count, body):
        def step(n, carry):
            body(n)
            return carry

        lax.fori_loop(0, count, step, 0)

    pending = {}

    def load(name, source, target):
        copy = pltpu.make_async_copy(source, target, load_sem.at[len(pending)])
        copy.start()
        pending[name] = copy

    def ready(*names):
        for name in names:
            pending[name].wait()

    results = []

    def give(source, target):
        copy = pltpu.make_async_copy(source, target, result_sem.at[len(results)])
        copy.start()
        results.append(copy)
        return len(results) - 1

    def given(n):
        if results[n] is not None:
            results[n].wait()
            results[n] = None

    load("branch", branch_in, branch)
    for n in range(4):
        load("output%d" % n, output_w.at[pl.ds(n * row_len, row_len)], weights.at[n, :, pl.ds(0, small)])
    load("gate", gate_in, gate)
    load("mixed", mixed_in, mixed)
    load("blended", blended_in, blended)
    load("normed", normed_in, normed)
    load("value", value_in, value)
    load("query", query_in, query)
    load("key", key_in, key)
    for r in range(2):
        for n in range(heads):
            load("probs%d%d" % (r, n), probs_in.at[r, n], held.at[3 + r, pl.ds(n * row_len, row_len)])
    load("query_pre", query_pre_in, query_pre)
    load("key_pre", key_pre_in, key_pre)
    meet([(other, core) for other in others] + [(me, 1 - core)])


    def rows_at(i, start, size):
        return held.at[i, pl.ds(pl.multiple_of(start, min(size, h)), size)]

    def step(i, j, start, size, target, bit):
        return remote(rows_at(i, start, size), target, send.at[i, j], recv.at[i, j], (flip(bit), core))

    def copies(i, j):
        if j == 0:
            return step(i, 0, block(3), h, near.at[i, 0], 1)
        if j == 1:
            return step(i, 1, block(3) + h, h, near.at[i, 1], 0)
        if j == 2:
            return step(i, 2, block(1) + h, h, far.at[i, 0, pl.ds(h, h)], 0)
        if j == 3:
            return step(i, 3, block(2), h, far.at[i, 1, pl.ds(0, h)], 1)
        if j == 4:
            return step(i, 4, block(1), h, far.at[i, 0, pl.ds(0, h)], 0)
        return step(i, 5, block(2) + h, h, far.at[i, 1, pl.ds(h, h)], 1)

    def line_copy(i, k):
        device, there = on_line(k)
        return remote(
            rows_at(i, block(0) + there * rb, rb), line.at[i, k - 1],
            line_send.at[i, k - 1], line_recv.at[i, k - 1], (device, core),
        )

    tile = min(64, h)

    def add(target, start, size, *sources):
        def body(n):
            at = pl.ds(pl.multiple_of(start + n * tile, tile), tile)
            total = target[at].astype(F32)
            for source in sources:
                total = total + source[pl.ds(pl.multiple_of(n * tile, tile), tile)].astype(F32)
            target[at] = total.astype(BF16)

        loops(size // tile, body)

    def begin(i, side, other):
        def fill(m):
            held[i, pl.ds(block(m), q)] = lax.dot_general(
                side[:, pl.ds(block(m), q)], other(), (((0,), (0,)), ((), ())), preferred_element_type=F32
            ).astype(BF16)

        if extra:
            loops(wide // LINE, fill)
            for e in reversed(range(len(extra))):
                size = q << (2 + e)
                half = plane_at >> (2 + e)
                copy = remote(
                    rows_at(i, (half ^ 1) * size, size), branch_more(i, e, size),
                    more_send.at[i, e], more_recv.at[i, e], (flip(extra[e]), core),
                )
                copy.start()
                copy.wait()
                add(held.at[i], half * size, size, branch_more(i, e, size))
            for j in range(4):
                copies(i, j).start()
        else:
            fill(3)
            copies(i, 0).start()
            copies(i, 1).start()
            fill(1)
            copies(i, 2).start()
            fill(2)
            copies(i, 3).start()
            fill(0)

    def branch_more(i, e, size):
        return far.at[i, e, pl.ds(0, size)]

    def fold(i):
        copies(i, 0).wait_recv()
        add(held.at[i], block(1), h, near.at[i, 0])
        copies(i, 4).start()
        copies(i, 1).wait_recv()
        add(held.at[i], block(2) + h, h, near.at[i, 1])
        copies(i, 5).start()

    def to_line(i):
        for j in range(2, 6):
            copies(i, j).wait_recv()
        add(held.at[i], block(0), q, far.at[i, 0], far.at[i, 1])
        for k in (1, 2, 3):
            line_copy(i, k).start()

    def finish(i, out):
        for k in (1, 2, 3):
            line_copy(i, k).wait_recv()
        own = held[i, pl.ds(block(0) + pl.multiple_of(z * rb, rb), rb)].astype(F32) + line[i, 1].astype(F32)
        other = line[i, 0].astype(F32) + line[i, 2].astype(F32)
        put(small_result.at[i % 2], own, other, small)
        return give(small_result.at[i % 2], out)

    def put(target, own, other, cols):
        @pl.when(lower)
        def _():
            target[:, pl.ds(0, cols)] = own
            target[:, pl.ds(cols, cols)] = other

        @pl.when(jnp.logical_not(lower))
        def _():
            target[:, pl.ds(0, cols)] = other
            target[:, pl.ds(cols, cols)] = own


    stage_count = [0]

    def stage_in(source, target):
        copy = pltpu.make_async_copy(source, target, stage_sem.at[stage_count[0]])
        stage_count[0] += 1
        copy.start()
        return copy

    def big_rows(start, size):
        return right_in.at[pl.ds(pl.multiple_of(start, min(size, h)), size)]

    def big_copy(j):
        sources = (
            lambda: big_rows(block(3), h), lambda: big_rows(block(3) + h, h), lambda: big_rows(block(1) + h, h),
            lambda: big_rows(block(2), h), lambda: stage.at[pl.ds(0, h)], lambda: stage.at[pl.ds(h, h)],
        )
        targets = (
            lambda: big_near.at[0], lambda: big_near.at[1], lambda: big_far.at[0, pl.ds(h, h)],
            lambda: big_far.at[1, pl.ds(0, h)], lambda: big_far.at[0, pl.ds(0, h)], lambda: big_far.at[1, pl.ds(h, h)],
        )
        bit = (1, 0, 0, 1, 0, 1)[j]
        return remote(sources[j](), targets[j](), big_send.at[j], big_recv.at[j], (flip(bit), core))

    def big_begin():
        for j in range(4):
            big_copy(j).start()

    def big_fold():
        for n, (m, start) in enumerate(((1, 0), (2, h))):
            here = pl.ds(n * h, h)
            first = stage_in(big_rows(block(m) + start, h), stage.at[here])
            big_copy(n).wait_recv()
            second = stage_in(big_near.at[n], added.at[here])
            first.wait()
            second.wait()
            add(stage, n * h, h, added.at[here])
            big_copy(4 + n).start()

    def big_to_line():
        for j in range(2, 6):
            big_copy(j).wait_recv()
        for j in (4, 5):
            big_copy(j).wait_send()
        stage_in(big_rows(block(0), q), stage).wait()
        for n in range(2):
            a = stage_in(big_far.at[0, pl.ds(n * h, h)], added.at[pl.ds(0, h)])
            b = stage_in(big_far.at[1, pl.ds(n * h, h)], added.at[pl.ds(h, h)])
            a.wait()
            b.wait()
            add(stage, n * h, h, added.at[pl.ds(0, h)], added.at[pl.ds(h, h)])
        for k in (1, 2, 3):
            big_line_copy(0, k).start()

    def big_line_copy(n, k):
        device, there = on_line(k)
        source = (stage, left_in, down_in)[n]
        return remote(
            source.at[pl.ds(pl.multiple_of(there * rb, rb), rb)], big_line.at[n, k - 1],
            big_line_send.at[n, k - 1], big_line_recv.at[n, k - 1], (device, core),
        )

    def big_finish(n, out):
        for k in (1, 2, 3):
            big_line_copy(n, k).wait_recv()
        source = (stage, left_in, down_in)[n]
        moves = [stage_in(big_line.at[n, k], added.at[pl.ds(k * rb, rb)]) for k in range(3)]
        moves.append(stage_in(source.at[pl.ds(pl.multiple_of(z * rb, rb), rb)], added.at[pl.ds(3 * rb, rb)]))
        for move in moves:
            move.wait()
        for n_big in results_of_big:
            given(n_big)
        got = [added[pl.ds(k * rb, rb)].astype(F32) for k in range(4)]
        put(big_result, got[3] + got[1], got[0] + got[2], large)
        results_of_big.append(give(big_result, out))

    results_of_big = []


    def grad_rows(row):
        at = pl.ds(row * row_len, row_len)
        total = jnp.zeros((row_len, small), F32)
        for n in range(4):
            total = total + jnp.dot(
                branch[at, pl.ds(n * row_len, row_len)], weights[n, :, pl.ds(0, small)], preferred_element_type=F32
            )
        grad_blended[at] = total
        m = mixed[at].astype(F32)
        vg_grad[at, pl.ds(small, small)] = (total * (m * scale[at, 0:1])).astype(BF16)
        inner[:, at] = lax.dot_general(
            jnp.ones((8, small), F32), total * gate[at].astype(F32) * m, (((1,), (1,)), ((), ())),
            preferred_element_type=F32, precision=lax.Precision.HIGHEST,
        )

    def mix_rows(n):
        at = pl.ds(pl.multiple_of(n * 128, 128), 128)
        s = scale[at, 0:1]
        value_of = s * (grad_blended[at] * gate[at].astype(F32))
        value_of = value_of - mixed[at].astype(F32) * (s * s * s * (inner_col[at, 0:1] / features))
        grad_mixed[at] = value_of.astype(BF16)

    first_head = (core * 2 + z % 2) * heads

    def attend_back(row):
        at = pl.ds(row * row_len, row_len)

        def place(dim):
            index = lax.broadcasted_iota(jnp.int32, (row_len, row_len), dim) + core * quarter
            return jnp.where(index >= row_len, index - row_len, index).astype(F32)

        def slope(pre):
            s = sigmoid(pre)
            return s * (1.0 + pre * (1.0 - s))

        def body(head):
            cols = pl.ds(pl.multiple_of(head * HEAD_DIM, HEAD_DIM), HEAD_DIM)
            more = pl.ds(pl.multiple_of(small + head * HEAD_DIM, HEAD_DIM), HEAD_DIM)
            got = grad_mixed[at, cols]
            grad_probs = lax.dot_general(
                got, value[at, cols], (((1,), (1,)), ((), ())), preferred_element_type=F32
            )
            to, source = place(0), place(1)
            allowed = (to >= source) & (to < ends[pl.ds(8 * row, 1), :])
            rate = (first_head + head).astype(F32) * (DECAY * HEAD_DIM / features)
            decay = jnp.where(allowed, jnp.exp(-rate * jnp.maximum(to - source, 0.0)), 0.0)
            grad_scores = (grad_probs * decay).astype(BF16)
            probs = held[3 + row, pl.ds(pl.multiple_of(head * row_len, row_len), row_len)]
            vg_grad[at, cols] = lax.dot_general(
                probs, got, (((0,), (0,)), ((), ())), preferred_element_type=F32
            ).astype(BF16)
            grad_query = jnp.dot(grad_scores, key[at, cols], preferred_element_type=F32)
            qk_grad[at, cols] = (grad_query * slope(query_pre[at, cols].astype(F32))).astype(BF16)
            grad_key = lax.dot_general(
                grad_scores, query[at, cols], (((0,), (0,)), ((), ())), preferred_element_type=F32
            )
            qk_grad[at, more] = (grad_key * slope(key_pre[at, cols].astype(F32))).astype(BF16)

        loops(heads, body)

    def load_weights(pair):
        for n in range(2):
            here = pl.ds((2 * pair + n) * row_len, row_len)
            load("vg%d%d" % (pair, n), vg_w.at[here], weights.at[n])
            load("qk%d%d" % (pair, n), qk_w.at[here], weights.at[2 + n])

    def normed_part(pair, row):
        at = pl.ds(row * row_len, row_len)
        for n in range(2):
            total = lax.dot_general(vg_grad[at], weights[n], (((1,), (1,)), ((), ())), preferred_element_type=F32)
            total = total + lax.dot_general(
                qk_grad[at], weights[2 + n], (((1,), (1,)), ((), ())), preferred_element_type=F32
            )
            branch[at, pl.ds((2 * pair + n) * row_len, row_len)] = total.astype(BF16)


    big_begin()
    ready("branch", "output0", "output1", "output2", "output3", "gate", "mixed")
    grad_rows(1)
    grad_rows(0)
    core_copy = remote(inner, inner_core, small_send.at[0], small_recv.at[0], near_device)
    core_copy.start()
    ready("blended")
    core_copy.wait_recv()
    for b in range(4):
        inner_sum[:, rows(b)] = inner[:, rows(b)] + inner_core[:, rows(b ^ 1)]
    far_copy = remote(inner_sum, inner_far, small_send.at[1], small_recv.at[1], far_device)
    far_copy.start()
    begin(0, branch, lambda: blended[...])
    far_copy.wait_recv()
    for b in range(4):
        total = inner_sum[:, rows(b)] + inner_far[:, rows(b ^ 2)]
        inner_col[rows(b)] = jnp.broadcast_to(total.T[:, 0:1], (quarter, HEAD_DIM))
    for n in (2, 1):
        for k in (1, 2, 3):
            big_line_copy(n, k).start()
    loops(tokens // 128, mix_rows)
    load_weights(0)
    ready("normed")
    begin(1, normed, lambda: vg_grad[:, pl.ds(small, small)])
    ready("value", "query", "key", "query_pre", "key_pre")
    for r in range(2):
        ready(*("probs%d%d" % (r, n) for n in range(heads)))
    attend_back(1)
    big_fold()
    fold(0)
    attend_back(0)
    begin(2, normed, lambda: vg_grad[:, pl.ds(0, small)])
    fold(1)
    begin(3, normed, lambda: qk_grad[:, pl.ds(0, small)])
    begin(4, normed, lambda: qk_grad[:, pl.ds(small, small)])
    big_to_line()
    to_line(0)
    fold(2)
    ready("vg00", "vg01", "qk00", "qk01")
    normed_part(0, 1)
    normed_part(0, 0)
    load_weights(1)
    to_line(1)
    ready("vg10", "vg11", "qk10", "qk11")
    normed_part(1, 1)
    part_near = remote(branch.at[rows(1)], part_core.at[rows(0)], small_send.at[2], small_recv.at[2], near_device)
    part_diag = remote(branch.at[rows(3)], part_core.at[rows(1)], small_send.at[3], small_recv.at[3], near_device)
    part_pair = remote(branch.at[rows(2)], part_far, small_send.at[4], small_recv.at[4], far_device)
    part_diag.start()
    normed_part(1, 0)
    part_near.start()
    part_diag.wait_recv()
    add(branch, 2 * quarter, quarter, part_core.at[rows(1)])
    part_pair.start()
    fold(3)
    fold(4)
    to_line(2)
    big_finish(2, down_out)
    big_finish(1, left_out)
    first = finish(0, output_out)
    second = finish(1, gate_out)
    to_line(3)
    big_finish(0, right_out)
    given(first)
    first = finish(2, value_out)
    to_line(4)
    part_near.wait_recv()
    part_pair.wait_recv()
    add(part_far, 0, quarter, branch.at[rows(0)], part_core.at[rows(0)])
    give(part_far, normed_grad_out)
    given(second)
    finish(3, query_out)
    given(first)
    finish(4, key_out)
    for copy in (core_copy, far_copy, part_near, part_diag, part_pair):
        copy.wait_send()
    for i in range(5):
        for j in range(6):
            copies(i, j).wait_send()
        for k in (1, 2, 3):
            line_copy(i, k).wait_send()
    for j in range(4):
        big_copy(j).wait_send()
    for n in range(3):
        for k in (1, 2, 3):
            big_line_copy(n, k).wait_send()
    for n in range(len(results)):
        given(n)


def backward(wide, arrays, small, large):
    tokens, features = arrays[0].shape
    quarter, row_len = tokens // 4, tokens // 2
    rb = features // wide
    q = LINE * rb
    extra = max(1, wide.bit_length() - 5)
    anywhere, vmem = pl.BlockSpec(memory_space=pl.ANY), pl.BlockSpec(memory_space=pltpu.VMEM)
    dma = pltpu.SemaphoreType.DMA
    far_rows = q if wide == 16 else features // 2
    outs = [((rb, 2 * small), F32)] * 5 + [((rb, 2 * large), F32)] * 3 + [
        ((quarter, features), BF16),
        ((2, q // 2, large), BF16),
        ((2, q, large), BF16),
        ((3, 3, rb, large), BF16),
    ]
    held = [
        ((tokens, features), BF16),
        ((tokens, features), BF16),
        ((4, row_len, 2 * small), BF16),
        ((tokens, small), BF16),
        ((tokens, small), BF16),
        ((tokens, small), BF16),
        ((tokens, small), BF16),
        ((tokens, small), BF16),
        ((tokens, small), BF16),
        ((tokens, small), BF16),
        ((tokens, small), F32),
        ((tokens, small), BF16),
        ((tokens, small), BF16),
        ((tokens, 2 * small), BF16),
        ((tokens, 2 * small), BF16),
        ((8, tokens), F32),
        ((8, tokens), F32),
        ((8, tokens), F32),
        ((8, tokens), F32),
        ((tokens, HEAD_DIM), F32),
        ((row_len, features), BF16),
        ((quarter, features), BF16),
        ((5, features, small), BF16),
        ((5, 2, q // 2, small), BF16),
        ((5, 2, far_rows, small), BF16),
        ((5, 3, rb, small), BF16),
        ((q, large), BF16),
        ((q, large), BF16),
        ((2, rb, 2 * small), F32),
        ((rb, 2 * large), F32),
    ]
    sems = [
        (40,), (5, 6), (5, 6), (5, 3), (5, 3), (6,), (6,), (3, 3), (3, 3), (5,), (5,), (24,), (9,), (5, extra), (5, extra),
    ]
    return pl.pallas_call(
        functools.partial(backward_kernel, wide, small, large),
        out_shape=[jax.ShapeDtypeStruct(s, t) for s, t in outs],
        in_specs=[anywhere] * 17 + [vmem] * 2,
        out_specs=[anywhere] * len(outs),
        scratch_shapes=[pltpu.VMEM(s, t) for s, t in held] + [dma(s) for s in sems],
        compiler_params=pltpu.CompilerParams(
            has_side_effects=True, collective_id=2, vmem_limit_bytes=60 << 20
        ),
        cost_estimate=pl.CostEstimate(flops=0, bytes_accessed=300 << 20, transcendentals=0),
    )(*arrays)


def ends_of(lengths, places):
    total, ends = 0, 0
    for c in range(lengths.shape[1]):
        ends = ends + jnp.where(places >= total, lengths[0, c], 0)
        total = total + lengths[0, c]
    return jnp.broadcast_to(ends.astype(F32)[None], (8, places.shape[0]))


def sigmoid(z):
    return 1.0 / (1.0 + jnp.exp(-z))


def on_device(
    layer_input, doc_lengths, w_query, w_key, w_value, w_gate, w_output, w_left, w_right, w_down, cotangent, *, wide
):
    net = Net(wide)
    core = lax.axis_index("narrow")
    half = (net.me >> 2) & 1
    features = layer_input.shape[1]

    x = net.permute(layer_input)
    inputs = x.astype(F32)
    norm_one = norm_scale_of(inputs)
    cot = net.permute(cotangent)
    quarter = inputs.shape[0]
    tokens = 4 * quarter
    row_len = 2 * quarter
    own = jnp.arange(quarter, dtype=jnp.int32)
    places = jnp.concatenate([own + core * quarter, own + (1 - core) * quarter])
    (
        qk_w, vg_w, output_w, left_w, right_w, down_w, normed, cot_all, query_pre, key_pre, gate, queries, keys, values,
        mixed, probs, middle, mid, left, right, product,
    ) = forward(
        wide,
        [w_query, w_key, w_value, w_gate, w_output, w_left, w_right, w_down],
        (inputs * norm_one).astype(BF16),
        cot,
        x,
        ends_of(doc_lengths, places),
    )

    mixed_32 = mixed.astype(F32)
    squares = net.group_sum(jnp.sum(mixed_32 * mixed_32, axis=1))
    attn_scale = lax.rsqrt(squares / features + EPS)[:, None]
    blended = (gate.astype(F32) * (mixed_32 * attn_scale)).astype(BF16)
    both_ends = jnp.concatenate([ends_of(doc_lengths, places), ends_of(net.flip(doc_lengths, 2), places)])
    norm_two = norm_scale_of(middle)
    grad_down = t_mm(cot_all, product, BF16)
    output_part = mm_t(product, down_w, BF16)
    layer_output = middle + net.group_scatter(output_part)
    layer_output = net.restore(layer_output.astype(BF16))

    grad_product = mm(cot_all, down_w)
    grad_left_pre = (grad_product * right.astype(F32)).astype(BF16)
    grad_right_pre = (grad_product * left.astype(F32)).astype(BF16)
    grad_mid = net.group_scatter(
        (mm_t(grad_left_pre, left_w) + mm_t(grad_right_pre, right_w)).astype(BF16)
    )
    grad_left = t_mm(mid, grad_left_pre, BF16)
    grad_right = t_mm(mid, grad_right_pre, BF16)
    grad_mid = after(grad_mid, grad_left, grad_right)
    grad_middle = cot.astype(F32) + norm_back(middle, norm_two, grad_mid)
    branch = net.group_gather(grad_middle.astype(BF16))
    branch = after(branch, output_part, grad_down)
    grad_down, grad_left = net.plane_sum(grad_down), net.plane_sum(grad_left)
    (
        grad_output, grad_gate, grad_value, grad_query, grad_key, grad_right, grad_left, grad_down, grad_normed, *_
    ) = backward(
        wide,
        [
            branch, normed, gate, mixed, query_pre, key_pre, queries, keys, values, probs, blended, output_w, vg_w, qk_w,
            grad_right, grad_left, grad_down, jnp.broadcast_to(attn_scale, (tokens, HEAD_DIM)), both_ends,
        ],
        queries.shape[1],
        left.shape[1],
    )
    grad_normed = grad_normed.astype(F32)
    input_grad = net.restore(grad_middle + norm_back(inputs, norm_one, grad_normed))
    return (
        layer_output,
        input_grad,
        grad_query,
        grad_key,
        grad_value,
        grad_gate,
        grad_output,
        grad_left,
        grad_right,
        grad_down,
    )


def solution(mesh):
    both, weight = P(("wide", "narrow"), None), P("wide", "narrow")
    wide = mesh.shape["wide"]

    def body(*args):
        return on_device(*args, wide=wide)

    return jax.shard_map(
        body,
        mesh=mesh,
        in_specs=(both, P("wide", None)) + (weight,) * 8 + (both,),
        out_specs=(both, both) + (weight,) * 8,
        check_vma=False,
    )
```

```python
import functools

import jax
import jax.numpy as jnp
from jax import lax
from jax.experimental import pallas as pl
from jax.experimental.pallas import tpu as pltpu
from jax.sharding import PartitionSpec as P

HEAD_DIM = 128
LINE = 4
EPS = 1e-06
DECAY = 2.0
F32 = jnp.float32
BF16 = jnp.bfloat16


def mm(a, b, out=F32):
    return lax.dot_general(a, b, (((1,), (0,)), ((), ())), preferred_element_type=F32).astype(out)


def mm_t(a, b, out=F32):
    return lax.dot_general(a, b, (((1,), (1,)), ((), ())), preferred_element_type=F32).astype(out)


def t_mm(a, b, out=F32):
    return lax.dot_general(a, b, (((0,), (0,)), ((), ())), preferred_element_type=F32).astype(out)


def norm_scale_of(values):
    return lax.rsqrt(jnp.mean(values * values, axis=-1, keepdims=True) + EPS)


def norm_back(values, scale, gradient):
    inner = jnp.mean(gradient * values, axis=-1, keepdims=True)
    return scale * gradient - values * (scale * scale * scale) * inner


def after(value, *deps):
    return lax.optimization_barrier((value,) + deps)[0]


class Net:
    def __init__(self, wide):
        self.wide = wide
        self.me = lax.axis_index("wide")
        self.n_plane = wide // LINE
        self.lines = [
            [base + 4 * k for k in range(LINE)] for base in range(wide) if not base & 12
        ]
        self.planes = [[w for w in range(wide) if (w >> 2) % LINE == z] for z in range(LINE)]

    def flip(self, value, bit):
        return lax.ppermute(value, "wide", [(w, w ^ (1 << bit)) for w in range(self.wide)])

    def core(self, value):
        return lax.ppermute(value, "narrow", [(0, 1), (1, 0)])

    def line(self, value):
        return lax.all_to_all(
            value, "wide", 0, 0, axis_index_groups=self.lines, tiled=True
        )

    def permute(self, value):
        tokens, cols = value.shape
        value = value.reshape(tokens, self.n_plane // 4, LINE, 4, cols // self.wide)
        return value.transpose(0, 1, 3, 2, 4).reshape(tokens, cols)

    def restore(self, value):
        tokens, cols = value.shape
        value = value.reshape(tokens, self.n_plane // 4, 4, LINE, cols // self.wide)
        return value.transpose(0, 1, 3, 2, 4).reshape(tokens, cols)

    def gather(self, lined):
        return lax.all_gather(lined, "wide", axis=0, axis_index_groups=self.planes, tiled=True)

    def plane_sum(self, grad):
        return lax.psum_scatter(
            grad, "wide", scatter_dimension=0, axis_index_groups=self.planes, tiled=True
        )

    def line_sum(self, lined):
        got = self.line(lined.reshape(LINE, -1, lined.shape[1])).astype(F32)
        return jnp.concatenate([got[0] + got[2], got[1] + got[3]], axis=1)

    def group_gather(self, value):
        near = self.core(value)
        far = self.flip(value, 2)
        return jnp.concatenate([value, near, far, self.core(far)], axis=0)

    def group_sum(self, value):
        quarter = value.shape[0] // 4
        b = value.reshape(4, quarter)
        got = self.core(b)
        b = b + jnp.concatenate([got[1:2], got[0:1], got[3:4], got[2:3]])
        got = self.flip(b, 2)
        return (b + jnp.concatenate([got[2:], got[:2]])).reshape(-1)

    def group_scatter(self, value):
        quarter = value.shape[0] // 4
        b = [value[i * quarter : (i + 1) * quarter] for i in range(4)]
        got = self.core(jnp.concatenate([b[1], b[3]]))
        far = (b[2].astype(F32) + got[quarter:].astype(F32)).astype(BF16)
        own = b[0].astype(F32) + got[:quarter].astype(F32)
        return own + self.flip(far, 2).astype(F32)


def place_of(wide):
    me = lax.axis_index("wide")
    z = (me // 4) % LINE

    def on_line(k):
        there = (z + k) % LINE
        return me + (there - z) * 4, there

    def flip(bit):
        return me + (1 - 2 * ((me >> bit) & 1)) * (1 << bit)

    return me, lax.axis_index("narrow"), z, on_line, flip


def meet(devices):
    barrier = pltpu.get_barrier_semaphore()
    for device in devices:
        pl.semaphore_signal(
            barrier, inc=1, device_id=device, device_id_type=pl.DeviceIdType.MESH
        )
    pl.semaphore_wait(barrier, len(devices))


def forward_kernel(wide, small, large, *refs):
    (
        w_in, (normed_own, cot_own, x_own, ends_own),
        w_out, (normed_out, cot_out, query_pre_out, key_pre_out, gate_out, query_out, key_out, value_out, mixed_out,
                probs_out, middle_out, mid_out, left_out, right_out, product_out, square_out, ends_out),
        (normed, wide_w, query_pre, key_pre, gate, query, key, value, mixed, probs, blended, part, part_core, part_far,
         square, square_core, square_far, square_all, ends_far, mid, middle, large_w, left, right, product),
        (line_send, line_recv, own_sem, plane_send, plane_recv, load_sem, save_sem, token_sem, token_send, token_recv,
         small_send, small_recv),
    ) = split_refs(refs, (8, 4, 6, 17, 25, 12))
    me, core, z, on_line, flip = place_of(wide)
    extra = list(range(4, wide.bit_length() - 1))
    plane_at = (me // 16) * 4 + me % 4
    others = [on_line(k)[0] for k in (1, 2, 3)] + [flip(b) for b in [0, 1] + extra]
    meet([(other, core) for other in others] + [(me, 1 - core)])
    rb = w_in[0].shape[0]
    q = LINE * rb
    h = q // 2
    quarter, features = x_own.shape
    row_len = 2 * quarter
    chunks = [(0, 0), (0, small), (1, 0), (1, small), (2, 0), (3, 0), (4, 0), (5, 0)]
    near_device, far_device = (me, 1 - core), (flip(2), core)


    def part_of(i, start, size):
        out, col = chunks[i]
        cols = w_in[i].shape[1] // 2
        return w_out[out].at[pl.ds(pl.multiple_of(start, min(size, rb)), size), pl.ds(col, cols)]

    def block(m):
        return (plane_at ^ m) * q

    def remote(source, target, send_sem, recv_sem, device):
        return pltpu.make_async_remote_copy(
            src_ref=source, dst_ref=target, send_sem=send_sem, recv_sem=recv_sem,
            device_id=device, device_id_type=pl.DeviceIdType.MESH,
        )

    def mine(i, there):
        cols = w_in[i].shape[1] // 2
        return w_in[i].at[:, pl.ds(pl.multiple_of((there % 2) * cols, HEAD_DIM), cols)]

    def line_copy(i, k):
        device, there = on_line(k)
        return remote(
            mine(i, there), part_of(i, block(0) + z * rb, rb),
            line_send.at[i, k - 1], line_recv.at[i, k - 1], (device, core),
        )

    def own_copy(i):
        return pltpu.make_async_copy(mine(i, z), part_of(i, block(0) + z * rb, rb), own_sem.at[i])

    def plane(i, j, start, size, bit):
        place = part_of(i, start, size)
        return remote(place, place, plane_send.at[i, j], plane_recv.at[i, j], (flip(bit), core))

    def first(i):
        return plane(i, 0, block(0), q, 0), plane(i, 1, block(0), q, 1)

    def second(i):
        return plane(i, 2, block(1), h, 1), plane(i, 3, block(2) + h, h, 0)

    def start_line(i):
        own_copy(i).start()
        for k in (1, 2, 3):
            line_copy(i, k).start()

    def start_plane(i):
        own_copy(i).wait()
        for k in (1, 2, 3):
            line_copy(i, k).wait_recv()
        for copy in first(i):
            copy.start()

    def forward_plane(i):
        for got, onward in zip(first(i), second(i)):
            got.wait_recv()
            onward.start()

    def complete(i):
        for copy in second(i):
            copy.wait_recv()
        for e, bit in enumerate(extra):
            size = q << (2 + e)
            copy = plane(i, 4 + e, (plane_at >> (2 + e)) * size, size, bit)
            copy.start()
            copy.wait()


    def rows(b):
        return pl.ds(b * quarter, quarter)

    def token_copies(n, source, out):
        send = lambda j, source, device: remote(
            source, out.at[rows(j + 1)], token_send.at[n, j], token_recv.at[n, j], device
        )
        return send(0, source, near_device), send(1, source, far_device), send(2, out.at[rows(2)], near_device)

    def start_tokens(copies):
        copies[0].start()
        copies[1].start()

    def pass_tokens(copies):
        copies[1].wait_recv()
        copies[2].start()

    def end_tokens(copies):
        copies[0].wait_recv()
        copies[2].wait_recv()

    def sent_tokens(copies):
        for copy in copies:
            copy.wait_send()

    saves = []

    def save(source, target):
        copy = pltpu.make_async_copy(source, target, save_sem.at[len(saves)])
        copy.start()
        saves.append(copy)

    normed_copies = token_copies(0, normed_own, normed)
    cot_copies = token_copies(1, cot_own, cot_out)
    mid_copies = token_copies(2, mid.at[rows(0)], mid)
    square_copies = token_copies(3, square_all.at[rows(0)], square_all)
    normed_local = pltpu.make_async_copy(normed_own, normed.at[rows(0)], token_sem.at[0])
    cot_local = pltpu.make_async_copy(cot_own, cot_out.at[rows(0)], token_sem.at[1])
    ends_copy = remote(ends_own, ends_far, small_send.at[0], small_recv.at[0], far_device)


    def load(i, slot):
        return pltpu.make_async_copy(
            part_of(i, 0, features), wide_w.at[slot] if i < 5 else large_w, load_sem.at[i]
        )

    def project(i, slot, keep):
        copy = load(i, slot)
        copy.start()
        copy.wait()

        def body(n, carry):
            at = pl.ds(pl.multiple_of(n * row_len, row_len), row_len)
            keep(at, jnp.dot(normed[at], wide_w[slot], preferred_element_type=F32))
            return carry

        lax.fori_loop(0, 2, body, 0)

    def keep_query(at, total):
        query_pre[at] = total.astype(BF16)
        query[at] = (total * sigmoid(total)).astype(BF16)

    def keep_key(at, total):
        key_pre[at] = total.astype(BF16)
        key[at] = (total * sigmoid(total)).astype(BF16)

    def keep_value(at, total):
        value[at] = total.astype(BF16)

    def keep_gate(at, total):
        gate[at] = total.astype(BF16)

    heads = small // HEAD_DIM
    first_head = (core * 2 + z % 2) * heads

    def attend(row, ends):
        at = pl.ds(row * row_len, row_len)

        def place(dim):
            index = lax.broadcasted_iota(jnp.int32, (row_len, row_len), dim) + core * quarter
            return jnp.where(index >= row_len, index - row_len, index).astype(F32)

        def body(head, carry):
            cols = pl.ds(pl.multiple_of(head * HEAD_DIM, HEAD_DIM), HEAD_DIM)
            scores = lax.dot_general(
                query[at, cols], key[at, cols], (((1,), (1,)), ((), ())), preferred_element_type=F32
            )
            to, source = place(0), place(1)
            allowed = (to >= source) & (to < ends[0:1, :])
            rate = (first_head + head).astype(F32) * (DECAY * HEAD_DIM / features)
            decay = jnp.where(allowed, jnp.exp(-rate * jnp.maximum(to - source, 0.0)), 0.0)
            weights = (scores * decay).astype(BF16)
            probs[row, head] = weights
            mixed[at, cols] = jnp.dot(weights, value[at, cols], preferred_element_type=F32).astype(BF16)
            return carry

        lax.fori_loop(0, heads, body, 0)
        for b in (2 * row, 2 * row + 1):
            m = mixed[rows(b)].astype(F32)
            total = jnp.sum(m * m, axis=1, keepdims=True)
            square[rows(b)] = jnp.broadcast_to(total, (quarter, HEAD_DIM))
            blended[rows(b)] = (gate[rows(b)].astype(F32) * m).astype(BF16)

    def output_part(row, slot):
        at = pl.ds(row * row_len, row_len)

        def body(n, carry):
            cols = pl.ds(pl.multiple_of(n * row_len, row_len), row_len)
            part[at, cols] = lax.dot_general(
                blended[at], wide_w[slot, cols], (((1,), (1,)), ((), ())), preferred_element_type=F32
            ).astype(BF16)
            return carry

        lax.fori_loop(0, features // row_len, body, 0)

    tile = 32

    def tiles(body):
        def step(n, carry):
            body(pl.multiple_of(n * tile, tile))
            return carry

        lax.fori_loop(0, quarter // tile, step, 0)


    normed_local.start()
    start_tokens(normed_copies)
    ends_copy.start()
    start_line(0)
    start_line(1)
    start_plane(0)
    start_line(2)
    start_plane(1)
    start_line(3)
    pass_tokens(normed_copies)
    forward_plane(0)
    start_plane(2)
    start_line(4)
    forward_plane(1)
    normed_local.wait()
    end_tokens(normed_copies)
    save(normed, normed_out)
    complete(0)
    project(0, 0, keep_query)
    save(query_pre, query_pre_out)
    save(query, query_out)
    start_plane(3)
    start_line(5)
    forward_plane(2)
    complete(1)
    project(1, 1, keep_key)
    save(key_pre, key_pre_out)
    save(key, key_out)
    start_plane(4)
    start_line(6)
    forward_plane(3)
    complete(2)
    project(2, 0, keep_value)
    save(value, value_out)
    forward_plane(4)
    complete(3)
    project(3, 1, keep_gate)
    save(gate, gate_out)
    ends_copy.wait()
    attend(1, ends_far)
    square_near = remote(
        square.at[rows(1)], square_core.at[rows(0)], small_send.at[1], small_recv.at[1], near_device
    )
    square_diag = remote(
        square.at[rows(3)], square_core.at[rows(1)], small_send.at[2], small_recv.at[2], near_device
    )
    square_pair = remote(square.at[rows(2)], square_far, small_send.at[3], small_recv.at[3], far_device)
    square_diag.start()
    start_plane(5)
    attend(0, ends_own)
    save(mixed, mixed_out)
    save(probs, probs_out)
    square_near.start()
    square_diag.wait_recv()
    square[rows(2)] += square_core[rows(1)]
    square_pair.start()
    complete(4)
    copy = load(4, 0)
    copy.start()
    copy.wait()
    output_part(1, 0)
    part_near = remote(part.at[rows(1)], part_core.at[rows(0)], small_send.at[4], small_recv.at[4], near_device)
    part_diag = remote(part.at[rows(3)], part_core.at[rows(1)], small_send.at[5], small_recv.at[5], near_device)
    part_pair = remote(part.at[rows(2)], part_far, small_send.at[6], small_recv.at[6], far_device)
    part_diag.start()
    part_diag.wait_recv()

    @tiles
    def _(start):
        here = pl.ds(start + 2 * quarter, tile)
        part[here] = (part[here].astype(F32) + part_core[pl.ds(start + quarter, tile)].astype(F32)).astype(BF16)

    part_pair.start()
    output_part(0, 0)
    part_near.start()
    forward_plane(5)
    start_plane(6)
    square_near.wait_recv()
    square_pair.wait_recv()
    part_near.wait_recv()
    part_pair.wait_recv()

    @tiles
    def _(start):
        here = pl.ds(start, tile)
        total = part[here].astype(F32) + part_core[here].astype(F32) + part_far[here].astype(F32)
        squares = square[here, 0:1] + square_core[here, 0:1] + square_far[here, 0:1]
        square_all[here] = jnp.broadcast_to(squares, (tile, HEAD_DIM))
        total = x_own[here].astype(F32) + total * lax.rsqrt(squares / features + EPS)
        middle[here] = total
        mid[here] = (total * lax.rsqrt(jnp.mean(total * total, axis=1, keepdims=True) + EPS)).astype(BF16)

    start_tokens(mid_copies)
    start_tokens(square_copies)
    save(middle, middle_out)
    save(ends_own, ends_out.at[pl.ds(0, 8)])
    save(ends_far, ends_out.at[pl.ds(8, 8)])
    complete(5)
    copy = load(5, 0)
    copy.start()
    copy.wait()
    mid_copies[0].wait_recv()

    def left_rows(row):
        at = pl.ds(row * row_len, row_len)
        left[at] = jnp.dot(mid[at], large_w[...], preferred_element_type=F32).astype(BF16)

    left_rows(0)
    pass_tokens(mid_copies)
    start_line(7)
    cot_local.start()
    start_tokens(cot_copies)
    forward_plane(6)
    pass_tokens(square_copies)
    mid_copies[2].wait_recv()
    left_rows(1)
    end_tokens(square_copies)
    save(square_all, square_out)
    save(mid, mid_out)
    save(left, left_out)
    complete(6)
    copy = load(6, 0)
    copy.start()
    copy.wait()

    def right_rows(n, carry):
        at = pl.ds(pl.multiple_of(n * row_len, row_len), row_len)
        total = jnp.dot(mid[at], large_w[...], preferred_element_type=F32)
        right[at] = total.astype(BF16)
        product[at] = (left[at].astype(F32) * total).astype(BF16)
        return carry

    start_plane(7)
    lax.fori_loop(0, 2, right_rows, 0)
    save(right, right_out)
    save(product, product_out)
    pass_tokens(cot_copies)
    forward_plane(7)
    complete(7)
    cot_local.wait()
    end_tokens(cot_copies)
    for copies in (normed_copies, cot_copies, mid_copies, square_copies):
        sent_tokens(copies)
    for copy in (square_near, square_diag, square_pair, part_near, part_diag, part_pair):
        copy.wait_send()
    for i in range(8):
        for k in (1, 2, 3):
            line_copy(i, k).wait_send()
        for copy in first(i) + second(i):
            copy.wait_send()
    for copy in saves:
        copy.wait()


def split_refs(refs, counts):
    parts, at = [], 0
    for count in counts:
        parts.append(refs[at : at + count])
        at += count
    return parts


def forward(wide, weights, normed, cot, x, ends):
    small, large = weights[0].shape[1] // 2, weights[5].shape[1] // 2
    quarter, features = x.shape
    tokens, row_len, heads = 4 * quarter, 2 * quarter, small // HEAD_DIM
    steps = wide.bit_length() - 1
    anywhere, vmem = pl.BlockSpec(memory_space=pl.ANY), pl.BlockSpec(memory_space=pltpu.VMEM)
    dma = pltpu.SemaphoreType.DMA
    outs = [
        ((features, 2 * small), BF16),
        ((features, 2 * small), BF16),
        ((features, small), BF16),
        ((features, large), BF16),
        ((features, large), BF16),
        ((features, large), BF16),
        ((tokens, features), BF16),
        ((tokens, features), BF16),
        ((tokens, small), BF16),
        ((tokens, small), BF16),
        ((tokens, small), BF16),
        ((tokens, small), BF16),
        ((tokens, small), BF16),
        ((tokens, small), BF16),
        ((tokens, small), BF16),
        ((2, heads, row_len, row_len), BF16),
        ((quarter, features), F32),
        ((tokens, features), BF16),
        ((tokens, large), BF16),
        ((tokens, large), BF16),
        ((tokens, large), BF16),
        ((tokens, HEAD_DIM), F32),
        ((16, row_len), F32),
    ]
    held = [
        ((tokens, features), BF16),
        ((2, features, small), BF16),
        ((tokens, small), BF16),
        ((tokens, small), BF16),
        ((tokens, small), BF16),
        ((tokens, small), BF16),
        ((tokens, small), BF16),
        ((tokens, small), BF16),
        ((tokens, small), BF16),
        ((2, heads, row_len, row_len), BF16),
        ((tokens, small), BF16),
        ((tokens, features), BF16),
        ((row_len, features), BF16),
        ((quarter, features), BF16),
        ((tokens, HEAD_DIM), F32),
        ((row_len, HEAD_DIM), F32),
        ((quarter, HEAD_DIM), F32),
        ((tokens, HEAD_DIM), F32),
        (ends.shape, F32),
        ((tokens, features), BF16),
        ((quarter, features), F32),
        ((features, large), BF16),
        ((tokens, large), BF16),
        ((tokens, large), BF16),
        ((tokens, large), BF16),
    ]
    sems = [(8, 3), (8, 3), (8,), (8, steps), (8, steps), (8,), (17,), (2,), (4, 3), (4, 3), (7,), (7,)]
    return pl.pallas_call(
        functools.partial(forward_kernel, wide, small, large),
        out_shape=[jax.ShapeDtypeStruct(s, t) for s, t in outs],
        in_specs=[anywhere] * 10 + [vmem] * 2,
        out_specs=[anywhere] * len(outs),
        scratch_shapes=[pltpu.VMEM(s, t) for s, t in held] + [dma(s) for s in sems],
        compiler_params=pltpu.CompilerParams(
            has_side_effects=True, collective_id=1, vmem_limit_bytes=60 << 20
        ),
        cost_estimate=pl.CostEstimate(flops=0, bytes_accessed=300 << 20, transcendentals=0),
    )(*weights, normed, cot, x, ends)


def backward_kernel(wide, small, large, *refs):
    (
        (cot_in, product_in, left_in, right_in, mid_in, middle_in, normed_in, gate_in, mixed_in, query_pre_in,
         key_pre_in, query_in, key_in, value_in, probs_in, square_in, ends_in, output_w, vg_w, qk_w, left_w, right_w,
         down_w),
        (output_out, gate_out, value_out, query_out, key_out, left_out, right_out, down_out, grad_middle_out,
         out_own, out_near, out_far, out_source, grad_own, grad_near, grad_far, branch_out, big_grad, big_near, big_far,
         big_line, big_more),
        (held_tokens, normed, weights, gate, mixed, query, key, value, grad_blended, grad_mixed, vg_grad, qk_grad,
         inner, inner_core, inner_sum, inner_far, inner_col, scale, ends, part_core, part_far, out_core, grad_core, own,
         middle, held, near, far, line, stage, added, filled, small_result, big_result),
        (load_sem, send, recv, line_send, line_recv, big_send, big_recv, big_line_send, big_line_recv, small_send,
         small_recv, stage_sem, result_sem, more_send, more_recv, chunk_sem, big_more_send, big_more_recv),
    ) = split_refs(refs, (23, 22, 34, 18))
    branch = held_tokens
    me, core, z, on_line, flip = place_of(wide)
    extra = list(range(4, wide.bit_length() - 1))
    plane_at = (me // 16) * 4 + me % 4
    others = [on_line(k)[0] for k in (1, 2, 3)] + [flip(b) for b in [0, 1] + extra]
    tokens, features = held_tokens.shape
    quarter, row_len = tokens // 4, tokens // 2
    rb = features // wide
    q = LINE * rb
    h = q // 2
    heads = small // HEAD_DIM
    near_device, far_device = (me, 1 - core), (flip(2), core)
    lower = z % 2 == 0
    widths = [min(small, large - at) for at in range(0, large, small)]
    products = [query, key, value]
    lefts = [gate, mixed, grad_blended]
    rights = [grad_mixed, vg_grad.at[:, pl.ds(0, small)], vg_grad.at[:, pl.ds(small, small)]]

    def remote(source, target, send_sem, recv_sem, device):
        return pltpu.make_async_remote_copy(
            src_ref=source, dst_ref=target, send_sem=send_sem, recv_sem=recv_sem,
            device_id=device, device_id_type=pl.DeviceIdType.MESH,
        )

    def block(m):
        return pl.multiple_of((plane_at ^ m) * q, q)

    def rows(b):
        return pl.ds(b * quarter, quarter)

    def loops(count, body):
        def step(n, carry):
            body(n)
            return carry

        lax.fori_loop(0, count, step, 0)

    pending = {}

    def load(name, source, target):
        copy = pltpu.make_async_copy(source, target, load_sem.at[len(pending)])
        copy.start()
        pending[name] = copy

    def load_cut(name, source, targets):
        for n, target in enumerate(targets):
            load(name + str(n), source.at[:, pl.ds(n * small, widths[n])], target.at[:, pl.ds(0, widths[n])])

    def ready(*names):
        for name in names:
            pending[name].wait()

    def ready_cut(name):
        ready(*(name + str(n) for n in range(len(widths))))

    results = []

    def give(source, target):
        copy = pltpu.make_async_copy(source, target, result_sem.at[len(results)])
        copy.start()
        results.append(copy)
        return len(results) - 1

    def given(n):
        if results[n] is not None:
            results[n].wait()
            results[n] = None

    load("cot", cot_in, held_tokens)
    load_cut("product", product_in, products)
    load_cut("down", down_w, [held.at[n] for n in range(3)])
    load_cut("right", right_in, rights)
    load_cut("left", left_in, lefts)
    load("mid", mid_in, normed)
    load("middle", middle_in, middle)
    load("own", cot_in.at[rows(0)], own)
    load("square", square_in, scale)
    load("ends", ends_in, ends)
    for r in range(2):
        for n in range(heads):
            load("probs%d%d" % (r, n), probs_in.at[r, n], held.at[3 + r, pl.ds(n * row_len, row_len)])
    meet([(other, core) for other in others] + [(me, 1 - core)])


    def rows_at(i, start, size):
        return held.at[i, pl.ds(pl.multiple_of(start, min(size, h)), size)]

    def step(i, j, start, size, target, bit):
        return remote(rows_at(i, start, size), target, send.at[i, j], recv.at[i, j], (flip(bit), core))

    def copies(i, j):
        if j == 0:
            return step(i, 0, block(3), h, near.at[i, 0], 1)
        if j == 1:
            return step(i, 1, block(3) + h, h, near.at[i, 1], 0)
        if j == 2:
            return step(i, 2, block(1) + h, h, far.at[i, 0, pl.ds(h, h)], 0)
        if j == 3:
            return step(i, 3, block(2), h, far.at[i, 1, pl.ds(0, h)], 1)
        if j == 4:
            return step(i, 4, block(1), h, far.at[i, 0, pl.ds(0, h)], 0)
        return step(i, 5, block(2) + h, h, far.at[i, 1, pl.ds(h, h)], 1)

    def line_copy(i, k):
        device, there = on_line(k)
        return remote(
            rows_at(i, block(0) + there * rb, rb), line.at[i, k - 1],
            line_send.at[i, k - 1], line_recv.at[i, k - 1], (device, core),
        )

    tile = min(64, h)

    def add(target, start, size, *sources):
        def body(n):
            at = pl.ds(pl.multiple_of(start + n * tile, tile), tile)
            total = target[at].astype(F32)
            for source in sources:
                total = total + source[pl.ds(pl.multiple_of(n * tile, tile), tile)].astype(F32)
            target[at] = total.astype(BF16)

        loops(size // tile, body)

    def begin(i, side, other):
        def fill(m):
            held[i, pl.ds(block(m), q)] = lax.dot_general(
                side[:, pl.ds(block(m), q)], other(), (((0,), (0,)), ((), ())), preferred_element_type=F32
            ).astype(BF16)

        if extra:
            loops(wide // LINE, fill)
            for e in reversed(range(len(extra))):
                size = q << (2 + e)
                half = plane_at >> (2 + e)
                copy = remote(
                    rows_at(i, (half ^ 1) * size, size), branch_more(i, e, size),
                    more_send.at[i, e], more_recv.at[i, e], (flip(extra[e]), core),
                )
                copy.start()
                copy.wait()
                add(held.at[i], half * size, size, branch_more(i, e, size))
            for j in range(4):
                copies(i, j).start()
        else:
            fill(3)
            copies(i, 0).start()
            copies(i, 1).start()
            fill(1)
            copies(i, 2).start()
            fill(2)
            copies(i, 3).start()
            fill(0)

    def branch_more(i, e, size):
        return far.at[i, e, pl.ds(0, size)]

    def fold(i):
        copies(i, 0).wait_recv()
        add(held.at[i], block(1), h, near.at[i, 0])
        copies(i, 4).start()
        copies(i, 1).wait_recv()
        add(held.at[i], block(2) + h, h, near.at[i, 1])
        copies(i, 5).start()

    def to_line(i):
        for j in range(2, 6):
            copies(i, j).wait_recv()
        add(held.at[i], block(0), q, far.at[i, 0], far.at[i, 1])
        for k in (1, 2, 3):
            line_copy(i, k).start()

    def finish(i, out):
        for k in (1, 2, 3):
            line_copy(i, k).wait_recv()
        own = held[i, pl.ds(block(0) + pl.multiple_of(z * rb, rb), rb)].astype(F32) + line[i, 1].astype(F32)
        other = line[i, 0].astype(F32) + line[i, 2].astype(F32)
        if small_done:
            given(small_done[-1])
        put(small_result, own, other, small)
        small_done.append(give(small_result, out))

    small_done = []

    def put(target, own, other, cols):
        @pl.when(lower)
        def _():
            target[:, pl.ds(0, cols)] = own
            target[:, pl.ds(cols, cols)] = other

        @pl.when(jnp.logical_not(lower))
        def _():
            target[:, pl.ds(0, cols)] = other
            target[:, pl.ds(cols, cols)] = own


    def big_rows(n, start, size):
        return big_grad.at[n, pl.ds(pl.multiple_of(start, min(size, rb)), size)]

    def big_copy(n, j):
        if j == 0:
            source, target = big_rows(n, block(3), h), big_near.at[n, 0]
        elif j == 1:
            source, target = big_rows(n, block(3) + h, h), big_near.at[n, 1]
        elif j == 2:
            source, target = big_rows(n, block(1) + h, h), big_far.at[n, 0, pl.ds(h, h)]
        elif j == 3:
            source, target = big_rows(n, block(2), h), big_far.at[n, 1, pl.ds(0, h)]
        elif j == 4:
            source, target = big_rows(n, block(1), h), big_far.at[n, 0, pl.ds(0, h)]
        else:
            source, target = big_rows(n, block(2) + h, h), big_far.at[n, 1, pl.ds(h, h)]
        bit = (1, 0, 0, 1, 0, 1)[j]
        return remote(source, target, big_send.at[n, j], big_recv.at[n, j], (flip(bit), core))

    def big_line_copy(n, k):
        device, there = on_line(k)
        return remote(
            big_rows(n, block(0) + there * rb, rb), big_line.at[n, k - 1],
            big_line_send.at[n, k - 1], big_line_recv.at[n, k - 1], (device, core),
        )

    def move(j, source, target):
        copy = pltpu.make_async_copy(source, target, stage_sem.at[j])
        copy.start()
        return copy

    def big_add(n, start, *sources):
        moves = [move(0, big_rows(n, start, h), stage.at[pl.ds(0, h)])]
        for j, source in enumerate(sources):
            moves.append(move(1 + j, source, added.at[pl.ds(j * h, h)]))
        for copy in moves:
            copy.wait()
        add(stage, 0, h, *(added.at[pl.ds(j * h, h)] for j in range(len(sources))))
        move(0, stage.at[pl.ds(0, h)], big_rows(n, start, h)).wait()

    def big_begin(n, side, parts):
        def fill(m):
            for c, width in enumerate(widths):
                filled[:, pl.ds(c * small, width)] = lax.dot_general(
                    side[:, pl.ds(block(m), q)], parts[c][:, pl.ds(0, width)], (((0,), (0,)), ((), ())),
                    preferred_element_type=F32,
                ).astype(BF16)
            move(3, filled, big_rows(n, block(m), q)).wait()

        if extra:
            loops(wide // LINE, fill)
            for e in reversed(range(len(extra))):
                size = q << (2 + e)
                half = plane_at >> (2 + e)
                copy = remote(
                    big_rows(n, (half ^ 1) * size, size), big_more.at[n, e, pl.ds(0, size)],
                    big_more_send.at[n, e], big_more_recv.at[n, e], (flip(extra[e]), core),
                )
                copy.start()
                copy.wait()
                loops(
                    size // h,
                    lambda i: big_add(
                        n, half * size + i * h, big_more.at[n, e, pl.ds(pl.multiple_of(i * h, h), h)]
                    ),
                )
            for j in range(4):
                big_copy(n, j).start()
        else:
            fill(3)
            big_copy(n, 0).start()
            big_copy(n, 1).start()
            fill(1)
            big_copy(n, 2).start()
            fill(2)
            big_copy(n, 3).start()
            fill(0)

    def big_fold(n):
        big_copy(n, 0).wait_recv()
        big_add(n, block(1), big_near.at[n, 0])
        big_copy(n, 4).start()
        big_copy(n, 1).wait_recv()
        big_add(n, block(2) + h, big_near.at[n, 1])
        big_copy(n, 5).start()

    def big_to_line(n):
        for j in range(2, 6):
            big_copy(n, j).wait_recv()
        for j in range(2):
            here = pl.ds(j * h, h)
            big_add(n, block(0) + j * h, big_far.at[n, 0, here], big_far.at[n, 1, here])
        for k in (1, 2, 3):
            big_line_copy(n, k).start()

    def big_finish(n, out):
        for k in (1, 2, 3):
            big_line_copy(n, k).wait_recv()
        moves = [move(k, big_line.at[n, k], added.at[pl.ds(k * rb, rb)]) for k in range(3)]
        moves.append(move(3, big_rows(n, block(0) + z * rb, rb), added.at[pl.ds(3 * rb, rb)]))
        for copy in moves:
            copy.wait()
        if results_of_big:
            given(results_of_big[-1])
        got = [added[pl.ds(k * rb, rb)].astype(F32) for k in range(4)]
        put(big_result, got[3] + got[1], got[0] + got[2], large)
        results_of_big.append(give(big_result, out))

    results_of_big = []


    def gate_product(r):
        at = pl.ds(r * row_len, row_len)
        for c, width in enumerate(widths):
            here = pl.ds(0, width)
            total = jnp.dot(held_tokens[at], held[c, :, here], preferred_element_type=F32)
            grad_left = (total * rights[c][at, here].astype(F32)).astype(BF16)
            lefts[c][at, here] = (total * lefts[c][at, here].astype(F32)).astype(BF16)
            rights[c][at, here] = grad_left

    chunk = row_len // 2
    chunks = features // chunk
    wide_cols = 2 * small

    def chunk_copies(n, slot):
        source = pl.ds(pl.multiple_of(n * chunk, chunk), chunk)
        target = pl.ds(pl.multiple_of(slot * chunk, chunk), chunk)
        return [
            pltpu.make_async_copy(
                w.at[source, pl.ds(at, cols)], weights.at[2 * i + j, target, pl.ds(0, cols)], chunk_sem.at[slot, 2 * i + j]
            )
            for i, w in enumerate((left_w, right_w))
            for j, (at, cols) in enumerate(((0, wide_cols), (wide_cols, large - wide_cols)))
        ]

    def mid_part(r):
        at = pl.ds(r * row_len, row_len)
        for copy in chunk_copies(0, 0):
            copy.start()

        def body(n):
            slot = n % 2

            @pl.when(n + 1 < chunks)
            def _():
                for copy in chunk_copies(n + 1, 1 - slot):
                    copy.start()

            for copy in chunk_copies(n, slot):
                copy.wait()
            here = pl.ds(pl.multiple_of(slot * chunk, chunk), chunk)
            total = jnp.zeros((row_len, chunk), F32)
            for i, parts in enumerate((rights, lefts)):
                for c, width in enumerate(widths):
                    w = weights[2 * i + c // 2, here, pl.ds((c % 2) * small, width)]
                    total = total + lax.dot_general(
                        parts[c][at, pl.ds(0, width)], w, (((1,), (1,)), ((), ())), preferred_element_type=F32
                    )
            held_tokens[at, pl.ds(pl.multiple_of(n * chunk, chunk), chunk)] = total.astype(BF16)

        loops(chunks, body)

    def output_part(r):
        at = pl.ds(r * row_len, row_len)

        def body(n):
            here = pl.ds(pl.multiple_of(n * row_len, row_len), row_len)
            total = jnp.zeros((row_len, row_len), F32)
            for c, width in enumerate(widths):
                total = total + lax.dot_general(
                    products[c][at, pl.ds(0, width)], held[c, here, pl.ds(0, width)], (((1,), (1,)), ((), ())),
                    preferred_element_type=F32,
                )
            held_tokens[at, here] = total.astype(BF16)

        loops(features // row_len, body)

    def middle_rows(n):
        at = pl.ds(pl.multiple_of(n * 32, 32), 32)
        grad = held_tokens[at].astype(F32) + part_core[at].astype(F32) + part_far[at].astype(F32)
        values = middle[at]
        s = lax.rsqrt(jnp.mean(values * values, axis=1, keepdims=True) + EPS)
        grad = own[at].astype(F32) + norm_back(values, s, grad)
        middle[at] = grad
        own[at] = grad.astype(BF16)


    def grad_rows(row):
        at = pl.ds(row * row_len, row_len)
        total = jnp.zeros((row_len, small), F32)
        for n in range(4):
            total = total + jnp.dot(
                branch[at, pl.ds(n * row_len, row_len)], weights[n, :, pl.ds(0, small)], preferred_element_type=F32
            )
        grad_blended[at] = total.astype(BF16)
        m = mixed[at].astype(F32)
        g = gate[at].astype(F32)
        scaled = m * scale[at, 0:1]
        vg_grad[at, pl.ds(small, small)] = (total * scaled).astype(BF16)
        grad_mixed[at] = (g * scaled).astype(BF16)
        inner[:, at] = lax.dot_general(
            jnp.ones((8, small), F32), total * g * m, (((1,), (1,)), ((), ())),
            preferred_element_type=F32, precision=lax.Precision.HIGHEST,
        )

    def scale_rows(n):
        at = pl.ds(pl.multiple_of(n * 128, 128), 128)
        scale[at] = lax.rsqrt(scale[at] / features + EPS)

    def mix_rows(n):
        at = pl.ds(pl.multiple_of(n * 128, 128), 128)
        s = scale[at, 0:1]
        value_of = s * (grad_blended[at].astype(F32) * gate[at].astype(F32))
        value_of = value_of - mixed[at].astype(F32) * (s * s * s * (inner_col[at, 0:1] / features))
        grad_mixed[at] = value_of.astype(BF16)

    first_head = (core * 2 + z % 2) * heads

    def attend_back(row):
        at = pl.ds(row * row_len, row_len)

        def place(dim):
            index = lax.broadcasted_iota(jnp.int32, (row_len, row_len), dim) + core * quarter
            return jnp.where(index >= row_len, index - row_len, index).astype(F32)

        def slope(pre):
            s = sigmoid(pre)
            return s * (1.0 + pre * (1.0 - s))

        def body(head):
            cols = pl.ds(pl.multiple_of(head * HEAD_DIM, HEAD_DIM), HEAD_DIM)
            more = pl.ds(pl.multiple_of(small + head * HEAD_DIM, HEAD_DIM), HEAD_DIM)
            got = grad_mixed[at, cols]
            grad_probs = lax.dot_general(
                got, value[at, cols], (((1,), (1,)), ((), ())), preferred_element_type=F32
            )
            to, source = place(0), place(1)
            allowed = (to >= source) & (to < ends[pl.ds(8 * row, 1), :])
            rate = (first_head + head).astype(F32) * (DECAY * HEAD_DIM / features)
            decay = jnp.where(allowed, jnp.exp(-rate * jnp.maximum(to - source, 0.0)), 0.0)
            grad_scores = (grad_probs * decay).astype(BF16)
            probs = held[3 + row, pl.ds(pl.multiple_of(head * row_len, row_len), row_len)]
            vg_grad[at, cols] = lax.dot_general(
                probs, got, (((0,), (0,)), ((), ())), preferred_element_type=F32
            ).astype(BF16)
            grad_query = jnp.dot(grad_scores, key[at, cols], preferred_element_type=F32)
            qk_grad[at, cols] = (grad_query * slope(gate[at, cols].astype(F32))).astype(BF16)
            grad_key = lax.dot_general(
                grad_scores, query[at, cols], (((0,), (0,)), ((), ())), preferred_element_type=F32
            )
            qk_grad[at, more] = (grad_key * slope(mixed[at, cols].astype(F32))).astype(BF16)

        loops(heads, body)

    def load_weights(pair):
        for n in range(2):
            here = pl.ds((2 * pair + n) * row_len, row_len)
            load("vg%d%d" % (pair, n), vg_w.at[here], weights.at[n])
            load("qk%d%d" % (pair, n), qk_w.at[here], weights.at[2 + n])

    def normed_part(pair, row):
        at = pl.ds(row * row_len, row_len)
        for n in range(2):
            total = lax.dot_general(vg_grad[at], weights[n], (((1,), (1,)), ((), ())), preferred_element_type=F32)
            total = total + lax.dot_general(
                qk_grad[at], weights[2 + n], (((1,), (1,)), ((), ())), preferred_element_type=F32
            )
            branch[at, pl.ds((2 * pair + n) * row_len, row_len)] = total.astype(BF16)

    def small_copy(n, source, target, device):
        return remote(source, target, small_send.at[n], small_recv.at[n], device)


    ready("cot")
    ready_cut("product")
    big_begin(0, held_tokens, products)
    ready_cut("down")
    ready_cut("left")
    ready_cut("right")
    gate_product(1)
    gate_product(0)
    mid_part(1)
    part_diag = small_copy(0, held_tokens.at[rows(3)], part_core.at[rows(1)], near_device)
    part_near = small_copy(1, held_tokens.at[rows(1)], part_core.at[rows(0)], near_device)
    part_pair = small_copy(2, held_tokens.at[rows(2)], part_far, far_device)
    part_diag.start()
    part_diag.wait_recv()
    add(held_tokens, 2 * quarter, quarter, part_core.at[rows(1)])
    part_pair.start()
    big_fold(0)
    mid_part(0)
    part_near.start()
    ready("mid")
    big_begin(1, normed, rights)
    ready("middle", "own")
    part_near.wait_recv()
    part_pair.wait_recv()
    loops(quarter // 32, middle_rows)
    branch_own = move(4, own, branch_out.at[rows(0)])
    branch_near = small_copy(3, own, branch_out.at[rows(1)], near_device)
    branch_far = small_copy(4, own, branch_out.at[rows(2)], far_device)
    branch_pass = small_copy(5, branch_out.at[rows(2)], branch_out.at[rows(3)], near_device)
    branch_far.start()
    branch_near.start()
    give(middle, grad_middle_out)
    for n in range(4):
        load("output%d" % n, output_w.at[pl.ds(n * row_len, row_len)], weights.at[n, :, pl.ds(0, small)])
    big_to_line(0)
    big_begin(2, normed, lefts)
    load("gate", gate_in, gate)
    load("mixed", mixed_in, mixed)
    load("normed", normed_in, normed)
    big_fold(1)
    for copy in (part_diag, part_near, part_pair):
        copy.wait_send()
    output_part(1)
    out_diag = small_copy(6, held_tokens.at[rows(3)], out_core, near_device)
    out_diag.start()
    output_part(0)
    out_next = small_copy(7, held_tokens.at[rows(1)], out_near, near_device)
    out_next.start()
    out_mine = move(5, held_tokens.at[rows(0)], out_own)
    out_diag.wait_recv()
    add(held_tokens, 2 * quarter, quarter, out_core)
    out_pair = small_copy(8, out_source, out_far, far_device)
    move(0, held_tokens.at[rows(2)], out_source).wait()
    out_pair.start()
    load("value", value_in, value)
    load("query", query_in, query)
    load("key", key_in, key)
    out_mine.wait()
    out_next.wait_send()
    out_diag.wait_send()
    branch_own.wait()
    branch_near.wait_recv()
    load("branch0", branch_out.at[pl.ds(0, row_len)], branch.at[pl.ds(0, row_len)])
    ready("square")
    loops(tokens // 128, scale_rows)
    branch_far.wait_recv()
    branch_pass.start()
    ready("branch0", "output0", "output1", "output2", "output3", "gate", "mixed")
    grad_rows(0)
    branch_pass.wait_recv()
    load("branch1", branch_out.at[pl.ds(row_len, row_len)], branch.at[pl.ds(row_len, row_len)])
    ready("branch1")
    grad_rows(1)
    core_copy = small_copy(9, inner, inner_core, near_device)
    core_copy.start()
    core_copy.wait_recv()
    for b in range(4):
        inner_sum[:, rows(b)] = inner[:, rows(b)] + inner_core[:, rows(b ^ 1)]
    far_copy = small_copy(10, inner_sum, inner_far, far_device)
    far_copy.start()
    begin(0, branch, lambda: grad_mixed[...])
    far_copy.wait_recv()
    for b in range(4):
        total = inner_sum[:, rows(b)] + inner_far[:, rows(b ^ 2)]
        inner_col[rows(b)] = jnp.broadcast_to(total.T[:, 0:1], (quarter, HEAD_DIM))
    loops(tokens // 128, mix_rows)
    load("query_pre", query_pre_in, gate)
    load("key_pre", key_pre_in, mixed)
    load_weights(0)
    ready("normed")
    begin(1, normed, lambda: vg_grad[:, pl.ds(small, small)])
    big_to_line(1)
    big_fold(2)
    ready("value", "query", "key", "query_pre", "key_pre", "ends")
    for r in range(2):
        ready(*("probs%d%d" % (r, n) for n in range(heads)))
    attend_back(1)
    fold(0)
    attend_back(0)
    begin(2, normed, lambda: vg_grad[:, pl.ds(0, small)])
    fold(1)
    begin(3, normed, lambda: qk_grad[:, pl.ds(0, small)])
    begin(4, normed, lambda: qk_grad[:, pl.ds(small, small)])
    big_to_line(2)
    to_line(0)
    fold(2)
    ready("vg00", "vg01", "qk00", "qk01")
    normed_part(0, 1)
    normed_part(0, 0)
    load_weights(1)
    big_finish(0, down_out)
    to_line(1)
    ready("vg10", "vg11", "qk10", "qk11")
    normed_part(1, 1)
    grad_diag = small_copy(11, branch.at[rows(3)], grad_core, near_device)
    grad_next = small_copy(12, branch.at[rows(1)], grad_near, near_device)
    grad_pair = small_copy(13, branch.at[rows(2)], grad_far, far_device)
    grad_diag.start()
    normed_part(1, 0)
    grad_next.start()
    give(branch.at[rows(0)], grad_own)
    grad_diag.wait_recv()
    add(branch, 2 * quarter, quarter, grad_core)
    grad_pair.start()
    fold(3)
    fold(4)
    big_finish(1, left_out)
    to_line(2)
    finish(0, output_out)
    finish(1, gate_out)
    to_line(3)
    big_finish(2, right_out)
    finish(2, value_out)
    to_line(4)
    for copy in (out_next, out_pair, grad_next, grad_pair):
        copy.wait_recv()
    finish(3, query_out)
    finish(4, key_out)
    for copy in (branch_near, branch_far, branch_pass, out_pair, core_copy, far_copy, grad_diag, grad_next, grad_pair):
        copy.wait_send()
    for i in range(5):
        for j in range(6):
            copies(i, j).wait_send()
        for k in (1, 2, 3):
            line_copy(i, k).wait_send()
    for n in range(3):
        for j in range(6):
            big_copy(n, j).wait_send()
        for k in (1, 2, 3):
            big_line_copy(n, k).wait_send()
    for n in range(len(results)):
        given(n)


def backward(wide, arrays, small, large):
    tokens, features = arrays[0].shape
    quarter, row_len = tokens // 4, tokens // 2
    rb = features // wide
    q = LINE * rb
    extra = max(1, wide.bit_length() - 5)
    anywhere = pl.BlockSpec(memory_space=pl.ANY)
    dma = pltpu.SemaphoreType.DMA
    many = features // 2 if wide > 16 else 16
    far_rows = max(q, many)
    part = (quarter, features)
    outs = [((rb, 2 * small), F32)] * 5 + [((rb, 2 * large), F32)] * 3 + [(part, F32)] + [(part, BF16)] * 7 + [
        ((tokens, features), BF16),
        ((3, features, large), BF16),
        ((3, 2, q // 2, large), BF16),
        ((3, 2, q, large), BF16),
        ((3, 3, rb, large), BF16),
        ((3, extra, many, large), BF16),
    ]
    held = [
        ((tokens, features), BF16),
        ((tokens, features), BF16),
        ((4, row_len, 2 * small), BF16),
        *[((tokens, small), BF16)] * 7,
        ((tokens, 2 * small), BF16),
        ((tokens, 2 * small), BF16),
        *[((8, tokens), F32)] * 4,
        ((tokens, HEAD_DIM), F32),
        ((tokens, HEAD_DIM), F32),
        ((16, row_len), F32),
        ((row_len, features), BF16),
        *[(part, BF16)] * 4,
        (part, F32),
        ((5, features, small), BF16),
        ((5, 2, q // 2, small), BF16),
        ((5, 2, far_rows, small), BF16),
        ((5, 3, rb, small), BF16),
        ((q // 2, large), BF16),
        ((q, large), BF16),
        ((q, large), BF16),
        ((rb, 2 * small), F32),
        ((rb, 2 * large), F32),
    ]
    sems = [
        (52,), (5, 6), (5, 6), (5, 3), (5, 3), (3, 6), (3, 6), (3, 3), (3, 3), (14,), (14,), (6,), (10,), (5, extra),
        (5, extra), (2, 4), (3, extra), (3, extra),
    ]
    return pl.pallas_call(
        functools.partial(backward_kernel, wide, small, large),
        out_shape=[jax.ShapeDtypeStruct(s, t) for s, t in outs],
        in_specs=[anywhere] * len(arrays),
        out_specs=[anywhere] * len(outs),
        scratch_shapes=[pltpu.VMEM(s, t) for s, t in held] + [dma(s) for s in sems],
        compiler_params=pltpu.CompilerParams(
            has_side_effects=True, collective_id=2, vmem_limit_bytes=60 << 20
        ),
        cost_estimate=pl.CostEstimate(flops=0, bytes_accessed=300 << 20, transcendentals=0),
    )(*arrays)


def ends_of(lengths, places):
    total, ends = 0, 0
    for c in range(lengths.shape[1]):
        ends = ends + jnp.where(places >= total, lengths[0, c], 0)
        total = total + lengths[0, c]
    return jnp.broadcast_to(ends.astype(F32)[None], (8, places.shape[0]))


def sigmoid(z):
    return 1.0 / (1.0 + jnp.exp(-z))


def on_device(
    layer_input, doc_lengths, w_query, w_key, w_value, w_gate, w_output, w_left, w_right, w_down, cotangent, *, wide
):
    net = Net(wide)
    core = lax.axis_index("narrow")
    half = (net.me >> 2) & 1
    features = layer_input.shape[1]

    x = net.permute(layer_input)
    inputs = x.astype(F32)
    norm_one = norm_scale_of(inputs)
    cot = net.permute(cotangent)
    quarter = inputs.shape[0]
    tokens = 4 * quarter
    row_len = 2 * quarter
    own = jnp.arange(quarter, dtype=jnp.int32)
    places = jnp.concatenate([own + core * quarter, own + (1 - core) * quarter])
    (
        qk_w, vg_w, output_w, left_w, right_w, down_w, normed, cot_all, query_pre, key_pre, gate, queries, keys, values,
        mixed, probs, middle, mid, left, right, product, squares, ends,
    ) = forward(
        wide,
        [w_query, w_key, w_value, w_gate, w_output, w_left, w_right, w_down],
        (inputs * norm_one).astype(BF16),
        cot,
        x,
        ends_of(doc_lengths, places),
    )

    (
        grad_output, grad_gate, grad_value, grad_query, grad_key, grad_left, grad_right, grad_down, grad_middle,
        out_own, out_near, out_far, _, grad_own, grad_near, grad_far, *_
    ) = backward(
        wide,
        [
            cot_all, product, left, right, mid, middle, normed, gate, mixed, query_pre, key_pre, queries, keys, values,
            probs, squares, ends, output_w, vg_w, qk_w, left_w, right_w, down_w,
        ],
        queries.shape[1],
        left.shape[1],
    )
    layer_output = middle + out_own.astype(F32) + out_near.astype(F32) + out_far.astype(F32)
    layer_output = net.restore(layer_output.astype(BF16))
    grad_normed = grad_own.astype(F32) + grad_near.astype(F32) + grad_far.astype(F32)
    input_grad = net.restore(grad_middle + norm_back(inputs, norm_one, grad_normed))
    return (
        layer_output,
        input_grad,
        grad_query,
        grad_key,
        grad_value,
        grad_gate,
        grad_output,
        grad_left,
        grad_right,
        grad_down,
    )


def solution(mesh):
    both, weight = P(("wide", "narrow"), None), P("wide", "narrow")
    wide = mesh.shape["wide"]

    def body(*args):
        return on_device(*args, wide=wide)

    return jax.shard_map(
        body,
        mesh=mesh,
        in_specs=(both, P("wide", None)) + (weight,) * 8 + (both,),
        out_specs=(both, both) + (weight,) * 8,
        check_vma=False,
    )
```

```python
import functools

import jax
import jax.numpy as jnp
from jax import lax
from jax.experimental import pallas as pl
from jax.experimental.pallas import tpu as pltpu
from jax.sharding import PartitionSpec as P

HEAD_DIM = 128
LINE = 4
EPS = 1e-06
DECAY = 2.0
F32 = jnp.float32
BF16 = jnp.bfloat16


def norm_back(values, scale, gradient):
    inner = jnp.mean(gradient * values, axis=-1, keepdims=True)
    return scale * gradient - values * (scale * scale * scale) * inner


def to_kept(value, wide):
    tokens, cols = value.shape
    value = value.reshape(tokens, wide // 16, LINE, 4, cols // wide)
    return value.transpose(0, 1, 3, 2, 4).reshape(tokens, cols)


def from_kept(value, wide):
    tokens, cols = value.shape
    value = value.reshape(tokens, wide // 16, 4, LINE, cols // wide)
    return value.transpose(0, 1, 3, 2, 4).reshape(tokens, cols)


def place_of(wide):
    me = lax.axis_index("wide")
    z = (me // 4) % LINE

    def on_line(k):
        there = (z + k) % LINE
        return me + (there - z) * 4, there

    def flip(bit):
        return me + (1 - 2 * ((me >> bit) & 1)) * (1 << bit)

    return me, lax.axis_index("narrow"), z, on_line, flip


def meet(devices):
    barrier = pltpu.get_barrier_semaphore()
    for device in devices:
        pl.semaphore_signal(
            barrier, inc=1, device_id=device, device_id_type=pl.DeviceIdType.MESH
        )
    pl.semaphore_wait(barrier, len(devices))


def forward_kernel(wide, small, large, *refs):
    (
        w_in, (cot_in, x_in, lengths),
        w_out, (normed_out, cot_out, query_pre_out, key_pre_out, gate_out, query_out, key_out, value_out, mixed_out,
                probs_out, middle_out, mid_out, left_out, right_out, product_out, square_out, ends_out, big_grad),
        (normed, wide_w, query_pre, key_pre, gate, query, key, value, mixed, probs, blended, part, part_core, part_far,
         square, square_core, square_far, square_all, ends_far, mid, middle, large_w, left, right, product, x_own, ends_own,
         filled),
        (line_send, line_recv, own_sem, plane_send, plane_recv, load_sem, save_sem, token_sem, token_send, token_recv,
         small_send, small_recv, piece_sem),
    ) = split_refs(refs, (8, 3, 6, 18, 28, 13))
    me, core, z, on_line, flip = place_of(wide)
    extra = list(range(4, wide.bit_length() - 1))
    plane_at = (me // 16) * 4 + me % 4
    others = [on_line(k)[0] for k in (1, 2, 3)] + [flip(b) for b in [0, 1] + extra]
    quarter, features = x_own.shape
    pieces = pieces_of(wide, features)
    x_loads = [
        pltpu.make_async_copy(x_in.at[:, pl.ds(a, size)], x_own.at[:, pl.ds(b, size)], piece_sem.at[0, n])
        for n, (a, b, size) in enumerate(pieces)
    ]
    cot_loads = [
        pltpu.make_async_copy(
            cot_in.at[:, pl.ds(a, size)], cot_out.at[pl.ds(0, quarter), pl.ds(b, size)], piece_sem.at[1, n]
        )
        for n, (a, b, size) in enumerate(pieces)
    ]
    for copy in x_loads + cot_loads:
        copy.start()
    meet([(other, core) for other in others] + [(me, 1 - core)])
    rb = w_in[0].shape[0]
    q = LINE * rb
    h = q // 2
    row_len = 2 * quarter
    chunks = [(0, 0), (0, small), (1, 0), (1, small), (2, 0), (3, 0), (4, 0), (5, 0)]
    near_device, far_device = (me, 1 - core), (flip(2), core)


    def part_of(i, start, size):
        out, col = chunks[i]
        cols = w_in[i].shape[1] // 2
        return w_out[out].at[pl.ds(pl.multiple_of(start, min(size, rb)), size), pl.ds(col, cols)]

    def block(m):
        return (plane_at ^ m) * q

    def remote(source, target, send_sem, recv_sem, device):
        return pltpu.make_async_remote_copy(
            src_ref=source, dst_ref=target, send_sem=send_sem, recv_sem=recv_sem,
            device_id=device, device_id_type=pl.DeviceIdType.MESH,
        )

    def mine(i, there):
        cols = w_in[i].shape[1] // 2
        return w_in[i].at[:, pl.ds(pl.multiple_of((there % 2) * cols, HEAD_DIM), cols)]

    def line_copy(i, k):
        device, there = on_line(k)
        return remote(
            mine(i, there), part_of(i, block(0) + z * rb, rb),
            line_send.at[i, k - 1], line_recv.at[i, k - 1], (device, core),
        )

    def own_copy(i):
        return pltpu.make_async_copy(mine(i, z), part_of(i, block(0) + z * rb, rb), own_sem.at[i])

    def plane(i, j, start, size, bit):
        place = part_of(i, start, size)
        return remote(place, place, plane_send.at[i, j], plane_recv.at[i, j], (flip(bit), core))

    def first(i, k):
        target = part_of(i, block(0) + ((z - k) % LINE) * rb, rb)
        source = target if k else mine(i, z)
        return [
            remote(source, target, plane_send.at[i, 4 * b + k], plane_recv.at[i, 4 * b + k], (flip(b), core))
            for b in (0, 1)
        ]

    def second(i):
        return plane(i, 8, block(1), h, 1), plane(i, 9, block(2) + h, h, 0)

    def start_line(i):
        own_copy(i).start()
        for k in (1, 2, 3):
            line_copy(i, k).start()

    def start_own(i):
        for copy in first(i, 0):
            copy.start()

    def start_plane(i):
        own_copy(i).wait()
        for k in (1, 3, 2):
            line_copy(i, k).wait_recv()
            for copy in first(i, k):
                copy.start()

    def forward_plane(i):
        for b, onward in enumerate(second(i)):
            for k in range(LINE):
                first(i, k)[b].wait_recv()
            onward.start()

    def complete(i):
        for copy in second(i):
            copy.wait_recv()
        for e, bit in enumerate(extra):
            size = q << (2 + e)
            copy = plane(i, 10 + e, (plane_at >> (2 + e)) * size, size, bit)
            copy.start()
            copy.wait()


    def rows(b):
        return pl.ds(b * quarter, quarter)

    def token_copies(n, source, out):
        send = lambda j, source, device: remote(
            source, out.at[rows(j + 1)], token_send.at[n, j], token_recv.at[n, j], device
        )
        return send(0, source, near_device), send(1, source, far_device), send(2, out.at[rows(2)], near_device)

    def start_tokens(copies):
        copies[0].start()
        copies[1].start()

    def pass_tokens(copies):
        copies[1].wait_recv()
        copies[2].start()

    def end_tokens(copies):
        copies[0].wait_recv()
        copies[2].wait_recv()

    def sent_tokens(copies):
        for copy in copies:
            copy.wait_send()

    saves = []

    def save(source, target):
        copy = pltpu.make_async_copy(source, target, save_sem.at[len(saves)])
        copy.start()
        saves.append(copy)

    normed_copies = token_copies(0, normed.at[rows(0)], normed)
    cot_copies = token_copies(1, cot_out.at[rows(0)], cot_out)
    mid_copies = token_copies(2, mid.at[rows(0)], mid)
    square_copies = token_copies(3, square_all.at[rows(0)], square_all)
    ends_copy = remote(ends_own, ends_far, small_send.at[0], small_recv.at[0], far_device)


    def load(i, slot):
        return pltpu.make_async_copy(
            part_of(i, 0, features), wide_w.at[slot] if i < 5 else large_w, load_sem.at[i]
        )

    def project(i, slot, keep):
        copy = load(i, slot)
        copy.start()
        copy.wait()

        def body(n, carry):
            at = pl.ds(pl.multiple_of(n * row_len, row_len), row_len)
            keep(at, jnp.dot(normed[at], wide_w[slot], preferred_element_type=F32))
            return carry

        lax.fori_loop(0, 2, body, 0)

    def keep_query(at, total):
        query_pre[at] = total.astype(BF16)
        query[at] = (total * sigmoid(total)).astype(BF16)

    def keep_key(at, total):
        key_pre[at] = total.astype(BF16)
        key[at] = (total * sigmoid(total)).astype(BF16)

    def keep_value(at, total):
        value[at] = total.astype(BF16)

    def keep_gate(at, total):
        gate[at] = total.astype(BF16)

    heads = small // HEAD_DIM
    first_head = (core * 2 + z % 2) * heads

    def attend(row, ends):
        at = pl.ds(row * row_len, row_len)

        def place(dim):
            index = lax.broadcasted_iota(jnp.int32, (row_len, row_len), dim) + core * quarter
            return jnp.where(index >= row_len, index - row_len, index).astype(F32)

        def body(head, carry):
            cols = pl.ds(pl.multiple_of(head * HEAD_DIM, HEAD_DIM), HEAD_DIM)
            scores = lax.dot_general(
                query[at, cols], key[at, cols], (((1,), (1,)), ((), ())), preferred_element_type=F32
            )
            to, source = place(0), place(1)
            allowed = (to >= source) & (to < ends[0:1, :])
            rate = (first_head + head).astype(F32) * (DECAY * HEAD_DIM / features)
            decay = jnp.where(allowed, jnp.exp(-rate * jnp.maximum(to - source, 0.0)), 0.0)
            weights = (scores * decay).astype(BF16)
            probs[row, head] = weights
            mixed[at, cols] = jnp.dot(weights, value[at, cols], preferred_element_type=F32).astype(BF16)
            return carry

        lax.fori_loop(0, heads, body, 0)
        for b in (2 * row, 2 * row + 1):
            m = mixed[rows(b)].astype(F32)
            total = jnp.sum(m * m, axis=1, keepdims=True)
            square[rows(b)] = jnp.broadcast_to(total, (quarter, HEAD_DIM))
            blended[rows(b)] = (gate[rows(b)].astype(F32) * m).astype(BF16)

    def output_part(row, slot):
        at = pl.ds(row * row_len, row_len)

        def body(n, carry):
            cols = pl.ds(pl.multiple_of(n * row_len, row_len), row_len)
            part[at, cols] = lax.dot_general(
                blended[at], wide_w[slot, cols], (((1,), (1,)), ((), ())), preferred_element_type=F32
            ).astype(BF16)
            return carry

        lax.fori_loop(0, features // row_len, body, 0)

    tile = 32

    def tiles(body):
        def step(n, carry):
            body(pl.multiple_of(n * tile, tile))
            return carry

        lax.fori_loop(0, quarter // tile, step, 0)


    start_line(0)
    for i in range(6):
        start_own(i)
    for copy in x_loads:
        copy.wait()

    @tiles
    def _(start):
        here = pl.ds(start, tile)
        values = x_own[here].astype(F32)
        normed[here] = (values * lax.rsqrt(jnp.mean(values * values, axis=1, keepdims=True) + EPS)).astype(BF16)

    start_tokens(normed_copies)
    start_line(1)
    total, ends = 0, jnp.zeros(ends_own.shape, jnp.int32)
    places = lax.broadcasted_iota(jnp.int32, ends_own.shape, 1) + core * quarter
    places = jnp.where(places >= row_len, places - row_len, places)
    for c in range(lengths.shape[1]):
        ends = ends + jnp.where(places >= total, lengths[0, c], 0)
        total = total + lengths[0, c]
    ends_own[...] = ends.astype(F32)
    ends_copy.start()
    start_plane(0)
    start_line(2)
    start_plane(1)
    start_line(3)
    pass_tokens(normed_copies)
    forward_plane(0)
    start_plane(2)
    start_line(4)
    forward_plane(1)
    end_tokens(normed_copies)
    save(normed, normed_out)
    complete(0)
    project(0, 0, keep_query)
    save(query_pre, query_pre_out)
    save(query, query_out)
    start_plane(3)
    start_line(5)
    forward_plane(2)
    complete(1)
    project(1, 1, keep_key)
    save(key_pre, key_pre_out)
    save(key, key_out)
    start_plane(4)
    start_line(6)
    forward_plane(3)
    complete(2)
    project(2, 0, keep_value)
    save(value, value_out)
    forward_plane(4)
    complete(3)
    project(3, 1, keep_gate)
    save(gate, gate_out)
    ends_copy.wait()
    attend(1, ends_far)
    square_near = remote(
        square.at[rows(1)], square_core.at[rows(0)], small_send.at[1], small_recv.at[1], near_device
    )
    square_diag = remote(
        square.at[rows(3)], square_core.at[rows(1)], small_send.at[2], small_recv.at[2], near_device
    )
    square_pair = remote(square.at[rows(2)], square_far, small_send.at[3], small_recv.at[3], far_device)
    square_diag.start()
    start_plane(5)
    attend(0, ends_own)
    save(mixed, mixed_out)
    save(probs, probs_out)
    square_near.start()
    square_diag.wait_recv()
    square[rows(2)] += square_core[rows(1)]
    square_pair.start()
    complete(4)
    copy = load(4, 0)
    copy.start()
    copy.wait()
    output_part(1, 0)
    part_near = remote(part.at[rows(1)], part_core.at[rows(0)], small_send.at[4], small_recv.at[4], near_device)
    part_diag = remote(part.at[rows(3)], part_core.at[rows(1)], small_send.at[5], small_recv.at[5], near_device)
    part_pair = remote(part.at[rows(2)], part_far, small_send.at[6], small_recv.at[6], far_device)
    part_diag.start()
    part_diag.wait_recv()

    @tiles
    def _(start):
        here = pl.ds(start + 2 * quarter, tile)
        part[here] = (part[here].astype(F32) + part_core[pl.ds(start + quarter, tile)].astype(F32)).astype(BF16)

    part_pair.start()
    output_part(0, 0)
    part_near.start()
    forward_plane(5)
    start_plane(6)
    square_near.wait_recv()
    square_pair.wait_recv()
    part_near.wait_recv()
    part_pair.wait_recv()

    @tiles
    def _(start):
        here = pl.ds(start, tile)
        total = part[here].astype(F32) + part_core[here].astype(F32) + part_far[here].astype(F32)
        squares = square[here, 0:1] + square_core[here, 0:1] + square_far[here, 0:1]
        square_all[here] = jnp.broadcast_to(squares, (tile, HEAD_DIM))
        total = x_own[here].astype(F32) + total * lax.rsqrt(squares / features + EPS)
        middle[here] = total
        mid[here] = (total * lax.rsqrt(jnp.mean(total * total, axis=1, keepdims=True) + EPS)).astype(BF16)

    start_tokens(mid_copies)
    start_tokens(square_copies)
    save(middle, middle_out)
    save(ends_own, ends_out.at[pl.ds(0, 8)])
    save(ends_far, ends_out.at[pl.ds(8, 8)])
    complete(5)
    copy = load(5, 0)
    copy.start()
    copy.wait()
    mid_copies[0].wait_recv()

    def left_rows(row):
        at = pl.ds(row * row_len, row_len)
        left[at] = jnp.dot(mid[at], large_w[...], preferred_element_type=F32).astype(BF16)

    left_rows(0)
    pass_tokens(mid_copies)
    start_line(7)
    start_own(6)
    start_own(7)
    for copy in cot_loads:
        copy.wait()
    start_tokens(cot_copies)
    forward_plane(6)
    pass_tokens(square_copies)
    mid_copies[2].wait_recv()
    left_rows(1)
    end_tokens(square_copies)
    save(square_all, square_out)
    save(mid, mid_out)
    save(left, left_out)
    complete(6)
    copy = load(6, 0)
    copy.start()
    copy.wait()

    def right_rows(n, carry):
        at = pl.ds(pl.multiple_of(n * row_len, row_len), row_len)
        total = jnp.dot(mid[at], large_w[...], preferred_element_type=F32)
        right[at] = total.astype(BF16)
        product[at] = (left[at].astype(F32) * total).astype(BF16)
        return carry

    start_plane(7)
    lax.fori_loop(0, 2, right_rows, 0)
    save(right, right_out)
    save(product, product_out)
    pass_tokens(cot_copies)
    forward_plane(7)
    end_tokens(cot_copies)
    saves[0].wait()
    sent_tokens(normed_copies)
    copy = pltpu.make_async_copy(cot_out, normed, token_sem.at[0])
    copy.start()
    copy.wait()

    def down_rows(n, carry):
        at = pl.ds(pl.multiple_of(n * row_len, row_len), row_len)
        filled[...] = lax.dot_general(
            normed[:, at], product[...], (((0,), (0,)), ((), ())), preferred_element_type=F32
        ).astype(BF16)
        copy = pltpu.make_async_copy(filled, big_grad.at[0, at], token_sem.at[1])
        copy.start()
        copy.wait()
        return carry

    lax.fori_loop(0, features // row_len, down_rows, 0)
    complete(7)
    for copies in (cot_copies, mid_copies, square_copies):
        sent_tokens(copies)
    for copy in (square_near, square_diag, square_pair, part_near, part_diag, part_pair):
        copy.wait_send()
    for i in range(8):
        for k in (1, 2, 3):
            line_copy(i, k).wait_send()
        for k in range(LINE):
            for copy in first(i, k):
                copy.wait_send()
        for copy in second(i):
            copy.wait_send()
    for copy in saves[1:]:
        copy.wait()


def pieces_of(wide, features):
    size = features // wide
    if size % HEAD_DIM:
        return [(0, 0, features)]
    places = [(w, (w // 16 * 4 + w % 4) * LINE + w // 4 % LINE) for w in range(wide)]
    return [(whole * size, kept * size, size) for whole, kept in places]


def split_refs(refs, counts):
    parts, at = [], 0
    for count in counts:
        parts.append(refs[at : at + count])
        at += count
    return parts


def forward(wide, weights, cot, x, lengths):
    small, large = weights[0].shape[1] // 2, weights[5].shape[1] // 2
    quarter, features = x.shape
    tokens, row_len, heads = 4 * quarter, 2 * quarter, small // HEAD_DIM
    steps = wide.bit_length() - 1
    anywhere = pl.BlockSpec(memory_space=pl.ANY)
    dma = pltpu.SemaphoreType.DMA
    outs = [
        ((features, 2 * small), BF16),
        ((features, 2 * small), BF16),
        ((features, small), BF16),
        ((features, large), BF16),
        ((features, large), BF16),
        ((features, large), BF16),
        ((tokens, features), BF16),
        ((tokens, features), BF16),
        ((tokens, small), BF16),
        ((tokens, small), BF16),
        ((tokens, small), BF16),
        ((tokens, small), BF16),
        ((tokens, small), BF16),
        ((tokens, small), BF16),
        ((tokens, small), BF16),
        ((2, heads, row_len, row_len), BF16),
        ((quarter, features), F32),
        ((tokens, features), BF16),
        ((tokens, large), BF16),
        ((tokens, large), BF16),
        ((tokens, large), BF16),
        ((tokens, HEAD_DIM), F32),
        ((16, row_len), F32),
        ((3, features, large), BF16),
    ]
    held = [
        ((tokens, features), BF16),
        ((2, features, small), BF16),
        ((tokens, small), BF16),
        ((tokens, small), BF16),
        ((tokens, small), BF16),
        ((tokens, small), BF16),
        ((tokens, small), BF16),
        ((tokens, small), BF16),
        ((tokens, small), BF16),
        ((2, heads, row_len, row_len), BF16),
        ((tokens, small), BF16),
        ((tokens, features), BF16),
        ((row_len, features), BF16),
        ((quarter, features), BF16),
        ((tokens, HEAD_DIM), F32),
        ((row_len, HEAD_DIM), F32),
        ((quarter, HEAD_DIM), F32),
        ((tokens, HEAD_DIM), F32),
        ((8, row_len), F32),
        ((tokens, features), BF16),
        ((quarter, features), F32),
        ((features, large), BF16),
        ((tokens, large), BF16),
        ((tokens, large), BF16),
        ((tokens, large), BF16),
        ((quarter, features), BF16),
        ((8, row_len), F32),
        ((row_len, large), BF16),
    ]
    sems = [
        (8, 3), (8, 3), (8,), (8, 6 + steps), (8, 6 + steps), (8,), (17,), (2,), (4, 3), (4, 3), (7,), (7,),
        (2, len(pieces_of(wide, features))),
    ]
    return pl.pallas_call(
        functools.partial(forward_kernel, wide, small, large),
        out_shape=[jax.ShapeDtypeStruct(s, t) for s, t in outs],
        in_specs=[anywhere] * 10 + [pl.BlockSpec(memory_space=pltpu.SMEM)],
        out_specs=[anywhere] * len(outs),
        scratch_shapes=[pltpu.VMEM(s, t) for s, t in held] + [dma(s) for s in sems],
        compiler_params=pltpu.CompilerParams(
            has_side_effects=True, collective_id=1, vmem_limit_bytes=60 << 20
        ),
        cost_estimate=pl.CostEstimate(flops=0, bytes_accessed=300 << 20, transcendentals=0),
    )(*weights, cot, x, lengths)


def backward_kernel(wide, small, large, *refs):
    (
        (cot_in, product_in, left_in, right_in, mid_in, middle_in, normed_in, gate_in, mixed_in, query_pre_in,
         key_pre_in, query_in, key_in, value_in, probs_in, square_in, ends_in, output_w, vg_w, qk_w, left_w, right_w,
         down_w, x_in, _),
        (output_out, gate_out, value_out, query_out, key_out, left_out, right_out, down_out, layer_out, input_grad_out,
         grad_middle_out,
         out_own, out_near, out_far, out_source, grad_own, grad_near, grad_far, branch_out, big_grad, big_near, big_far,
         big_line, big_more),
        (held_tokens, normed, weights, gate, mixed, query, key, value, grad_blended, grad_mixed, vg_grad, qk_grad,
         inner, inner_core, inner_sum, inner_far, inner_col, scale, ends, part_core, part_far, out_core, grad_core, own,
         middle, held, near, far, line, stage, added, filled, small_result, big_result),
        (load_sem, send, recv, line_send, line_recv, big_send, big_recv, big_line_send, big_line_recv, small_send,
         small_recv, stage_sem, result_sem, more_send, more_recv, chunk_sem, big_more_send, big_more_recv, piece_sem),
    ) = split_refs(refs, (25, 24, 34, 19))
    branch = held_tokens
    me, core, z, on_line, flip = place_of(wide)
    extra = list(range(4, wide.bit_length() - 1))
    plane_at = (me // 16) * 4 + me % 4
    others = [on_line(k)[0] for k in (1, 2, 3)] + [flip(b) for b in [0, 1] + extra]
    tokens, features = held_tokens.shape
    quarter, row_len = tokens // 4, tokens // 2
    rb = features // wide
    q = LINE * rb
    h = q // 2
    heads = small // HEAD_DIM
    near_device, far_device = (me, 1 - core), (flip(2), core)
    lower = z % 2 == 0
    widths = [min(small, large - at) for at in range(0, large, small)]
    products = [query, key, value]
    lefts = [gate, mixed, grad_blended]
    rights = [grad_mixed, vg_grad.at[:, pl.ds(0, small)], vg_grad.at[:, pl.ds(small, small)]]

    def remote(source, target, send_sem, recv_sem, device):
        return pltpu.make_async_remote_copy(
            src_ref=source, dst_ref=target, send_sem=send_sem, recv_sem=recv_sem,
            device_id=device, device_id_type=pl.DeviceIdType.MESH,
        )

    def block(m):
        return pl.multiple_of((plane_at ^ m) * q, q)

    def rows(b):
        return pl.ds(b * quarter, quarter)

    def loops(count, body):
        def step(n, carry):
            body(n)
            return carry

        lax.fori_loop(0, count, step, 0)

    pending = {}

    def load(name, source, target):
        copy = pltpu.make_async_copy(source, target, load_sem.at[len(pending)])
        copy.start()
        pending[name] = copy

    def load_cut(name, source, targets):
        for n, target in enumerate(targets):
            load(name + str(n), source.at[:, pl.ds(n * small, widths[n])], target.at[:, pl.ds(0, widths[n])])

    def ready(*names):
        for name in names:
            pending[name].wait()

    def ready_cut(name):
        ready(*(name + str(n) for n in range(len(widths))))

    results = []

    def give(source, target):
        copy = pltpu.make_async_copy(source, target, result_sem.at[len(results)])
        copy.start()
        results.append(copy)
        return len(results) - 1

    def given(n):
        if results[n] is not None:
            results[n].wait()
            results[n] = None

    load("cot", cot_in, held_tokens)
    load_cut("product", product_in, products)
    load_cut("down", down_w, [held.at[n] for n in range(3)])
    load_cut("right", right_in, rights)
    load_cut("left", left_in, lefts)
    load("mid", mid_in, normed)
    load("middle", middle_in, middle)
    load("own", cot_in.at[rows(0)], own)
    load("square", square_in, scale)
    load("ends", ends_in, ends)
    for r in range(2):
        for n in range(heads):
            load("probs%d%d" % (r, n), probs_in.at[r, n], held.at[3 + r, pl.ds(n * row_len, row_len)])
    meet([(other, core) for other in others] + [(me, 1 - core)])


    def rows_at(i, start, size):
        return held.at[i, pl.ds(pl.multiple_of(start, min(size, h)), size)]

    def step(i, j, start, size, target, bit):
        return remote(rows_at(i, start, size), target, send.at[i, j], recv.at[i, j], (flip(bit), core))

    def copies(i, j):
        if j == 0:
            return step(i, 0, block(3), h, near.at[i, 0], 1)
        if j == 1:
            return step(i, 1, block(3) + h, h, near.at[i, 1], 0)
        if j == 2:
            return step(i, 2, block(1) + h, h, far.at[i, 0, pl.ds(h, h)], 0)
        if j == 3:
            return step(i, 3, block(2), h, far.at[i, 1, pl.ds(0, h)], 1)
        if j == 4:
            return step(i, 4, block(1), h, far.at[i, 0, pl.ds(0, h)], 0)
        return step(i, 5, block(2) + h, h, far.at[i, 1, pl.ds(h, h)], 1)

    def line_copy(i, k):
        device, there = on_line(k)
        return remote(
            rows_at(i, block(0) + there * rb, rb), line.at[i, k - 1],
            line_send.at[i, k - 1], line_recv.at[i, k - 1], (device, core),
        )

    tile = min(64, h)

    def add(target, start, size, *sources):
        def body(n):
            at = pl.ds(pl.multiple_of(start + n * tile, tile), tile)
            total = target[at].astype(F32)
            for source in sources:
                total = total + source[pl.ds(pl.multiple_of(n * tile, tile), tile)].astype(F32)
            target[at] = total.astype(BF16)

        loops(size // tile, body)

    def begin(i, side, other):
        def fill(m):
            held[i, pl.ds(block(m), q)] = lax.dot_general(
                side[:, pl.ds(block(m), q)], other(), (((0,), (0,)), ((), ())), preferred_element_type=F32
            ).astype(BF16)

        if extra:
            loops(wide // LINE, fill)
            for e in reversed(range(len(extra))):
                size = q << (2 + e)
                half = plane_at >> (2 + e)
                copy = remote(
                    rows_at(i, (half ^ 1) * size, size), branch_more(i, e, size),
                    more_send.at[i, e], more_recv.at[i, e], (flip(extra[e]), core),
                )
                copy.start()
                copy.wait()
                add(held.at[i], half * size, size, branch_more(i, e, size))
            for j in range(4):
                copies(i, j).start()
        else:
            fill(3)
            copies(i, 0).start()
            copies(i, 1).start()
            fill(1)
            copies(i, 2).start()
            fill(2)
            copies(i, 3).start()
            fill(0)

    def branch_more(i, e, size):
        return far.at[i, e, pl.ds(0, size)]

    def fold(i):
        copies(i, 0).wait_recv()
        add(held.at[i], block(1), h, near.at[i, 0])
        copies(i, 4).start()
        copies(i, 1).wait_recv()
        add(held.at[i], block(2) + h, h, near.at[i, 1])
        copies(i, 5).start()

    def to_line(i):
        for j in range(2, 6):
            copies(i, j).wait_recv()
        add(held.at[i], block(0), q, far.at[i, 0], far.at[i, 1])
        for k in (1, 2, 3):
            line_copy(i, k).start()

    def finish(i, out):
        for k in (1, 2, 3):
            line_copy(i, k).wait_recv()
        own = held[i, pl.ds(block(0) + pl.multiple_of(z * rb, rb), rb)].astype(F32) + line[i, 1].astype(F32)
        other = line[i, 0].astype(F32) + line[i, 2].astype(F32)
        if small_done:
            given(small_done[-1])
        put(small_result, own, other, small)
        small_done.append(give(small_result, out))

    small_done = []

    def put(target, own, other, cols):
        @pl.when(lower)
        def _():
            target[:, pl.ds(0, cols)] = own
            target[:, pl.ds(cols, cols)] = other

        @pl.when(jnp.logical_not(lower))
        def _():
            target[:, pl.ds(0, cols)] = other
            target[:, pl.ds(cols, cols)] = own


    def big_rows(n, start, size):
        return big_grad.at[n, pl.ds(pl.multiple_of(start, min(size, rb)), size)]

    def big_copy(n, j):
        if j == 0:
            source, target = big_rows(n, block(3), h), big_near.at[n, 0]
        elif j == 1:
            source, target = big_rows(n, block(3) + h, h), big_near.at[n, 1]
        elif j == 2:
            source, target = big_rows(n, block(1) + h, h), big_far.at[n, 0, pl.ds(h, h)]
        elif j == 3:
            source, target = big_rows(n, block(2), h), big_far.at[n, 1, pl.ds(0, h)]
        elif j == 4:
            source, target = big_rows(n, block(1), h), big_far.at[n, 0, pl.ds(0, h)]
        else:
            source, target = big_rows(n, block(2) + h, h), big_far.at[n, 1, pl.ds(h, h)]
        bit = (1, 0, 0, 1, 0, 1)[j]
        return remote(source, target, big_send.at[n, j], big_recv.at[n, j], (flip(bit), core))

    def big_line_copy(n, k):
        device, there = on_line(k)
        return remote(
            big_rows(n, block(0) + there * rb, rb), big_line.at[n, k - 1],
            big_line_send.at[n, k - 1], big_line_recv.at[n, k - 1], (device, core),
        )

    def move(j, source, target):
        copy = pltpu.make_async_copy(source, target, stage_sem.at[j])
        copy.start()
        return copy

    def big_add(n, start, *sources):
        moves = [move(0, big_rows(n, start, h), stage.at[pl.ds(0, h)])]
        for j, source in enumerate(sources):
            moves.append(move(1 + j, source, added.at[pl.ds(j * h, h)]))
        for copy in moves:
            copy.wait()
        add(stage, 0, h, *(added.at[pl.ds(j * h, h)] for j in range(len(sources))))
        move(0, stage.at[pl.ds(0, h)], big_rows(n, start, h)).wait()

    def big_begin(n, side=None, parts=None):
        def fill(m):
            if side is None:
                return
            for c, width in enumerate(widths):
                filled[:, pl.ds(c * small, width)] = lax.dot_general(
                    side[:, pl.ds(block(m), q)], parts[c][:, pl.ds(0, width)], (((0,), (0,)), ((), ())),
                    preferred_element_type=F32,
                ).astype(BF16)
            move(3, filled, big_rows(n, block(m), q)).wait()

        if extra:
            loops(wide // LINE, fill)
            for e in reversed(range(len(extra))):
                size = q << (2 + e)
                half = plane_at >> (2 + e)
                copy = remote(
                    big_rows(n, (half ^ 1) * size, size), big_more.at[n, e, pl.ds(0, size)],
                    big_more_send.at[n, e], big_more_recv.at[n, e], (flip(extra[e]), core),
                )
                copy.start()
                copy.wait()
                loops(
                    size // h,
                    lambda i: big_add(
                        n, half * size + i * h, big_more.at[n, e, pl.ds(pl.multiple_of(i * h, h), h)]
                    ),
                )
            for j in range(4):
                big_copy(n, j).start()
        else:
            fill(3)
            big_copy(n, 0).start()
            big_copy(n, 1).start()
            fill(1)
            big_copy(n, 2).start()
            fill(2)
            big_copy(n, 3).start()
            fill(0)

    def big_fold(n):
        big_copy(n, 0).wait_recv()
        big_add(n, block(1), big_near.at[n, 0])
        big_copy(n, 4).start()
        big_copy(n, 1).wait_recv()
        big_add(n, block(2) + h, big_near.at[n, 1])
        big_copy(n, 5).start()

    def big_to_line(n):
        for j in range(2, 6):
            big_copy(n, j).wait_recv()
        for j in range(2):
            here = pl.ds(j * h, h)
            big_add(n, block(0) + j * h, big_far.at[n, 0, here], big_far.at[n, 1, here])
        for k in (1, 2, 3):
            big_line_copy(n, k).start()

    def big_finish(n, out):
        for k in (1, 2, 3):
            big_line_copy(n, k).wait_recv()
        moves = [move(k, big_line.at[n, k], added.at[pl.ds(k * rb, rb)]) for k in range(3)]
        moves.append(move(3, big_rows(n, block(0) + z * rb, rb), added.at[pl.ds(3 * rb, rb)]))
        for copy in moves:
            copy.wait()
        if results_of_big:
            given(results_of_big[-1])
        got = [added[pl.ds(k * rb, rb)].astype(F32) for k in range(4)]
        put(big_result, got[3] + got[1], got[0] + got[2], large)
        results_of_big.append(give(big_result, out))

    results_of_big = []


    def gate_product(r):
        at = pl.ds(r * row_len, row_len)
        for c, width in enumerate(widths):
            here = pl.ds(0, width)
            total = jnp.dot(held_tokens[at], held[c, :, here], preferred_element_type=F32)
            grad_left = (total * rights[c][at, here].astype(F32)).astype(BF16)
            lefts[c][at, here] = (total * lefts[c][at, here].astype(F32)).astype(BF16)
            rights[c][at, here] = grad_left

    chunk = row_len // 2
    chunks = features // chunk
    wide_cols = 2 * small

    def chunk_copies(n, slot):
        source = pl.ds(pl.multiple_of(n * chunk, chunk), chunk)
        target = pl.ds(pl.multiple_of(slot * chunk, chunk), chunk)
        return [
            pltpu.make_async_copy(
                w.at[source, pl.ds(at, cols)], weights.at[2 * i + j, target, pl.ds(0, cols)], chunk_sem.at[slot, 2 * i + j]
            )
            for i, w in enumerate((left_w, right_w))
            for j, (at, cols) in enumerate(((0, wide_cols), (wide_cols, large - wide_cols)))
        ]

    def mid_part(r):
        at = pl.ds(r * row_len, row_len)
        for copy in chunk_copies(0, 0):
            copy.start()

        def body(n):
            slot = n % 2

            @pl.when(n + 1 < chunks)
            def _():
                for copy in chunk_copies(n + 1, 1 - slot):
                    copy.start()

            for copy in chunk_copies(n, slot):
                copy.wait()
            here = pl.ds(pl.multiple_of(slot * chunk, chunk), chunk)
            total = jnp.zeros((row_len, chunk), F32)
            for i, parts in enumerate((rights, lefts)):
                for c, width in enumerate(widths):
                    w = weights[2 * i + c // 2, here, pl.ds((c % 2) * small, width)]
                    total = total + lax.dot_general(
                        parts[c][at, pl.ds(0, width)], w, (((1,), (1,)), ((), ())), preferred_element_type=F32
                    )
            held_tokens[at, pl.ds(pl.multiple_of(n * chunk, chunk), chunk)] = total.astype(BF16)

        loops(chunks, body)

    def output_part(r):
        at = pl.ds(r * row_len, row_len)

        def body(n):
            here = pl.ds(pl.multiple_of(n * row_len, row_len), row_len)
            total = jnp.zeros((row_len, row_len), F32)
            for c, width in enumerate(widths):
                total = total + lax.dot_general(
                    products[c][at, pl.ds(0, width)], held[c, here, pl.ds(0, width)], (((1,), (1,)), ((), ())),
                    preferred_element_type=F32,
                )
            held_tokens[at, here] = total.astype(BF16)

        loops(features // row_len, body)

    def middle_rows(n):
        at = pl.ds(pl.multiple_of(n * 32, 32), 32)
        grad = held_tokens[at].astype(F32) + part_core[at].astype(F32) + part_far[at].astype(F32)
        values = middle[at]
        s = lax.rsqrt(jnp.mean(values * values, axis=1, keepdims=True) + EPS)
        grad = own[at].astype(F32) + norm_back(values, s, grad)
        middle[at] = grad
        own[at] = grad.astype(BF16)


    def grad_rows(row):
        at = pl.ds(row * row_len, row_len)
        total = jnp.zeros((row_len, small), F32)
        for n in range(4):
            total = total + jnp.dot(
                branch[at, pl.ds(n * row_len, row_len)], weights[n, :, pl.ds(0, small)], preferred_element_type=F32
            )
        grad_blended[at] = total.astype(BF16)
        m = mixed[at].astype(F32)
        g = gate[at].astype(F32)
        scaled = m * scale[at, 0:1]
        vg_grad[at, pl.ds(small, small)] = (total * scaled).astype(BF16)
        grad_mixed[at] = (g * scaled).astype(BF16)
        inner[:, at] = lax.dot_general(
            jnp.ones((8, small), F32), total * g * m, (((1,), (1,)), ((), ())),
            preferred_element_type=F32, precision=lax.Precision.HIGHEST,
        )

    def scale_rows(n):
        at = pl.ds(pl.multiple_of(n * 128, 128), 128)
        scale[at] = lax.rsqrt(scale[at] / features + EPS)

    def mix_rows(n):
        at = pl.ds(pl.multiple_of(n * 128, 128), 128)
        s = scale[at, 0:1]
        value_of = s * (grad_blended[at].astype(F32) * gate[at].astype(F32))
        value_of = value_of - mixed[at].astype(F32) * (s * s * s * (inner_col[at, 0:1] / features))
        grad_mixed[at] = value_of.astype(BF16)

    first_head = (core * 2 + z % 2) * heads

    def attend_back(row):
        at = pl.ds(row * row_len, row_len)

        def place(dim):
            index = lax.broadcasted_iota(jnp.int32, (row_len, row_len), dim) + core * quarter
            return jnp.where(index >= row_len, index - row_len, index).astype(F32)

        def slope(pre):
            s = sigmoid(pre)
            return s * (1.0 + pre * (1.0 - s))

        def body(head):
            cols = pl.ds(pl.multiple_of(head * HEAD_DIM, HEAD_DIM), HEAD_DIM)
            more = pl.ds(pl.multiple_of(small + head * HEAD_DIM, HEAD_DIM), HEAD_DIM)
            got = grad_mixed[at, cols]
            grad_probs = lax.dot_general(
                got, value[at, cols], (((1,), (1,)), ((), ())), preferred_element_type=F32
            )
            to, source = place(0), place(1)
            allowed = (to >= source) & (to < ends[pl.ds(8 * row, 1), :])
            rate = (first_head + head).astype(F32) * (DECAY * HEAD_DIM / features)
            decay = jnp.where(allowed, jnp.exp(-rate * jnp.maximum(to - source, 0.0)), 0.0)
            grad_scores = (grad_probs * decay).astype(BF16)
            probs = held[3 + row, pl.ds(pl.multiple_of(head * row_len, row_len), row_len)]
            vg_grad[at, cols] = lax.dot_general(
                probs, got, (((0,), (0,)), ((), ())), preferred_element_type=F32
            ).astype(BF16)
            grad_query = jnp.dot(grad_scores, key[at, cols], preferred_element_type=F32)
            qk_grad[at, cols] = (grad_query * slope(gate[at, cols].astype(F32))).astype(BF16)
            grad_key = lax.dot_general(
                grad_scores, query[at, cols], (((0,), (0,)), ((), ())), preferred_element_type=F32
            )
            qk_grad[at, more] = (grad_key * slope(mixed[at, cols].astype(F32))).astype(BF16)

        loops(heads, body)

    def load_weights(pair):
        for n in range(2):
            here = pl.ds((2 * pair + n) * row_len, row_len)
            load("vg%d%d" % (pair, n), vg_w.at[here], weights.at[n])
            load("qk%d%d" % (pair, n), qk_w.at[here], weights.at[2 + n])

    def normed_part(pair, row):
        at = pl.ds(row * row_len, row_len)
        for n in range(2):
            total = lax.dot_general(vg_grad[at], weights[n], (((1,), (1,)), ((), ())), preferred_element_type=F32)
            total = total + lax.dot_general(
                qk_grad[at], weights[2 + n], (((1,), (1,)), ((), ())), preferred_element_type=F32
            )
            branch[at, pl.ds((2 * pair + n) * row_len, row_len)] = total.astype(BF16)

    def small_copy(n, source, target, device):
        return remote(source, target, small_send.at[n], small_recv.at[n], device)

    pieces = pieces_of(wide, features)

    def layer_rows(n):
        at = pl.ds(pl.multiple_of(n * 32, 32), 32)
        total = middle[at] + own[at].astype(F32) + part_core[at].astype(F32) + part_far[at].astype(F32)
        own[at] = total.astype(BF16)

    def input_rows(n):
        at = pl.ds(pl.multiple_of(n * 32, 32), 32)
        grad = own[at].astype(F32) + part_core[at].astype(F32) + part_far[at].astype(F32)
        values = part_core[pl.ds(pl.multiple_of(quarter + n * 32, 32), 32)].astype(F32)
        s = lax.rsqrt(jnp.mean(values * values, axis=1, keepdims=True) + EPS)
        middle[at] = middle[at] + norm_back(values, s, grad)

    def put_pieces(row, source, target):
        copies = [
            pltpu.make_async_copy(source.at[:, pl.ds(b, size)], target.at[:, pl.ds(a, size)], piece_sem.at[row, n])
            for n, (a, b, size) in enumerate(pieces)
        ]
        for copy in copies:
            copy.start()
        return copies


    big_begin(0)
    ready("cot")
    ready_cut("product")
    ready_cut("down")
    ready_cut("left")
    ready_cut("right")
    gate_product(1)
    gate_product(0)
    mid_part(1)
    part_diag = small_copy(0, held_tokens.at[rows(3)], part_core.at[rows(1)], near_device)
    part_near = small_copy(1, held_tokens.at[rows(1)], part_core.at[rows(0)], near_device)
    part_pair = small_copy(2, held_tokens.at[rows(2)], part_far, far_device)
    part_diag.start()
    part_diag.wait_recv()
    add(held_tokens, 2 * quarter, quarter, part_core.at[rows(1)])
    part_pair.start()
    big_fold(0)
    mid_part(0)
    part_near.start()
    ready("mid")
    big_begin(1, normed, rights)
    ready("middle", "own")
    part_near.wait_recv()
    part_pair.wait_recv()
    loops(quarter // 32, middle_rows)
    branch_own = move(4, own, branch_out.at[rows(0)])
    branch_near = small_copy(3, own, branch_out.at[rows(1)], near_device)
    branch_far = small_copy(4, own, branch_out.at[rows(2)], far_device)
    branch_pass = small_copy(5, branch_out.at[rows(2)], branch_out.at[rows(3)], near_device)
    branch_far.start()
    branch_near.start()
    middle_given = give(middle, grad_middle_out)
    for n in range(4):
        load("output%d" % n, output_w.at[pl.ds(n * row_len, row_len)], weights.at[n, :, pl.ds(0, small)])
    big_to_line(0)
    big_begin(2, normed, lefts)
    load("gate", gate_in, gate)
    load("mixed", mixed_in, mixed)
    load("normed", normed_in, normed)
    big_fold(1)
    for copy in (part_diag, part_near, part_pair):
        copy.wait_send()
    output_part(1)
    out_diag = small_copy(6, held_tokens.at[rows(3)], out_core, near_device)
    out_diag.start()
    output_part(0)
    out_next = small_copy(7, held_tokens.at[rows(1)], out_near, near_device)
    out_next.start()
    out_mine = move(5, held_tokens.at[rows(0)], out_own)
    out_diag.wait_recv()
    add(held_tokens, 2 * quarter, quarter, out_core)
    out_pair = small_copy(8, out_source, out_far, far_device)
    move(0, held_tokens.at[rows(2)], out_source).wait()
    out_pair.start()
    load("value", value_in, value)
    load("query", query_in, query)
    load("key", key_in, key)
    out_mine.wait()
    out_next.wait_send()
    out_diag.wait_send()
    branch_own.wait()
    branch_near.wait_recv()
    load("branch0", branch_out.at[pl.ds(0, row_len)], branch.at[pl.ds(0, row_len)])
    ready("square")
    loops(tokens // 128, scale_rows)
    branch_far.wait_recv()
    branch_pass.start()
    ready("branch0", "output0", "output1", "output2", "output3", "gate", "mixed")
    grad_rows(0)
    branch_pass.wait_recv()
    load("branch1", branch_out.at[pl.ds(row_len, row_len)], branch.at[pl.ds(row_len, row_len)])
    ready("branch1")
    grad_rows(1)
    core_copy = small_copy(9, inner, inner_core, near_device)
    core_copy.start()
    core_copy.wait_recv()
    for b in range(4):
        inner_sum[:, rows(b)] = inner[:, rows(b)] + inner_core[:, rows(b ^ 1)]
    far_copy = small_copy(10, inner_sum, inner_far, far_device)
    far_copy.start()
    begin(0, branch, lambda: grad_mixed[...])
    far_copy.wait_recv()
    for b in range(4):
        total = inner_sum[:, rows(b)] + inner_far[:, rows(b ^ 2)]
        inner_col[rows(b)] = jnp.broadcast_to(total.T[:, 0:1], (quarter, HEAD_DIM))
    loops(tokens // 128, mix_rows)
    load("query_pre", query_pre_in, gate)
    load("key_pre", key_pre_in, mixed)
    load_weights(0)
    ready("normed")
    begin(1, normed, lambda: vg_grad[:, pl.ds(small, small)])
    big_to_line(1)
    big_fold(2)
    ready("value", "query", "key", "query_pre", "key_pre", "ends")
    for r in range(2):
        ready(*("probs%d%d" % (r, n) for n in range(heads)))
    attend_back(1)
    fold(0)
    attend_back(0)
    begin(2, normed, lambda: vg_grad[:, pl.ds(0, small)])
    fold(1)
    begin(3, normed, lambda: qk_grad[:, pl.ds(0, small)])
    begin(4, normed, lambda: qk_grad[:, pl.ds(small, small)])
    big_to_line(2)
    to_line(0)
    fold(2)
    ready("vg00", "vg01", "qk00", "qk01")
    normed_part(0, 1)
    normed_part(0, 0)
    load_weights(1)
    big_finish(0, down_out)
    to_line(1)
    ready("vg10", "vg11", "qk10", "qk11")
    normed_part(1, 1)
    grad_diag = small_copy(11, branch.at[rows(3)], grad_core, near_device)
    grad_next = small_copy(12, branch.at[rows(1)], grad_near, near_device)
    grad_pair = small_copy(13, branch.at[rows(2)], grad_far, far_device)
    grad_diag.start()
    normed_part(1, 0)
    grad_next.start()
    grad_given = give(branch.at[rows(0)], grad_own)
    grad_diag.wait_recv()
    add(branch, 2 * quarter, quarter, grad_core)
    grad_pair.start()
    fold(3)
    fold(4)
    big_finish(1, left_out)
    given(middle_given)
    branch_near.wait_send()
    branch_far.wait_send()
    out_next.wait_recv()
    out_pair.wait_recv()
    load("middle2", middle_in, middle)
    load("out_own", out_own, own)
    load("out_near", out_near, part_core.at[rows(0)])
    load("out_far", out_far, part_far)
    to_line(2)
    ready("middle2", "out_own", "out_near", "out_far")
    loops(quarter // 32, layer_rows)
    layer_pieces = put_pieces(0, own, layer_out)
    load("middle3", grad_middle_out, middle)
    x_copies = [
        pltpu.make_async_copy(x_in.at[:, pl.ds(a, size)], part_core.at[rows(1), pl.ds(b, size)], piece_sem.at[1, n])
        for n, (a, b, size) in enumerate(pieces)
    ]
    for copy in x_copies:
        copy.start()
    finish(0, output_out)
    finish(1, gate_out)
    to_line(3)
    big_finish(2, right_out)
    finish(2, value_out)
    to_line(4)
    for copy in layer_pieces:
        copy.wait()
    given(grad_given)
    grad_next.wait_recv()
    grad_pair.wait_recv()
    load("grad_own", grad_own, own)
    load("grad_near", grad_near, part_core.at[rows(0)])
    load("grad_far", grad_far, part_far)
    for copy in x_copies:
        copy.wait()
    ready("middle3", "grad_own", "grad_near", "grad_far")
    loops(quarter // 32, input_rows)
    grad_pieces = put_pieces(2, middle, input_grad_out)
    finish(3, query_out)
    finish(4, key_out)
    for copy in grad_pieces:
        copy.wait()
    for copy in (branch_pass, out_pair, core_copy, far_copy, grad_diag, grad_next, grad_pair):
        copy.wait_send()
    for i in range(5):
        for j in range(6):
            copies(i, j).wait_send()
        for k in (1, 2, 3):
            line_copy(i, k).wait_send()
    for n in range(3):
        for j in range(6):
            big_copy(n, j).wait_send()
        for k in (1, 2, 3):
            big_line_copy(n, k).wait_send()
    for n in range(len(results)):
        given(n)


def backward(wide, arrays, small, large):
    tokens, features = arrays[0].shape
    quarter, row_len = tokens // 4, tokens // 2
    rb = features // wide
    q = LINE * rb
    extra = max(1, wide.bit_length() - 5)
    anywhere = pl.BlockSpec(memory_space=pl.ANY)
    dma = pltpu.SemaphoreType.DMA
    many = features // 2 if wide > 16 else 16
    far_rows = max(q, many)
    part = (quarter, features)
    outs = [((rb, 2 * small), F32)] * 5 + [((rb, 2 * large), F32)] * 3 + [
        (part, BF16),
        (part, F32),
        (part, F32),
        *[(part, BF16)] * 7,

        ((tokens, features), BF16),
        ((3, features, large), BF16),
        ((3, 2, q // 2, large), BF16),
        ((3, 2, q, large), BF16),
        ((3, 3, rb, large), BF16),
        ((3, extra, many, large), BF16),
    ]
    held = [
        ((tokens, features), BF16),
        ((tokens, features), BF16),
        ((4, row_len, 2 * small), BF16),
        *[((tokens, small), BF16)] * 7,
        ((tokens, 2 * small), BF16),
        ((tokens, 2 * small), BF16),
        *[((8, tokens), F32)] * 4,
        ((tokens, HEAD_DIM), F32),
        ((tokens, HEAD_DIM), F32),
        ((16, row_len), F32),
        ((row_len, features), BF16),
        *[(part, BF16)] * 4,
        (part, F32),
        ((5, features, small), BF16),
        ((5, 2, q // 2, small), BF16),
        ((5, 2, far_rows, small), BF16),
        ((5, 3, rb, small), BF16),
        ((q // 2, large), BF16),
        ((q, large), BF16),
        ((q, large), BF16),
        ((rb, 2 * small), F32),
        ((rb, 2 * large), F32),
    ]
    sems = [
        (60,), (5, 6), (5, 6), (5, 3), (5, 3), (3, 6), (3, 6), (3, 3), (3, 3), (14,), (14,), (6,), (10,), (5, extra),
        (5, extra), (2, 4), (3, extra), (3, extra), (3, len(pieces_of(wide, features))),
    ]
    return pl.pallas_call(
        functools.partial(backward_kernel, wide, small, large),
        out_shape=[jax.ShapeDtypeStruct(s, t) for s, t in outs],
        in_specs=[anywhere] * len(arrays),
        out_specs=[anywhere] * len(outs),
        scratch_shapes=[pltpu.VMEM(s, t) for s, t in held] + [dma(s) for s in sems],
        input_output_aliases={24: 19},
        compiler_params=pltpu.CompilerParams(
            has_side_effects=True, collective_id=2, vmem_limit_bytes=60 << 20
        ),
        cost_estimate=pl.CostEstimate(flops=0, bytes_accessed=300 << 20, transcendentals=0),
    )(*arrays)


def sigmoid(z):
    return 1.0 / (1.0 + jnp.exp(-z))


def on_device(
    layer_input, doc_lengths, w_query, w_key, w_value, w_gate, w_output, w_left, w_right, w_down, cotangent, *, wide
):
    features = layer_input.shape[1]
    cut = len(pieces_of(wide, features)) == 1
    x = to_kept(layer_input, wide) if cut else layer_input
    cot = to_kept(cotangent, wide) if cut else cotangent
    weights = [w_query, w_key, w_value, w_gate, w_output, w_left, w_right, w_down]
    (
        qk_w, vg_w, output_w, left_w, right_w, down_w, normed, cot_all, query_pre, key_pre, gate, queries, keys, values,
        mixed, probs, middle, mid, left, right, product, squares, ends, big_grad,
    ) = forward(wide, weights, cot, x, doc_lengths)
    (
        grad_output, grad_gate, grad_value, grad_query, grad_key, grad_left, grad_right, grad_down, layer_output,
        input_grad, *_
    ) = backward(
        wide,
        [
            cot_all, product, left, right, mid, middle, normed, gate, mixed, query_pre, key_pre, queries, keys, values,
            probs, squares, ends, output_w, vg_w, qk_w, left_w, right_w, down_w, x, big_grad,
        ],
        queries.shape[1],
        left.shape[1],
    )
    if cut:
        layer_output, input_grad = from_kept(layer_output, wide), from_kept(input_grad, wide)
    return (
        layer_output,
        input_grad,
        grad_query,
        grad_key,
        grad_value,
        grad_gate,
        grad_output,
        grad_left,
        grad_right,
        grad_down,
    )


def solution(mesh):
    both, weight = P(("wide", "narrow"), None), P("wide", "narrow")
    wide = mesh.shape["wide"]

    def body(*args):
        return on_device(*args, wide=wide)

    return jax.shard_map(
        body,
        mesh=mesh,
        in_specs=(both, P("wide", None)) + (weight,) * 8 + (both,),
        out_specs=(both, both) + (weight,) * 8,
        check_vma=False,
    )
```

```python
import functools

import jax
import jax.numpy as jnp
from jax import lax
from jax.experimental import pallas as pl
from jax.experimental.pallas import tpu as pltpu
from jax.sharding import PartitionSpec as P

HEAD_DIM = 128
LINE = 4
LATE = 2
EPS = 1e-06
DECAY = 2.0
F32 = jnp.float32
BF16 = jnp.bfloat16


def norm_back(values, scale, gradient):
    inner = jnp.mean(gradient * values, axis=-1, keepdims=True)
    return scale * gradient - values * (scale * scale * scale) * inner


def to_kept(value, wide):
    tokens, cols = value.shape
    value = value.reshape(tokens, wide // 16, LINE, 4, cols // wide)
    return value.transpose(0, 1, 3, 2, 4).reshape(tokens, cols)


def from_kept(value, wide):
    tokens, cols = value.shape
    value = value.reshape(tokens, wide // 16, 4, LINE, cols // wide)
    return value.transpose(0, 1, 3, 2, 4).reshape(tokens, cols)


def place_of(wide):
    me = lax.axis_index("wide")
    z = (me // 4) % LINE

    def on_line(k):
        there = (z + k) % LINE
        return me + (there - z) * 4, there

    def flip(bit):
        return me + (1 - 2 * ((me >> bit) & 1)) * (1 << bit)

    return me, lax.axis_index("narrow"), z, on_line, flip


def meet(devices):
    barrier = pltpu.get_barrier_semaphore()
    for device in devices:
        pl.semaphore_signal(
            barrier, inc=1, device_id=device, device_id_type=pl.DeviceIdType.MESH
        )
    pl.semaphore_wait(barrier, len(devices))


def forward_kernel(wide, small, large, *refs):
    (
        w_in, (cot_in, x_in, lengths),
        w_out, (normed_out, cot_out, query_pre_out, key_pre_out, gate_out, query_out, key_out, value_out, mixed_out,
                probs_out, middle_out, mid_out, left_out, right_out, product_out, square_out, ends_out, big_grad),
        (normed, wide_w, query_pre, key_pre, gate, query, key, value, mixed, probs, blended, part, part_core, part_far,
         square, square_core, square_far, square_all, ends_far, mid, middle, large_w, left, right, product, x_own, ends_own,
         filled, cot_own, small_own, large_own),
        (line_send, line_recv, own_sem, plane_send, plane_recv, load_sem, save_sem, token_sem, token_send, token_recv,
         small_send, small_recv, piece_sem),
    ) = split_refs(refs, (8, 3, 6, 18, 31, 13))
    me, core, z, on_line, flip = place_of(wide)
    extra = list(range(4, wide.bit_length() - 1))
    plane_at = (me // 16) * 4 + me % 4
    others = [on_line(k)[0] for k in (1, 2, 3)] + [flip(b) for b in [0, 1] + extra]
    quarter, features = x_own.shape
    pieces = pieces_of(wide, features)
    x_loads = [
        pltpu.make_async_copy(x_in.at[:, pl.ds(a, size)], x_own.at[:, pl.ds(b, size)], piece_sem.at[0, n])
        for n, (a, b, size) in enumerate(pieces)
    ]
    cot_loads = [
        pltpu.make_async_copy(cot_in.at[:, pl.ds(a, size)], cot_own.at[:, pl.ds(b, size)], piece_sem.at[1, n])
        for n, (a, b, size) in enumerate(pieces)
    ]
    for copy in x_loads + cot_loads:
        copy.start()
    meet([(other, core) for other in others] + [(me, 1 - core)])
    rb = w_in[0].shape[0]
    q = LINE * rb
    h = q // 2
    row_len = 2 * quarter
    chunks = [(0, 0), (0, small), (1, 0), (1, small), (2, 0), (3, 0), (4, 0), (5, 0)]
    near_device, far_device = (me, 1 - core), (flip(2), core)


    def part_of(i, start, size):
        out, col = chunks[i]
        cols = w_in[i].shape[1] // 2
        return w_out[out].at[pl.ds(pl.multiple_of(start, min(size, rb)), size), pl.ds(col, cols)]

    def block(m):
        return (plane_at ^ m) * q

    def remote(source, target, send_sem, recv_sem, device):
        return pltpu.make_async_remote_copy(
            src_ref=source, dst_ref=target, send_sem=send_sem, recv_sem=recv_sem,
            device_id=device, device_id_type=pl.DeviceIdType.MESH,
        )

    def mine(i, there):
        cols = w_in[i].shape[1] // 2
        return w_in[i].at[:, pl.ds(pl.multiple_of((there % 2) * cols, HEAD_DIM), cols)]

    def line_copy(i, k):
        device, there = on_line(k)
        return remote(
            mine(i, there), part_of(i, block(0) + z * rb, rb),
            line_send.at[i, k - 1], line_recv.at[i, k - 1], (device, core),
        )

    def own_held(i):
        return small_own.at[i] if i < 5 else large_own.at[i - 5]

    def own_load(i):
        return pltpu.make_async_copy(mine(i, z), own_held(i), own_sem.at[0, i])

    def own_store(i):
        return pltpu.make_async_copy(own_held(i), part_of(i, block(0) + z * rb, rb), own_sem.at[1, i])

    def plane(i, j, start, size, bit):
        place = part_of(i, start, size)
        return remote(place, place, plane_send.at[i, j], plane_recv.at[i, j], (flip(bit), core))

    def first(i, k):
        target = part_of(i, block(0) + ((z - k) % LINE) * rb, rb)
        source = target if k else mine(i, z)
        return [
            remote(source, target, plane_send.at[i, 4 * b + k], plane_recv.at[i, 4 * b + k], (flip(b), core))
            for b in (0, 1)
        ]

    def second(i):
        return plane(i, 8, block(1), h, 1), plane(i, 9, block(2) + h, h, 0)

    def start_line(i):
        own_load(i).start()
        for k in (1, 2, 3):
            line_copy(i, k).start()

    def start_own(i):
        for copy in first(i, 0):
            copy.start()

    def start_plane(i):
        own_load(i).wait()
        own_store(i).start()
        for k in (1, 2, 3):
            line_copy(i, k).wait_recv()
            for copy in first(i, k):
                copy.start()

    def forward_plane(i):
        for b, onward in enumerate(second(i)):
            for k in range(LINE):
                first(i, k)[b].wait_recv()
            onward.start()

    def complete(i):
        own_store(i).wait()
        for copy in second(i):
            copy.wait_recv()
        for e, bit in enumerate(extra):
            size = q << (2 + e)
            copy = plane(i, 10 + e, (plane_at >> (2 + e)) * size, size, bit)
            copy.start()
            copy.wait()


    def rows(b):
        return pl.ds(b * quarter, quarter)

    def token_copies(n, source, out):
        send = lambda j, source, device: remote(
            source, out.at[rows(j + 1)], token_send.at[n, j], token_recv.at[n, j], device
        )
        return send(0, source, near_device), send(1, source, far_device), send(2, out.at[rows(2)], near_device)

    def start_tokens(copies):
        copies[0].start()
        copies[1].start()

    def pass_tokens(copies):
        copies[1].wait_recv()
        copies[2].start()

    def end_tokens(copies):
        copies[0].wait_recv()
        copies[2].wait_recv()

    def sent_tokens(copies):
        for copy in copies:
            copy.wait_send()

    saves = []

    def save(source, target):
        copy = pltpu.make_async_copy(source, target, save_sem.at[len(saves)])
        copy.start()
        saves.append(copy)

    normed_copies = token_copies(0, normed.at[rows(0)], normed)
    cot_copies = token_copies(1, cot_own, cot_out)
    mid_copies = token_copies(2, mid.at[rows(0)], mid)
    square_copies = token_copies(3, square_all.at[rows(0)], square_all)
    ends_copy = remote(ends_own, ends_far, small_send.at[0], small_recv.at[0], far_device)


    def load(i, slot):
        return pltpu.make_async_copy(
            part_of(i, 0, features), wide_w.at[slot] if i < 5 else large_w, load_sem.at[i]
        )

    def project(i, slot, keep):
        copy = load(i, slot)
        copy.start()
        copy.wait()

        def body(n, carry):
            at = pl.ds(pl.multiple_of(n * row_len, row_len), row_len)
            keep(at, jnp.dot(normed[at], wide_w[slot], preferred_element_type=F32))
            return carry

        lax.fori_loop(0, 2, body, 0)

    def keep_query(at, total):
        query_pre[at] = total.astype(BF16)
        query[at] = (total * sigmoid(total)).astype(BF16)

    def keep_key(at, total):
        key_pre[at] = total.astype(BF16)
        key[at] = (total * sigmoid(total)).astype(BF16)

    def keep_value(at, total):
        value[at] = total.astype(BF16)

    def keep_gate(at, total):
        gate[at] = total.astype(BF16)

    heads = small // HEAD_DIM
    first_head = (core * 2 + z % 2) * heads

    def attend(row, ends):
        at = pl.ds(row * row_len, row_len)

        def place(dim):
            index = lax.broadcasted_iota(jnp.int32, (row_len, row_len), dim) + core * quarter
            return jnp.where(index >= row_len, index - row_len, index).astype(F32)

        def body(head, carry):
            cols = pl.ds(pl.multiple_of(head * HEAD_DIM, HEAD_DIM), HEAD_DIM)
            scores = lax.dot_general(
                query[at, cols], key[at, cols], (((1,), (1,)), ((), ())), preferred_element_type=F32
            )
            to, source = place(0), place(1)
            allowed = (to >= source) & (to < ends[0:1, :])
            rate = (first_head + head).astype(F32) * (DECAY * HEAD_DIM / features)
            decay = jnp.where(allowed, jnp.exp(-rate * jnp.maximum(to - source, 0.0)), 0.0)
            weights = (scores * decay).astype(BF16)
            probs[row, head] = weights
            mixed[at, cols] = jnp.dot(weights, value[at, cols], preferred_element_type=F32).astype(BF16)
            return carry

        lax.fori_loop(0, heads, body, 0)
        for b in (2 * row, 2 * row + 1):
            m = mixed[rows(b)].astype(F32)
            total = jnp.sum(m * m, axis=1, keepdims=True)
            square[rows(b)] = jnp.broadcast_to(total, (quarter, HEAD_DIM))
            blended[rows(b)] = (gate[rows(b)].astype(F32) * m).astype(BF16)

    def output_part(row, slot):
        at = pl.ds(row * row_len, row_len)

        def body(n, carry):
            cols = pl.ds(pl.multiple_of(n * row_len, row_len), row_len)
            part[at, cols] = lax.dot_general(
                blended[at], wide_w[slot, cols], (((1,), (1,)), ((), ())), preferred_element_type=F32
            ).astype(BF16)
            return carry

        lax.fori_loop(0, features // row_len, body, 0)

    tile = 32

    def tiles(body):
        def step(n, carry):
            body(pl.multiple_of(n * tile, tile))
            return carry

        lax.fori_loop(0, quarter // tile, step, 0)


    start_line(0)
    for i in range(6):
        start_own(i)
    for copy in x_loads:
        copy.wait()

    @tiles
    def _(start):
        here = pl.ds(start, tile)
        values = x_own[here].astype(F32)
        normed[here] = (values * lax.rsqrt(jnp.mean(values * values, axis=1, keepdims=True) + EPS)).astype(BF16)

    start_line(1)
    start_tokens(normed_copies)
    start_line(2)
    total, ends = 0, jnp.zeros(ends_own.shape, jnp.int32)
    places = lax.broadcasted_iota(jnp.int32, ends_own.shape, 1) + core * quarter
    places = jnp.where(places >= row_len, places - row_len, places)
    for c in range(lengths.shape[1]):
        ends = ends + jnp.where(places >= total, lengths[0, c], 0)
        total = total + lengths[0, c]
    ends_own[...] = ends.astype(F32)
    ends_copy.start()
    start_plane(0)
    start_line(3)
    start_plane(1)
    start_line(4)
    pass_tokens(normed_copies)
    forward_plane(0)
    start_plane(2)
    start_line(5)
    forward_plane(1)
    end_tokens(normed_copies)
    save(normed, normed_out)
    complete(0)
    project(0, 0, keep_query)
    save(query_pre, query_pre_out)
    save(query, query_out)
    start_plane(3)
    start_line(6)
    forward_plane(2)
    complete(1)
    project(1, 1, keep_key)
    save(key_pre, key_pre_out)
    save(key, key_out)
    start_plane(4)
    forward_plane(3)
    complete(2)
    project(2, 0, keep_value)
    save(value, value_out)
    forward_plane(4)
    complete(3)
    project(3, 1, keep_gate)
    save(gate, gate_out)
    ends_copy.wait()
    attend(1, ends_far)
    square_near = remote(
        square.at[rows(1)], square_core.at[rows(0)], small_send.at[1], small_recv.at[1], near_device
    )
    square_diag = remote(
        square.at[rows(3)], square_core.at[rows(1)], small_send.at[2], small_recv.at[2], near_device
    )
    square_pair = remote(square.at[rows(2)], square_far, small_send.at[3], small_recv.at[3], far_device)
    square_diag.start()
    start_plane(5)
    attend(0, ends_own)
    save(mixed, mixed_out)
    save(probs, probs_out)
    square_near.start()
    square_diag.wait_recv()
    square[rows(2)] += square_core[rows(1)]
    square_pair.start()
    complete(4)
    copy = load(4, 0)
    copy.start()
    copy.wait()
    output_part(1, 0)
    part_near = remote(part.at[rows(1)], part_core.at[rows(0)], small_send.at[4], small_recv.at[4], near_device)
    part_diag = remote(part.at[rows(3)], part_core.at[rows(1)], small_send.at[5], small_recv.at[5], near_device)
    part_pair = remote(part.at[rows(2)], part_far, small_send.at[6], small_recv.at[6], far_device)
    part_diag.start()
    part_diag.wait_recv()

    @tiles
    def _(start):
        here = pl.ds(start + 2 * quarter, tile)
        part[here] = (part[here].astype(F32) + part_core[pl.ds(start + quarter, tile)].astype(F32)).astype(BF16)

    part_pair.start()
    output_part(0, 0)
    part_near.start()
    forward_plane(5)
    start_plane(6)
    square_near.wait_recv()
    square_pair.wait_recv()
    part_near.wait_recv()
    part_pair.wait_recv()

    @tiles
    def _(start):
        here = pl.ds(start, tile)
        total = part[here].astype(F32) + part_core[here].astype(F32) + part_far[here].astype(F32)
        squares = square[here, 0:1] + square_core[here, 0:1] + square_far[here, 0:1]
        square_all[here] = jnp.broadcast_to(squares, (tile, HEAD_DIM))
        total = x_own[here].astype(F32) + total * lax.rsqrt(squares / features + EPS)
        middle[here] = total
        mid[here] = (total * lax.rsqrt(jnp.mean(total * total, axis=1, keepdims=True) + EPS)).astype(BF16)

    start_tokens(mid_copies)
    start_tokens(square_copies)
    save(middle, middle_out)
    save(ends_own, ends_out.at[pl.ds(0, 8)])
    save(ends_far, ends_out.at[pl.ds(8, 8)])
    complete(5)
    copy = load(5, 0)
    copy.start()
    copy.wait()
    mid_copies[0].wait_recv()

    def left_rows(row):
        at = pl.ds(row * row_len, row_len)
        left[at] = jnp.dot(mid[at], large_w[...], preferred_element_type=F32).astype(BF16)

    left_rows(0)
    pass_tokens(mid_copies)
    start_line(7)
    start_own(6)
    start_own(7)
    for copy in cot_loads:
        copy.wait()
    cot_kept = pltpu.make_async_copy(cot_own, cot_out.at[rows(0)], token_sem.at[2])
    cot_kept.start()
    start_tokens(cot_copies)
    forward_plane(6)
    pass_tokens(square_copies)
    mid_copies[2].wait_recv()
    left_rows(1)
    end_tokens(square_copies)
    save(square_all, square_out)
    save(mid, mid_out)
    save(left, left_out)
    complete(6)
    copy = load(6, 0)
    copy.start()
    copy.wait()

    def right_rows(n, carry):
        at = pl.ds(pl.multiple_of(n * row_len, row_len), row_len)
        total = jnp.dot(mid[at], large_w[...], preferred_element_type=F32)
        right[at] = total.astype(BF16)
        product[at] = (left[at].astype(F32) * total).astype(BF16)
        return carry

    start_plane(7)
    lax.fori_loop(0, 2, right_rows, 0)
    save(right, right_out)
    save(product, product_out)
    pass_tokens(cot_copies)
    forward_plane(7)
    end_tokens(cot_copies)
    cot_kept.wait()
    saves[0].wait()
    sent_tokens(normed_copies)
    copy = pltpu.make_async_copy(cot_out, normed, token_sem.at[0])
    copy.start()
    copy.wait()

    def down_rows(n, carry):
        at = pl.ds(pl.multiple_of(n * row_len, row_len), row_len)
        filled[...] = lax.dot_general(
            normed[:, at], product[...], (((0,), (0,)), ((), ())), preferred_element_type=F32
        ).astype(BF16)
        copy = pltpu.make_async_copy(filled, big_grad.at[0, at], token_sem.at[1])
        copy.start()
        copy.wait()
        return carry

    lax.fori_loop(0, features // row_len, down_rows, 0)
    complete(7)
    for copies in (cot_copies, mid_copies, square_copies):
        sent_tokens(copies)
    for copy in (square_near, square_diag, square_pair, part_near, part_diag, part_pair):
        copy.wait_send()
    for i in range(8):
        for k in (1, 2, 3):
            line_copy(i, k).wait_send()
        for k in range(LINE):
            for copy in first(i, k):
                copy.wait_send()
        for copy in second(i):
            copy.wait_send()
    for copy in saves[1:]:
        copy.wait()


def pieces_of(wide, features):
    size = features // wide
    if size % HEAD_DIM:
        return [(0, 0, features)]
    places = [(w, (w // 16 * 4 + w % 4) * LINE + w // 4 % LINE) for w in range(wide)]
    return [(whole * size, kept * size, size) for whole, kept in places]


def split_refs(refs, counts):
    parts, at = [], 0
    for count in counts:
        parts.append(refs[at : at + count])
        at += count
    return parts


def forward(wide, weights, cot, x, lengths):
    small, large = weights[0].shape[1] // 2, weights[5].shape[1] // 2
    quarter, features = x.shape
    tokens, row_len, heads = 4 * quarter, 2 * quarter, small // HEAD_DIM
    steps = wide.bit_length() - 1
    anywhere = pl.BlockSpec(memory_space=pl.ANY)
    dma = pltpu.SemaphoreType.DMA
    outs = [
        ((features, 2 * small), BF16),
        ((features, 2 * small), BF16),
        ((features, small), BF16),
        ((features, large), BF16),
        ((features, large), BF16),
        ((features, large), BF16),
        ((tokens, features), BF16),
        ((tokens, features), BF16),
        ((tokens, small), BF16),
        ((tokens, small), BF16),
        ((tokens, small), BF16),
        ((tokens, small), BF16),
        ((tokens, small), BF16),
        ((tokens, small), BF16),
        ((tokens, small), BF16),
        ((2, heads, row_len, row_len), BF16),
        ((quarter, features), F32),
        ((tokens, features), BF16),
        ((tokens, large), BF16),
        ((tokens, large), BF16),
        ((tokens, large), BF16),
        ((tokens, HEAD_DIM), F32),
        ((16, row_len), F32),
        ((3, features, large), BF16),
    ]
    held = [
        ((tokens, features), BF16),
        ((2, features, small), BF16),
        ((tokens, small), BF16),
        ((tokens, small), BF16),
        ((tokens, small), BF16),
        ((tokens, small), BF16),
        ((tokens, small), BF16),
        ((tokens, small), BF16),
        ((tokens, small), BF16),
        ((2, heads, row_len, row_len), BF16),
        ((tokens, small), BF16),
        ((tokens, features), BF16),
        ((row_len, features), BF16),
        ((quarter, features), BF16),
        ((tokens, HEAD_DIM), F32),
        ((row_len, HEAD_DIM), F32),
        ((quarter, HEAD_DIM), F32),
        ((tokens, HEAD_DIM), F32),
        ((8, row_len), F32),
        ((tokens, features), BF16),
        ((quarter, features), F32),
        ((features, large), BF16),
        ((tokens, large), BF16),
        ((tokens, large), BF16),
        ((tokens, large), BF16),
        ((quarter, features), BF16),
        ((8, row_len), F32),
        ((row_len, large), BF16),
        ((quarter, features), BF16),
        ((5, features // wide, small), BF16),
        ((3, features // wide, large), BF16),
    ]
    sems = [
        (8, 3), (8, 3), (2, 8), (8, 6 + steps), (8, 6 + steps), (8,), (17,), (3,), (4, 3), (4, 3), (7,), (7,),
        (2, len(pieces_of(wide, features))),
    ]
    return pl.pallas_call(
        functools.partial(forward_kernel, wide, small, large),
        out_shape=[jax.ShapeDtypeStruct(s, t) for s, t in outs],
        in_specs=[anywhere] * 10 + [pl.BlockSpec(memory_space=pltpu.SMEM)],
        out_specs=[anywhere] * len(outs),
        scratch_shapes=[pltpu.VMEM(s, t) for s, t in held] + [dma(s) for s in sems],
        compiler_params=pltpu.CompilerParams(
            has_side_effects=True, collective_id=1, vmem_limit_bytes=60 << 20
        ),
        cost_estimate=pl.CostEstimate(flops=0, bytes_accessed=300 << 20, transcendentals=0),
    )(*weights, cot, x, lengths)


def backward_kernel(wide, small, large, *refs):
    (
        (cot_in, product_in, left_in, right_in, mid_in, middle_in, normed_in, gate_in, mixed_in, query_pre_in,
         key_pre_in, query_in, key_in, value_in, probs_in, square_in, ends_in, output_w, vg_w, qk_w, left_w, right_w,
         down_w, x_in, _),
        (output_out, gate_out, value_out, query_out, key_out, left_out, right_out, down_out, layer_out, input_grad_out,
         grad_middle_out,
         out_own, out_near, out_far, out_source, grad_own, grad_near, grad_far, branch_out, big_grad, big_near, big_far,
         big_line, big_more),
        (held_tokens, normed, weights, gate, mixed, query, key, value, grad_blended, grad_mixed, vg_grad, qk_grad,
         inner, inner_core, inner_sum, inner_far, inner_col, scale, ends, part_core, part_far, out_core, grad_core, own,
         middle, held, near, far, line, stage, added, filled, small_result, big_result),
        (load_sem, send, recv, line_send, line_recv, big_send, big_recv, big_line_send, big_line_recv, small_send,
         small_recv, stage_sem, result_sem, more_send, more_recv, chunk_sem, big_more_send, big_more_recv, piece_sem),
    ) = split_refs(refs, (25, 24, 34, 19))
    branch = held_tokens
    me, core, z, on_line, flip = place_of(wide)
    extra = list(range(4, wide.bit_length() - 1))
    plane_at = (me // 16) * 4 + me % 4
    others = [on_line(k)[0] for k in (1, 2, 3)] + [flip(b) for b in [0, 1] + extra]
    tokens, features = held_tokens.shape
    quarter, row_len = tokens // 4, tokens // 2
    rb = features // wide
    q = LINE * rb
    h = q // 2
    heads = small // HEAD_DIM
    near_device, far_device = (me, 1 - core), (flip(2), core)
    lower = z % 2 == 0
    widths = [min(small, large - at) for at in range(0, large, small)]
    products = [query, key, value]
    lefts = [gate, mixed, grad_blended]
    rights = [grad_mixed, vg_grad.at[:, pl.ds(0, small)], vg_grad.at[:, pl.ds(small, small)]]

    def remote(source, target, send_sem, recv_sem, device):
        return pltpu.make_async_remote_copy(
            src_ref=source, dst_ref=target, send_sem=send_sem, recv_sem=recv_sem,
            device_id=device, device_id_type=pl.DeviceIdType.MESH,
        )

    def block(m):
        return pl.multiple_of((plane_at ^ m) * q, q)

    def rows(b):
        return pl.ds(b * quarter, quarter)

    def loops(count, body):
        def step(n, carry):
            body(n)
            return carry

        lax.fori_loop(0, count, step, 0)

    pending = {}

    def load(name, source, target):
        copy = pltpu.make_async_copy(source, target, load_sem.at[len(pending)])
        copy.start()
        pending[name] = copy

    def load_cut(name, source, targets):
        for n, target in enumerate(targets):
            load(name + str(n), source.at[:, pl.ds(n * small, widths[n])], target.at[:, pl.ds(0, widths[n])])

    def ready(*names):
        for name in names:
            pending[name].wait()

    def ready_cut(name):
        ready(*(name + str(n) for n in range(len(widths))))

    results = []

    def give(source, target):
        copy = pltpu.make_async_copy(source, target, result_sem.at[len(results)])
        copy.start()
        results.append(copy)
        return len(results) - 1

    def given(n):
        if results[n] is not None:
            results[n].wait()
            results[n] = None

    load("cot", cot_in, held_tokens)
    load_cut("product", product_in, products)
    load_cut("down", down_w, [held.at[n] for n in range(3)])
    load_cut("right", right_in, rights)
    load_cut("left", left_in, lefts)
    load("mid", mid_in, normed)
    load("middle", middle_in, middle)
    load("own", cot_in.at[rows(0)], own)
    load("square", square_in, scale)
    load("ends", ends_in, ends)
    for r in range(2):
        for n in range(heads):
            load("probs%d%d" % (r, n), probs_in.at[r, n], held.at[3 + r, pl.ds(n * row_len, row_len)])
    meet([(other, core) for other in others] + [(me, 1 - core)])


    def rows_at(i, start, size):
        return held.at[i, pl.ds(pl.multiple_of(start, min(size, rb)), size)]

    def step(i, j, start, size, target, bit):
        return remote(rows_at(i, start, size), target, send.at[i, j], recv.at[i, j], (flip(bit), core))

    apart = pl.multiple_of((1 - z // 2) * h, h)
    beside = pl.multiple_of(z // 2 * h + (1 - z % 2) * rb, rb)
    at_z = pl.multiple_of(z * rb, rb)

    def copies(i, j):
        if j == 0:
            return step(i, 0, block(3) + apart, h, near.at[i, 0], 1)
        if j == 1:
            return step(i, 1, block(3) + beside, rb, near.at[i, 1, pl.ds(0, rb)], 0)
        if j == 2:
            return step(i, 2, block(1) + beside, rb, far.at[i, 0, pl.ds(beside, rb)], 0)
        if j == 3:
            return step(i, 3, block(2) + apart, h, far.at[i, 1, pl.ds(apart, h)], 1)
        if j == 4:
            return step(i, 4, block(1) + apart, h, far.at[i, 0, pl.ds(apart, h)], 0)
        if j == 5:
            return step(i, 5, block(2) + beside, rb, far.at[i, 1, pl.ds(beside, rb)], 1)
        if j == 6:
            return step(i, 6, block(3) + at_z, rb, near.at[i, 1, pl.ds(rb, rb)], 0)
        if j == 7:
            return step(i, 7, block(1) + at_z, rb, far.at[i, 0, pl.ds(at_z, rb)], 0)
        return step(i, 8, block(2) + at_z, rb, far.at[i, 1, pl.ds(at_z, rb)], 1)

    def line_copy(i, k):
        device, there = on_line(k)
        return remote(
            rows_at(i, block(0) + there * rb, rb), line.at[i, k - 1],
            line_send.at[i, k - 1], line_recv.at[i, k - 1], (device, core),
        )

    tile = min(64, rb)

    def add(target, start, size, *sources):
        def body(n):
            at = pl.ds(pl.multiple_of(start + n * tile, tile), tile)
            total = target[at].astype(F32)
            for source in sources:
                total = total + source[pl.ds(pl.multiple_of(n * tile, tile), tile)].astype(F32)
            target[at] = total.astype(BF16)

        loops(size // tile, body)

    def begin(i, side, other):
        def fill(m):
            held[i, pl.ds(block(m), q)] = lax.dot_general(
                side[:, pl.ds(block(m), q)], other(), (((0,), (0,)), ((), ())), preferred_element_type=F32
            ).astype(BF16)

        if extra:
            loops(wide // LINE, fill)
            for e in reversed(range(len(extra))):
                size = q << (2 + e)
                half = plane_at >> (2 + e)
                copy = remote(
                    rows_at(i, (half ^ 1) * size, size), branch_more(i, e, size),
                    more_send.at[i, e], more_recv.at[i, e], (flip(extra[e]), core),
                )
                copy.start()
                copy.wait()
                add(held.at[i], half * size, size, branch_more(i, e, size))
            for j in range(4):
                copies(i, j).start()
            if i < LATE:
                begin_own(i)
        else:
            fill(3)
            copies(i, 0).start()
            copies(i, 1).start()
            fill(1)
            copies(i, 2).start()
            fill(2)
            copies(i, 3).start()
            if i < LATE:
                begin_own(i)
            fill(0)

    def branch_more(i, e, size):
        return far.at[i, e, pl.ds(0, size)]

    def fold(i):
        copies(i, 0).wait_recv()
        add(held.at[i], block(1) + apart, h, near.at[i, 0])
        copies(i, 4).start()
        copies(i, 1).wait_recv()
        add(held.at[i], block(2) + beside, rb, near.at[i, 1, pl.ds(0, rb)])
        copies(i, 5).start()

    def begin_own(i):
        copies(i, 6).start()
        copies(i, 7).start()

    def fold_own(i):
        copies(i, 6).wait_recv()
        add(held.at[i], block(2) + at_z, rb, near.at[i, 1, pl.ds(rb, rb)])
        copies(i, 8).start()

    def to_line(i):
        for j in range(2, 6):
            copies(i, j).wait_recv()
        for start, size in ((apart, h), (beside, rb)):
            here = pl.ds(start, size)
            add(held.at[i], block(0) + start, size, far.at[i, 0, here], far.at[i, 1, here])
        for k in (1, 2, 3):
            line_copy(i, k).start()

    def finish(i, out):
        for j in (7, 8):
            copies(i, j).wait_recv()
        here = pl.ds(at_z, rb)
        add(held.at[i], block(0) + at_z, rb, far.at[i, 0, here], far.at[i, 1, here])
        for k in (1, 2, 3):
            line_copy(i, k).wait_recv()
        own_sum = held[i, pl.ds(pl.multiple_of(block(0) + at_z, rb), rb)].astype(F32) + line[i, 1].astype(F32)
        other = line[i, 0].astype(F32) + line[i, 2].astype(F32)
        if small_done:
            given(small_done[-1])
        put(small_result, own_sum, other, small)
        small_done.append(give(small_result, out))

    small_done = []

    def put(target, own, other, cols):
        @pl.when(lower)
        def _():
            target[:, pl.ds(0, cols)] = own
            target[:, pl.ds(cols, cols)] = other

        @pl.when(jnp.logical_not(lower))
        def _():
            target[:, pl.ds(0, cols)] = other
            target[:, pl.ds(cols, cols)] = own


    def big_rows(n, start, size):
        return big_grad.at[n, pl.ds(pl.multiple_of(start, min(size, rb)), size)]

    def big_copy(n, j):
        if j == 0:
            source, target = big_rows(n, block(3), h), big_near.at[n, 0]
        elif j == 1:
            source, target = big_rows(n, block(3) + h, h), big_near.at[n, 1]
        elif j == 2:
            source, target = big_rows(n, block(1) + h, h), big_far.at[n, 0, pl.ds(h, h)]
        elif j == 3:
            source, target = big_rows(n, block(2), h), big_far.at[n, 1, pl.ds(0, h)]
        elif j == 4:
            source, target = big_rows(n, block(1), h), big_far.at[n, 0, pl.ds(0, h)]
        else:
            source, target = big_rows(n, block(2) + h, h), big_far.at[n, 1, pl.ds(h, h)]
        bit = (1, 0, 0, 1, 0, 1)[j]
        return remote(source, target, big_send.at[n, j], big_recv.at[n, j], (flip(bit), core))

    def big_line_copy(n, k):
        device, there = on_line(k)
        return remote(
            big_rows(n, block(0) + there * rb, rb), big_line.at[n, k - 1],
            big_line_send.at[n, k - 1], big_line_recv.at[n, k - 1], (device, core),
        )

    def move(j, source, target):
        copy = pltpu.make_async_copy(source, target, stage_sem.at[j])
        copy.start()
        return copy

    def big_add(n, start, *sources):
        moves = [move(0, big_rows(n, start, h), stage.at[pl.ds(0, h)])]
        for j, source in enumerate(sources):
            moves.append(move(1 + j, source, added.at[pl.ds(j * h, h)]))
        for copy in moves:
            copy.wait()
        add(stage, 0, h, *(added.at[pl.ds(j * h, h)] for j in range(len(sources))))
        move(0, stage.at[pl.ds(0, h)], big_rows(n, start, h)).wait()

    def big_begin(n, side=None, parts=None):
        def fill(m):
            if side is None:
                return
            for c, width in enumerate(widths):
                filled[:, pl.ds(c * small, width)] = lax.dot_general(
                    side[:, pl.ds(block(m), q)], parts[c][:, pl.ds(0, width)], (((0,), (0,)), ((), ())),
                    preferred_element_type=F32,
                ).astype(BF16)
            move(3, filled, big_rows(n, block(m), q)).wait()

        if extra:
            loops(wide // LINE, fill)
            for e in reversed(range(len(extra))):
                size = q << (2 + e)
                half = plane_at >> (2 + e)
                copy = remote(
                    big_rows(n, (half ^ 1) * size, size), big_more.at[n, e, pl.ds(0, size)],
                    big_more_send.at[n, e], big_more_recv.at[n, e], (flip(extra[e]), core),
                )
                copy.start()
                copy.wait()
                loops(
                    size // h,
                    lambda i: big_add(
                        n, half * size + i * h, big_more.at[n, e, pl.ds(pl.multiple_of(i * h, h), h)]
                    ),
                )
            for j in range(4):
                big_copy(n, j).start()
        else:
            fill(3)
            big_copy(n, 0).start()
            big_copy(n, 1).start()
            fill(1)
            big_copy(n, 2).start()
            fill(2)
            big_copy(n, 3).start()
            fill(0)

    def big_fold(n):
        big_copy(n, 0).wait_recv()
        big_add(n, block(1), big_near.at[n, 0])
        big_copy(n, 4).start()
        big_copy(n, 1).wait_recv()
        big_add(n, block(2) + h, big_near.at[n, 1])
        big_copy(n, 5).start()

    def big_to_line(n):
        for j in range(2, 6):
            big_copy(n, j).wait_recv()
        for j in range(2):
            here = pl.ds(j * h, h)
            big_add(n, block(0) + j * h, big_far.at[n, 0, here], big_far.at[n, 1, here])
        for k in (1, 2, 3):
            big_line_copy(n, k).start()

    def big_finish(n, out):
        for k in (1, 2, 3):
            big_line_copy(n, k).wait_recv()
        moves = [move(k, big_line.at[n, k], added.at[pl.ds(k * rb, rb)]) for k in range(3)]
        moves.append(move(3, big_rows(n, block(0) + z * rb, rb), added.at[pl.ds(3 * rb, rb)]))
        for copy in moves:
            copy.wait()
        if results_of_big:
            given(results_of_big[-1])
        got = [added[pl.ds(k * rb, rb)].astype(F32) for k in range(4)]
        put(big_result, got[3] + got[1], got[0] + got[2], large)
        results_of_big.append(give(big_result, out))

    results_of_big = []


    def gate_product(r):
        at = pl.ds(r * row_len, row_len)
        for c, width in enumerate(widths):
            here = pl.ds(0, width)
            total = jnp.dot(held_tokens[at], held[c, :, here], preferred_element_type=F32)
            grad_left = (total * rights[c][at, here].astype(F32)).astype(BF16)
            lefts[c][at, here] = (total * lefts[c][at, here].astype(F32)).astype(BF16)
            rights[c][at, here] = grad_left

    chunk = row_len // 2
    chunks = features // chunk
    wide_cols = 2 * small

    def chunk_copies(n, slot):
        source = pl.ds(pl.multiple_of(n * chunk, chunk), chunk)
        target = pl.ds(pl.multiple_of(slot * chunk, chunk), chunk)
        return [
            pltpu.make_async_copy(
                w.at[source, pl.ds(at, cols)], weights.at[2 * i + j, target, pl.ds(0, cols)], chunk_sem.at[slot, 2 * i + j]
            )
            for i, w in enumerate((left_w, right_w))
            for j, (at, cols) in enumerate(((0, wide_cols), (wide_cols, large - wide_cols)))
        ]

    def mid_part(r):
        at = pl.ds(r * row_len, row_len)
        for copy in chunk_copies(0, 0):
            copy.start()

        def body(n):
            slot = n % 2

            @pl.when(n + 1 < chunks)
            def _():
                for copy in chunk_copies(n + 1, 1 - slot):
                    copy.start()

            for copy in chunk_copies(n, slot):
                copy.wait()
            here = pl.ds(pl.multiple_of(slot * chunk, chunk), chunk)
            total = jnp.zeros((row_len, chunk), F32)
            for i, parts in enumerate((rights, lefts)):
                for c, width in enumerate(widths):
                    w = weights[2 * i + c // 2, here, pl.ds((c % 2) * small, width)]
                    total = total + lax.dot_general(
                        parts[c][at, pl.ds(0, width)], w, (((1,), (1,)), ((), ())), preferred_element_type=F32
                    )
            held_tokens[at, pl.ds(pl.multiple_of(n * chunk, chunk), chunk)] = total.astype(BF16)

        loops(chunks, body)

    def output_part(r):
        at = pl.ds(r * row_len, row_len)

        def body(n):
            here = pl.ds(pl.multiple_of(n * row_len, row_len), row_len)
            total = jnp.zeros((row_len, row_len), F32)
            for c, width in enumerate(widths):
                total = total + lax.dot_general(
                    products[c][at, pl.ds(0, width)], held[c, here, pl.ds(0, width)], (((1,), (1,)), ((), ())),
                    preferred_element_type=F32,
                )
            held_tokens[at, here] = total.astype(BF16)

        loops(features // row_len, body)

    def middle_rows(n):
        at = pl.ds(pl.multiple_of(n * 32, 32), 32)
        grad = held_tokens[at].astype(F32) + part_core[at].astype(F32) + part_far[at].astype(F32)
        values = middle[at]
        s = lax.rsqrt(jnp.mean(values * values, axis=1, keepdims=True) + EPS)
        grad = own[at].astype(F32) + norm_back(values, s, grad)
        middle[at] = grad
        own[at] = grad.astype(BF16)


    def grad_rows(row):
        at = pl.ds(row * row_len, row_len)
        total = jnp.zeros((row_len, small), F32)
        for n in range(4):
            total = total + jnp.dot(
                branch[at, pl.ds(n * row_len, row_len)], weights[n, :, pl.ds(0, small)], preferred_element_type=F32
            )
        grad_blended[at] = total.astype(BF16)
        m = mixed[at].astype(F32)
        g = gate[at].astype(F32)
        scaled = m * scale[at, 0:1]
        vg_grad[at, pl.ds(small, small)] = (total * scaled).astype(BF16)
        grad_mixed[at] = (g * scaled).astype(BF16)
        inner[:, at] = lax.dot_general(
            jnp.ones((8, small), F32), total * g * m, (((1,), (1,)), ((), ())),
            preferred_element_type=F32, precision=lax.Precision.HIGHEST,
        )

    def scale_rows(n):
        at = pl.ds(pl.multiple_of(n * 128, 128), 128)
        scale[at] = lax.rsqrt(scale[at] / features + EPS)

    def mix_rows(n):
        at = pl.ds(pl.multiple_of(n * 128, 128), 128)
        s = scale[at, 0:1]
        value_of = s * (grad_blended[at].astype(F32) * gate[at].astype(F32))
        value_of = value_of - mixed[at].astype(F32) * (s * s * s * (inner_col[at, 0:1] / features))
        grad_mixed[at] = value_of.astype(BF16)

    first_head = (core * 2 + z % 2) * heads

    def attend_back(row):
        at = pl.ds(row * row_len, row_len)

        def place(dim):
            index = lax.broadcasted_iota(jnp.int32, (row_len, row_len), dim) + core * quarter
            return jnp.where(index >= row_len, index - row_len, index).astype(F32)

        def slope(pre):
            s = sigmoid(pre)
            return s * (1.0 + pre * (1.0 - s))

        def body(head):
            cols = pl.ds(pl.multiple_of(head * HEAD_DIM, HEAD_DIM), HEAD_DIM)
            more = pl.ds(pl.multiple_of(small + head * HEAD_DIM, HEAD_DIM), HEAD_DIM)
            got = grad_mixed[at, cols]
            grad_probs = lax.dot_general(
                got, value[at, cols], (((1,), (1,)), ((), ())), preferred_element_type=F32
            )
            to, source = place(0), place(1)
            allowed = (to >= source) & (to < ends[pl.ds(8 * row, 1), :])
            rate = (first_head + head).astype(F32) * (DECAY * HEAD_DIM / features)
            decay = jnp.where(allowed, jnp.exp(-rate * jnp.maximum(to - source, 0.0)), 0.0)
            grad_scores = (grad_probs * decay).astype(BF16)
            probs = held[3 + row, pl.ds(pl.multiple_of(head * row_len, row_len), row_len)]
            vg_grad[at, cols] = lax.dot_general(
                probs, got, (((0,), (0,)), ((), ())), preferred_element_type=F32
            ).astype(BF16)
            grad_query = jnp.dot(grad_scores, key[at, cols], preferred_element_type=F32)
            qk_grad[at, cols] = (grad_query * slope(gate[at, cols].astype(F32))).astype(BF16)
            grad_key = lax.dot_general(
                grad_scores, query[at, cols], (((0,), (0,)), ((), ())), preferred_element_type=F32
            )
            qk_grad[at, more] = (grad_key * slope(mixed[at, cols].astype(F32))).astype(BF16)

        loops(heads, body)

    def load_weights(pair):
        for n in range(2):
            here = pl.ds((2 * pair + n) * row_len, row_len)
            load("vg%d%d" % (pair, n), vg_w.at[here], weights.at[n])
            load("qk%d%d" % (pair, n), qk_w.at[here], weights.at[2 + n])

    def normed_part(pair, row):
        at = pl.ds(row * row_len, row_len)
        for n in range(2):
            total = lax.dot_general(vg_grad[at], weights[n], (((1,), (1,)), ((), ())), preferred_element_type=F32)
            total = total + lax.dot_general(
                qk_grad[at], weights[2 + n], (((1,), (1,)), ((), ())), preferred_element_type=F32
            )
            branch[at, pl.ds((2 * pair + n) * row_len, row_len)] = total.astype(BF16)

    def small_copy(n, source, target, device):
        return remote(source, target, small_send.at[n], small_recv.at[n], device)

    pieces = pieces_of(wide, features)

    def layer_rows(n):
        at = pl.ds(pl.multiple_of(n * 32, 32), 32)
        total = middle[at] + own[at].astype(F32) + part_core[at].astype(F32) + part_far[at].astype(F32)
        own[at] = total.astype(BF16)

    def input_rows(n):
        at = pl.ds(pl.multiple_of(n * 32, 32), 32)
        grad = own[at].astype(F32) + part_core[at].astype(F32) + part_far[at].astype(F32)
        values = part_core[pl.ds(pl.multiple_of(quarter + n * 32, 32), 32)].astype(F32)
        s = lax.rsqrt(jnp.mean(values * values, axis=1, keepdims=True) + EPS)
        middle[at] = middle[at] + norm_back(values, s, grad)

    def put_pieces(row, source, target):
        copies = [
            pltpu.make_async_copy(source.at[:, pl.ds(b, size)], target.at[:, pl.ds(a, size)], piece_sem.at[row, n])
            for n, (a, b, size) in enumerate(pieces)
        ]
        for copy in copies:
            copy.start()
        return copies


    big_begin(0)
    ready("cot")
    ready_cut("product")
    ready_cut("down")
    ready_cut("left")
    ready_cut("right")
    gate_product(1)
    gate_product(0)
    mid_part(1)
    part_diag = small_copy(0, held_tokens.at[rows(3)], part_core.at[rows(1)], near_device)
    part_near = small_copy(1, held_tokens.at[rows(1)], part_core.at[rows(0)], near_device)
    part_pair = small_copy(2, held_tokens.at[rows(2)], part_far, far_device)
    part_diag.start()
    part_diag.wait_recv()
    add(held_tokens, 2 * quarter, quarter, part_core.at[rows(1)])
    part_pair.start()
    big_fold(0)
    mid_part(0)
    part_near.start()
    ready("mid")
    big_begin(1, normed, rights)
    ready("middle", "own")
    part_near.wait_recv()
    part_pair.wait_recv()
    loops(quarter // 32, middle_rows)
    branch_own = move(4, own, branch_out.at[rows(0)])
    branch_near = small_copy(3, own, branch_out.at[rows(1)], near_device)
    branch_far = small_copy(4, own, branch_out.at[rows(2)], far_device)
    branch_pass = small_copy(5, branch_out.at[rows(2)], branch_out.at[rows(3)], near_device)
    branch_far.start()
    branch_near.start()
    middle_given = give(middle, grad_middle_out)
    for n in range(4):
        load("output%d" % n, output_w.at[pl.ds(n * row_len, row_len)], weights.at[n, :, pl.ds(0, small)])
    big_to_line(0)
    big_begin(2, normed, lefts)
    load("gate", gate_in, gate)
    load("mixed", mixed_in, mixed)
    load("normed", normed_in, normed)
    big_fold(1)
    for copy in (part_diag, part_near, part_pair):
        copy.wait_send()
    output_part(1)
    out_diag = small_copy(6, held_tokens.at[rows(3)], out_core, near_device)
    out_diag.start()
    output_part(0)
    out_next = small_copy(7, held_tokens.at[rows(1)], out_near, near_device)
    out_next.start()
    out_mine = move(5, held_tokens.at[rows(0)], out_own)
    out_diag.wait_recv()
    add(held_tokens, 2 * quarter, quarter, out_core)
    out_pair = small_copy(8, out_source, out_far, far_device)
    move(0, held_tokens.at[rows(2)], out_source).wait()
    out_pair.start()
    load("value", value_in, value)
    load("query", query_in, query)
    load("key", key_in, key)
    out_mine.wait()
    out_next.wait_send()
    out_diag.wait_send()
    branch_own.wait()
    branch_near.wait_recv()
    load("branch0", branch_out.at[pl.ds(0, row_len)], branch.at[pl.ds(0, row_len)])
    ready("square")
    loops(tokens // 128, scale_rows)
    branch_far.wait_recv()
    branch_pass.start()
    ready("branch0", "output0", "output1", "output2", "output3", "gate", "mixed")
    grad_rows(0)
    branch_pass.wait_recv()
    load("branch1", branch_out.at[pl.ds(row_len, row_len)], branch.at[pl.ds(row_len, row_len)])
    ready("branch1")
    grad_rows(1)
    core_copy = small_copy(9, inner, inner_core, near_device)
    core_copy.start()
    core_copy.wait_recv()
    for b in range(4):
        inner_sum[:, rows(b)] = inner[:, rows(b)] + inner_core[:, rows(b ^ 1)]
    far_copy = small_copy(10, inner_sum, inner_far, far_device)
    far_copy.start()
    begin(0, branch, lambda: grad_mixed[...])
    far_copy.wait_recv()
    for b in range(4):
        total = inner_sum[:, rows(b)] + inner_far[:, rows(b ^ 2)]
        inner_col[rows(b)] = jnp.broadcast_to(total.T[:, 0:1], (quarter, HEAD_DIM))
    loops(tokens // 128, mix_rows)
    load("query_pre", query_pre_in, gate)
    load("key_pre", key_pre_in, mixed)
    load_weights(0)
    ready("normed")
    begin(1, normed, lambda: vg_grad[:, pl.ds(small, small)])
    big_to_line(1)
    big_fold(2)
    ready("value", "query", "key", "query_pre", "key_pre", "ends")
    for r in range(2):
        ready(*("probs%d%d" % (r, n) for n in range(heads)))
    attend_back(1)
    fold(0)
    fold_own(0)
    attend_back(0)
    begin(2, normed, lambda: vg_grad[:, pl.ds(0, small)])
    fold(1)
    fold_own(1)
    begin(3, normed, lambda: qk_grad[:, pl.ds(0, small)])
    begin(4, normed, lambda: qk_grad[:, pl.ds(small, small)])
    big_to_line(2)
    to_line(0)
    fold(2)
    ready("vg00", "vg01", "qk00", "qk01")
    normed_part(0, 1)
    normed_part(0, 0)
    load_weights(1)
    big_finish(0, down_out)
    to_line(1)
    ready("vg10", "vg11", "qk10", "qk11")
    normed_part(1, 1)
    grad_diag = small_copy(11, branch.at[rows(3)], grad_core, near_device)
    grad_next = small_copy(12, branch.at[rows(1)], grad_near, near_device)
    grad_pair = small_copy(13, branch.at[rows(2)], grad_far, far_device)
    grad_diag.start()
    normed_part(1, 0)
    grad_next.start()
    grad_given = give(branch.at[rows(0)], grad_own)
    grad_diag.wait_recv()
    add(branch, 2 * quarter, quarter, grad_core)
    grad_pair.start()
    fold(3)
    fold(4)
    for i in range(LATE, 5):
        begin_own(i)
    big_finish(1, left_out)
    given(middle_given)
    branch_near.wait_send()
    branch_far.wait_send()
    out_next.wait_recv()
    out_pair.wait_recv()
    load("middle2", middle_in, middle)
    load("out_own", out_own, own)
    load("out_near", out_near, part_core.at[rows(0)])
    load("out_far", out_far, part_far)
    to_line(2)
    ready("middle2", "out_own", "out_near", "out_far")
    loops(quarter // 32, layer_rows)
    layer_pieces = put_pieces(0, own, layer_out)
    load("middle3", grad_middle_out, middle)
    x_copies = [
        pltpu.make_async_copy(x_in.at[:, pl.ds(a, size)], part_core.at[rows(1), pl.ds(b, size)], piece_sem.at[1, n])
        for n, (a, b, size) in enumerate(pieces)
    ]
    for copy in x_copies:
        copy.start()
    finish(0, output_out)
    finish(1, gate_out)
    to_line(3)
    fold_own(2)
    big_finish(2, right_out)
    to_line(4)
    fold_own(3)
    fold_own(4)
    for copy in layer_pieces:
        copy.wait()
    given(grad_given)
    grad_next.wait_recv()
    grad_pair.wait_recv()
    load("grad_own", grad_own, own)
    load("grad_near", grad_near, part_core.at[rows(0)])
    load("grad_far", grad_far, part_far)
    for copy in x_copies:
        copy.wait()
    ready("middle3", "grad_own", "grad_near", "grad_far")
    loops(quarter // 32, input_rows)
    grad_pieces = put_pieces(2, middle, input_grad_out)
    finish(2, value_out)
    finish(3, query_out)
    finish(4, key_out)
    for copy in grad_pieces:
        copy.wait()
    for copy in (branch_pass, out_pair, core_copy, far_copy, grad_diag, grad_next, grad_pair):
        copy.wait_send()
    for i in range(5):
        for j in range(9):
            copies(i, j).wait_send()
        for k in (1, 2, 3):
            line_copy(i, k).wait_send()
    for n in range(3):
        for j in range(6):
            big_copy(n, j).wait_send()
        for k in (1, 2, 3):
            big_line_copy(n, k).wait_send()
    for n in range(len(results)):
        given(n)


def backward(wide, arrays, small, large):
    tokens, features = arrays[0].shape
    quarter, row_len = tokens // 4, tokens // 2
    rb = features // wide
    q = LINE * rb
    extra = max(1, wide.bit_length() - 5)
    anywhere = pl.BlockSpec(memory_space=pl.ANY)
    dma = pltpu.SemaphoreType.DMA
    many = features // 2 if wide > 16 else 16
    far_rows = max(q, many)
    part = (quarter, features)
    outs = [((rb, 2 * small), F32)] * 5 + [((rb, 2 * large), F32)] * 3 + [
        (part, BF16),
        (part, F32),
        (part, F32),
        *[(part, BF16)] * 7,

        ((tokens, features), BF16),
        ((3, features, large), BF16),
        ((3, 2, q // 2, large), BF16),
        ((3, 2, q, large), BF16),
        ((3, 3, rb, large), BF16),
        ((3, extra, many, large), BF16),
    ]
    held = [
        ((tokens, features), BF16),
        ((tokens, features), BF16),
        ((4, row_len, 2 * small), BF16),
        *[((tokens, small), BF16)] * 7,
        ((tokens, 2 * small), BF16),
        ((tokens, 2 * small), BF16),
        *[((8, tokens), F32)] * 4,
        ((tokens, HEAD_DIM), F32),
        ((tokens, HEAD_DIM), F32),
        ((16, row_len), F32),
        ((row_len, features), BF16),
        *[(part, BF16)] * 4,
        (part, F32),
        ((5, features, small), BF16),
        ((5, 2, q // 2, small), BF16),
        ((5, 2, far_rows, small), BF16),
        ((5, 3, rb, small), BF16),
        ((q // 2, large), BF16),
        ((q, large), BF16),
        ((q, large), BF16),
        ((rb, 2 * small), F32),
        ((rb, 2 * large), F32),
    ]
    sems = [
        (60,), (5, 9), (5, 9), (5, 3), (5, 3), (3, 6), (3, 6), (3, 3), (3, 3), (14,), (14,), (6,), (10,), (5, extra),
        (5, extra), (2, 4), (3, extra), (3, extra), (3, len(pieces_of(wide, features))),
    ]
    return pl.pallas_call(
        functools.partial(backward_kernel, wide, small, large),
        out_shape=[jax.ShapeDtypeStruct(s, t) for s, t in outs],
        in_specs=[anywhere] * len(arrays),
        out_specs=[anywhere] * len(outs),
        scratch_shapes=[pltpu.VMEM(s, t) for s, t in held] + [dma(s) for s in sems],
        input_output_aliases={24: 19},
        compiler_params=pltpu.CompilerParams(
            has_side_effects=True, collective_id=2, vmem_limit_bytes=60 << 20
        ),
        cost_estimate=pl.CostEstimate(flops=0, bytes_accessed=300 << 20, transcendentals=0),
    )(*arrays)


def sigmoid(z):
    return 1.0 / (1.0 + jnp.exp(-z))


def on_device(
    layer_input, doc_lengths, w_query, w_key, w_value, w_gate, w_output, w_left, w_right, w_down, cotangent, *, wide
):
    features = layer_input.shape[1]
    cut = len(pieces_of(wide, features)) == 1
    x = to_kept(layer_input, wide) if cut else layer_input
    cot = to_kept(cotangent, wide) if cut else cotangent
    weights = [w_query, w_key, w_value, w_gate, w_output, w_left, w_right, w_down]
    (
        qk_w, vg_w, output_w, left_w, right_w, down_w, normed, cot_all, query_pre, key_pre, gate, queries, keys, values,
        mixed, probs, middle, mid, left, right, product, squares, ends, big_grad,
    ) = forward(wide, weights, cot, x, doc_lengths)
    (
        grad_output, grad_gate, grad_value, grad_query, grad_key, grad_left, grad_right, grad_down, layer_output,
        input_grad, *_
    ) = backward(
        wide,
        [
            cot_all, product, left, right, mid, middle, normed, gate, mixed, query_pre, key_pre, queries, keys, values,
            probs, squares, ends, output_w, vg_w, qk_w, left_w, right_w, down_w, x, big_grad,
        ],
        queries.shape[1],
        left.shape[1],
    )
    if cut:
        layer_output, input_grad = from_kept(layer_output, wide), from_kept(input_grad, wide)
    return (
        layer_output,
        input_grad,
        grad_query,
        grad_key,
        grad_value,
        grad_gate,
        grad_output,
        grad_left,
        grad_right,
        grad_down,
    )


def solution(mesh):
    both, weight = P(("wide", "narrow"), None), P("wide", "narrow")
    wide = mesh.shape["wide"]

    def body(*args):
        return on_device(*args, wide=wide)

    return jax.shard_map(
        body,
        mesh=mesh,
        in_specs=(both, P("wide", None)) + (weight,) * 8 + (both,),
        out_specs=(both, both) + (weight,) * 8,
        check_vma=False,
    )
```

```python
import functools

import jax
import jax.numpy as jnp
from jax import lax
from jax.experimental import pallas as pl
from jax.experimental.pallas import tpu as pltpu
from jax.sharding import PartitionSpec as P

HEAD_DIM = 128
LINE = 4
LATE = 2
EPS = 1e-06
DECAY = 2.0
F32 = jnp.float32
BF16 = jnp.bfloat16


def norm_back(values, scale, gradient):
    inner = jnp.mean(gradient * values, axis=-1, keepdims=True)
    return scale * gradient - values * (scale * scale * scale) * inner


def to_kept(value, wide):
    tokens, cols = value.shape
    value = value.reshape(tokens, wide // 16, LINE, 4, cols // wide)
    return value.transpose(0, 1, 3, 2, 4).reshape(tokens, cols)


def from_kept(value, wide):
    tokens, cols = value.shape
    value = value.reshape(tokens, wide // 16, 4, LINE, cols // wide)
    return value.transpose(0, 1, 3, 2, 4).reshape(tokens, cols)


def place_of(wide):
    me = lax.axis_index("wide")
    z = (me // 4) % LINE

    def on_line(k):
        there = (z + k) % LINE
        return me + (there - z) * 4, there

    def flip(bit):
        return me + (1 - 2 * ((me >> bit) & 1)) * (1 << bit)

    return me, lax.axis_index("narrow"), z, on_line, flip


def meet(devices):
    barrier = pltpu.get_barrier_semaphore()
    for device in devices:
        pl.semaphore_signal(
            barrier, inc=1, device_id=device, device_id_type=pl.DeviceIdType.MESH
        )
    pl.semaphore_wait(barrier, len(devices))


def forward_kernel(wide, small, large, *refs):
    (
        w_in, (cot_in, x_in, lengths),
        w_out, (normed_out, cot_out, query_pre_out, key_pre_out, gate_out, query_out, key_out, value_out, mixed_out,
                probs_out, middle_out, mid_out, left_out, right_out, product_out, square_out, ends_out, big_grad),
        (normed, wide_w, query_pre, key_pre, gate, query, key, value, mixed, probs, blended, part, part_core, part_far,
         square, square_core, square_far, square_all, ends_far, mid, middle, large_w, left, right, product, x_own, ends_own,
         filled, cot_own, small_own, large_own),
        (line_send, line_recv, own_sem, plane_send, plane_recv, load_sem, save_sem, token_sem, token_send, token_recv,
         small_send, small_recv, piece_sem),
    ) = split_refs(refs, (8, 3, 6, 18, 31, 13))
    me, core, z, on_line, flip = place_of(wide)
    extra = list(range(4, wide.bit_length() - 1))
    plane_at = (me // 16) * 4 + me % 4
    others = [on_line(k)[0] for k in (1, 2, 3)] + [flip(b) for b in [0, 1] + extra]
    quarter, features = x_own.shape
    pieces = pieces_of(wide, features)
    x_loads = [
        pltpu.make_async_copy(x_in.at[:, pl.ds(a, size)], x_own.at[:, pl.ds(b, size)], piece_sem.at[0, n])
        for n, (a, b, size) in enumerate(pieces)
    ]
    cot_loads = [
        pltpu.make_async_copy(cot_in.at[:, pl.ds(a, size)], cot_own.at[:, pl.ds(b, size)], piece_sem.at[1, n])
        for n, (a, b, size) in enumerate(pieces)
    ]
    for copy in x_loads + cot_loads:
        copy.start()
    meet([(other, core) for other in others] + [(me, 1 - core)])
    rb = w_in[0].shape[0]
    q = LINE * rb
    h = q // 2
    row_len = 2 * quarter
    chunks = [(0, 0), (0, small), (1, 0), (1, small), (2, 0), (3, 0), (4, 0), (5, 0)]
    near_device, far_device = (me, 1 - core), (flip(2), core)


    def part_of(i, start, size):
        out, col = chunks[i]
        cols = w_in[i].shape[1] // 2
        return w_out[out].at[pl.ds(pl.multiple_of(start, min(size, rb)), size), pl.ds(col, cols)]

    def block(m):
        return (plane_at ^ m) * q

    def remote(source, target, send_sem, recv_sem, device):
        return pltpu.make_async_remote_copy(
            src_ref=source, dst_ref=target, send_sem=send_sem, recv_sem=recv_sem,
            device_id=device, device_id_type=pl.DeviceIdType.MESH,
        )

    def mine(i, there):
        cols = w_in[i].shape[1] // 2
        return w_in[i].at[:, pl.ds(pl.multiple_of((there % 2) * cols, HEAD_DIM), cols)]

    def line_copy(i, k):
        device, there = on_line(k)
        return remote(
            mine(i, there), part_of(i, block(0) + z * rb, rb),
            line_send.at[i, k - 1], line_recv.at[i, k - 1], (device, core),
        )

    def own_held(i):
        return small_own.at[i] if i < 5 else large_own.at[i - 5]

    def own_load(i):
        return pltpu.make_async_copy(mine(i, z), own_held(i), own_sem.at[0, i])

    def own_store(i):
        return pltpu.make_async_copy(own_held(i), part_of(i, block(0) + z * rb, rb), own_sem.at[1, i])

    def plane(i, j, start, size, bit):
        place = part_of(i, start, size)
        return remote(place, place, plane_send.at[i, j], plane_recv.at[i, j], (flip(bit), core))

    def first(i, k):
        target = part_of(i, block(0) + ((z - k) % LINE) * rb, rb)
        source = target if k else mine(i, z)
        return [
            remote(source, target, plane_send.at[i, 4 * b + k], plane_recv.at[i, 4 * b + k], (flip(b), core))
            for b in (0, 1)
        ]

    def second(i):
        return plane(i, 8, block(1), h, 1), plane(i, 9, block(2) + h, h, 0)

    def start_line(i):
        own_load(i).start()
        for k in (1, 2, 3):
            line_copy(i, k).start()

    def start_own(i):
        for copy in first(i, 0):
            copy.start()

    def start_plane(i):
        own_load(i).wait()
        own_store(i).start()
        for k in (1, 2, 3):
            line_copy(i, k).wait_recv()
            for copy in first(i, k):
                copy.start()

    def forward_plane(i):
        for b, onward in enumerate(second(i)):
            for k in range(LINE):
                first(i, k)[b].wait_recv()
            onward.start()

    def complete(i):
        own_store(i).wait()
        for copy in second(i):
            copy.wait_recv()
        for e, bit in enumerate(extra):
            size = q << (2 + e)
            copy = plane(i, 10 + e, (plane_at >> (2 + e)) * size, size, bit)
            copy.start()
            copy.wait()


    def rows(b):
        return pl.ds(b * quarter, quarter)

    def token_copies(n, source, out):
        send = lambda j, source, device: remote(
            source, out.at[rows(j + 1)], token_send.at[n, j], token_recv.at[n, j], device
        )
        return send(0, source, near_device), send(1, source, far_device), send(2, out.at[rows(2)], near_device)

    def start_tokens(copies):
        copies[0].start()
        copies[1].start()

    def pass_tokens(copies):
        copies[1].wait_recv()
        copies[2].start()

    def end_tokens(copies):
        copies[0].wait_recv()
        copies[2].wait_recv()

    def sent_tokens(copies):
        for copy in copies:
            copy.wait_send()

    saves = []

    def save(source, target):
        copy = pltpu.make_async_copy(source, target, save_sem.at[len(saves)])
        copy.start()
        saves.append(copy)

    normed_copies = token_copies(0, normed.at[rows(0)], normed)
    cot_copies = token_copies(1, cot_own, cot_out)
    mid_copies = token_copies(2, mid.at[rows(0)], mid)
    square_copies = token_copies(3, square_all.at[rows(0)], square_all)
    ends_copy = remote(ends_own, ends_far, small_send.at[0], small_recv.at[0], far_device)


    def load(i, slot):
        return pltpu.make_async_copy(
            part_of(i, 0, features), wide_w.at[slot] if i < 5 else large_w, load_sem.at[i]
        )

    def project(i, slot, keep):
        copy = load(i, slot)
        copy.start()
        copy.wait()

        def body(n, carry):
            at = pl.ds(pl.multiple_of(n * row_len, row_len), row_len)
            keep(at, jnp.dot(normed[at], wide_w[slot], preferred_element_type=F32))
            return carry

        lax.fori_loop(0, 2, body, 0)

    def keep_query(at, total):
        query_pre[at] = total.astype(BF16)
        query[at] = (total * sigmoid(total)).astype(BF16)

    def keep_key(at, total):
        key_pre[at] = total.astype(BF16)
        key[at] = (total * sigmoid(total)).astype(BF16)

    def keep_value(at, total):
        value[at] = total.astype(BF16)

    def keep_gate(at, total):
        gate[at] = total.astype(BF16)

    heads = small // HEAD_DIM
    first_head = (core * 2 + z % 2) * heads

    def attend(row, ends):
        at = pl.ds(row * row_len, row_len)

        def place(dim):
            index = lax.broadcasted_iota(jnp.int32, (row_len, row_len), dim) + core * quarter
            return jnp.where(index >= row_len, index - row_len, index).astype(F32)

        def body(head, carry):
            cols = pl.ds(pl.multiple_of(head * HEAD_DIM, HEAD_DIM), HEAD_DIM)
            scores = lax.dot_general(
                query[at, cols], key[at, cols], (((1,), (1,)), ((), ())), preferred_element_type=F32
            )
            to, source = place(0), place(1)
            allowed = (to >= source) & (to < ends[0:1, :])
            rate = (first_head + head).astype(F32) * (DECAY * HEAD_DIM / features)
            decay = jnp.where(allowed, jnp.exp(-rate * jnp.maximum(to - source, 0.0)), 0.0)
            weights = (scores * decay).astype(BF16)
            probs[row, head] = weights
            mixed[at, cols] = jnp.dot(weights, value[at, cols], preferred_element_type=F32).astype(BF16)
            return carry

        lax.fori_loop(0, heads, body, 0)
        for b in (2 * row, 2 * row + 1):
            m = mixed[rows(b)].astype(F32)
            total = jnp.sum(m * m, axis=1, keepdims=True)
            square[rows(b)] = jnp.broadcast_to(total, (quarter, HEAD_DIM))
            blended[rows(b)] = (gate[rows(b)].astype(F32) * m).astype(BF16)

    def output_part(row, slot):
        at = pl.ds(row * row_len, row_len)

        def body(n, carry):
            cols = pl.ds(pl.multiple_of(n * row_len, row_len), row_len)
            part[at, cols] = lax.dot_general(
                blended[at], wide_w[slot, cols], (((1,), (1,)), ((), ())), preferred_element_type=F32
            ).astype(BF16)
            return carry

        lax.fori_loop(0, features // row_len, body, 0)

    tile = 32

    def tiles(body):
        def step(n, carry):
            body(pl.multiple_of(n * tile, tile))
            return carry

        lax.fori_loop(0, quarter // tile, step, 0)


    start_line(0)
    for i in range(6):
        start_own(i)
    for copy in x_loads:
        copy.wait()

    @tiles
    def _(start):
        here = pl.ds(start, tile)
        values = x_own[here].astype(F32)
        normed[here] = (values * lax.rsqrt(jnp.mean(values * values, axis=1, keepdims=True) + EPS)).astype(BF16)

    start_line(1)
    start_tokens(normed_copies)
    start_line(2)
    total, ends = 0, jnp.zeros(ends_own.shape, jnp.int32)
    places = lax.broadcasted_iota(jnp.int32, ends_own.shape, 1) + core * quarter
    places = jnp.where(places >= row_len, places - row_len, places)
    for c in range(lengths.shape[1]):
        ends = ends + jnp.where(places >= total, lengths[0, c], 0)
        total = total + lengths[0, c]
    ends_own[...] = ends.astype(F32)
    ends_copy.start()
    start_plane(0)
    start_line(3)
    start_plane(1)
    start_line(4)
    pass_tokens(normed_copies)
    forward_plane(0)
    start_plane(2)
    start_line(5)
    forward_plane(1)
    end_tokens(normed_copies)
    save(normed, normed_out)
    complete(0)
    project(0, 0, keep_query)
    save(query_pre, query_pre_out)
    save(query, query_out)
    start_plane(3)
    start_line(6)
    forward_plane(2)
    complete(1)
    project(1, 1, keep_key)
    save(key_pre, key_pre_out)
    save(key, key_out)
    start_plane(4)
    forward_plane(3)
    complete(2)
    project(2, 0, keep_value)
    save(value, value_out)
    forward_plane(4)
    complete(3)
    project(3, 1, keep_gate)
    save(gate, gate_out)
    ends_copy.wait()
    attend(1, ends_far)
    square_near = remote(
        square.at[rows(1)], square_core.at[rows(0)], small_send.at[1], small_recv.at[1], near_device
    )
    square_diag = remote(
        square.at[rows(3)], square_core.at[rows(1)], small_send.at[2], small_recv.at[2], near_device
    )
    square_pair = remote(square.at[rows(2)], square_far, small_send.at[3], small_recv.at[3], far_device)
    square_diag.start()
    start_plane(5)
    attend(0, ends_own)
    save(mixed, mixed_out)
    save(probs, probs_out)
    square_near.start()
    square_diag.wait_recv()
    square[rows(2)] += square_core[rows(1)]
    square_pair.start()
    complete(4)
    copy = load(4, 0)
    copy.start()
    copy.wait()
    output_part(1, 0)
    part_near = remote(part.at[rows(1)], part_core.at[rows(0)], small_send.at[4], small_recv.at[4], near_device)
    part_diag = remote(part.at[rows(3)], part_core.at[rows(1)], small_send.at[5], small_recv.at[5], near_device)
    part_pair = remote(part.at[rows(2)], part_far, small_send.at[6], small_recv.at[6], far_device)
    part_diag.start()
    part_diag.wait_recv()

    @tiles
    def _(start):
        here = pl.ds(start + 2 * quarter, tile)
        part[here] = (part[here].astype(F32) + part_core[pl.ds(start + quarter, tile)].astype(F32)).astype(BF16)

    part_pair.start()
    output_part(0, 0)
    part_near.start()
    forward_plane(5)
    start_plane(6)
    square_near.wait_recv()
    square_pair.wait_recv()
    part_near.wait_recv()
    part_pair.wait_recv()

    @tiles
    def _(start):
        here = pl.ds(start, tile)
        total = part[here].astype(F32) + part_core[here].astype(F32) + part_far[here].astype(F32)
        squares = square[here, 0:1] + square_core[here, 0:1] + square_far[here, 0:1]
        square_all[here] = jnp.broadcast_to(squares, (tile, HEAD_DIM))
        total = x_own[here].astype(F32) + total * lax.rsqrt(squares / features + EPS)
        middle[here] = total
        mid[here] = (total * lax.rsqrt(jnp.mean(total * total, axis=1, keepdims=True) + EPS)).astype(BF16)

    start_tokens(mid_copies)
    start_tokens(square_copies)
    save(middle, middle_out)
    save(ends_own, ends_out.at[pl.ds(0, 8)])
    save(ends_far, ends_out.at[pl.ds(8, 8)])
    complete(5)
    copy = load(5, 0)
    copy.start()
    copy.wait()
    mid_copies[0].wait_recv()

    def left_rows(row):
        at = pl.ds(row * row_len, row_len)
        left[at] = jnp.dot(mid[at], large_w[...], preferred_element_type=F32).astype(BF16)

    left_rows(0)
    pass_tokens(mid_copies)
    start_line(7)
    start_own(6)
    start_own(7)
    for copy in cot_loads:
        copy.wait()
    cot_kept = pltpu.make_async_copy(cot_own, cot_out.at[rows(0)], token_sem.at[2])
    cot_kept.start()
    start_tokens(cot_copies)
    forward_plane(6)
    pass_tokens(square_copies)
    mid_copies[2].wait_recv()
    left_rows(1)
    end_tokens(square_copies)
    save(square_all, square_out)
    save(mid, mid_out)
    save(left, left_out)
    complete(6)
    copy = load(6, 0)
    copy.start()
    copy.wait()

    def right_rows(n, carry):
        at = pl.ds(pl.multiple_of(n * row_len, row_len), row_len)
        total = jnp.dot(mid[at], large_w[...], preferred_element_type=F32)
        right[at] = total.astype(BF16)
        product[at] = (left[at].astype(F32) * total).astype(BF16)
        return carry

    start_plane(7)
    lax.fori_loop(0, 2, right_rows, 0)
    save(right, right_out)
    save(product, product_out)
    pass_tokens(cot_copies)
    forward_plane(7)
    end_tokens(cot_copies)
    cot_kept.wait()
    saves[0].wait()
    sent_tokens(normed_copies)
    copy = pltpu.make_async_copy(cot_out, normed, token_sem.at[0])
    copy.start()
    copy.wait()

    def down_rows(n, carry):
        at = pl.ds(pl.multiple_of(n * row_len, row_len), row_len)
        filled[...] = lax.dot_general(
            normed[:, at], product[...], (((0,), (0,)), ((), ())), preferred_element_type=F32
        ).astype(BF16)
        copy = pltpu.make_async_copy(filled, big_grad.at[0, at], token_sem.at[1])
        copy.start()
        copy.wait()
        return carry

    lax.fori_loop(0, features // row_len, down_rows, 0)
    complete(7)
    for copies in (cot_copies, mid_copies, square_copies):
        sent_tokens(copies)
    for copy in (square_near, square_diag, square_pair, part_near, part_diag, part_pair):
        copy.wait_send()
    for i in range(8):
        for k in (1, 2, 3):
            line_copy(i, k).wait_send()
        for k in range(LINE):
            for copy in first(i, k):
                copy.wait_send()
        for copy in second(i):
            copy.wait_send()
    for copy in saves[1:]:
        copy.wait()


def pieces_of(wide, features):
    size = features // wide
    if size % HEAD_DIM:
        return [(0, 0, features)]
    places = [(w, (w // 16 * 4 + w % 4) * LINE + w // 4 % LINE) for w in range(wide)]
    return [(whole * size, kept * size, size) for whole, kept in places]


def split_refs(refs, counts):
    parts, at = [], 0
    for count in counts:
        parts.append(refs[at : at + count])
        at += count
    return parts


def forward(wide, weights, cot, x, lengths):
    small, large = weights[0].shape[1] // 2, weights[5].shape[1] // 2
    quarter, features = x.shape
    tokens, row_len, heads = 4 * quarter, 2 * quarter, small // HEAD_DIM
    steps = wide.bit_length() - 1
    anywhere = pl.BlockSpec(memory_space=pl.ANY)
    dma = pltpu.SemaphoreType.DMA
    outs = [
        ((features, 2 * small), BF16),
        ((features, 2 * small), BF16),
        ((features, small), BF16),
        ((features, large), BF16),
        ((features, large), BF16),
        ((features, large), BF16),
        ((tokens, features), BF16),
        ((tokens, features), BF16),
        ((tokens, small), BF16),
        ((tokens, small), BF16),
        ((tokens, small), BF16),
        ((tokens, small), BF16),
        ((tokens, small), BF16),
        ((tokens, small), BF16),
        ((tokens, small), BF16),
        ((2, heads, row_len, row_len), BF16),
        ((quarter, features), F32),
        ((tokens, features), BF16),
        ((tokens, large), BF16),
        ((tokens, large), BF16),
        ((tokens, large), BF16),
        ((tokens, HEAD_DIM), F32),
        ((16, row_len), F32),
        ((3, features, large), BF16),
    ]
    held = [
        ((tokens, features), BF16),
        ((2, features, small), BF16),
        ((tokens, small), BF16),
        ((tokens, small), BF16),
        ((tokens, small), BF16),
        ((tokens, small), BF16),
        ((tokens, small), BF16),
        ((tokens, small), BF16),
        ((tokens, small), BF16),
        ((2, heads, row_len, row_len), BF16),
        ((tokens, small), BF16),
        ((tokens, features), BF16),
        ((row_len, features), BF16),
        ((quarter, features), BF16),
        ((tokens, HEAD_DIM), F32),
        ((row_len, HEAD_DIM), F32),
        ((quarter, HEAD_DIM), F32),
        ((tokens, HEAD_DIM), F32),
        ((8, row_len), F32),
        ((tokens, features), BF16),
        ((quarter, features), F32),
        ((features, large), BF16),
        ((tokens, large), BF16),
        ((tokens, large), BF16),
        ((tokens, large), BF16),
        ((quarter, features), BF16),
        ((8, row_len), F32),
        ((row_len, large), BF16),
        ((quarter, features), BF16),
        ((5, features // wide, small), BF16),
        ((3, features // wide, large), BF16),
    ]
    sems = [
        (8, 3), (8, 3), (2, 8), (8, 6 + steps), (8, 6 + steps), (8,), (17,), (3,), (4, 3), (4, 3), (7,), (7,),
        (2, len(pieces_of(wide, features))),
    ]
    return pl.pallas_call(
        functools.partial(forward_kernel, wide, small, large),
        out_shape=[jax.ShapeDtypeStruct(s, t) for s, t in outs],
        in_specs=[anywhere] * 10 + [pl.BlockSpec(memory_space=pltpu.SMEM)],
        out_specs=[anywhere] * len(outs),
        scratch_shapes=[pltpu.VMEM(s, t) for s, t in held] + [dma(s) for s in sems],
        compiler_params=pltpu.CompilerParams(
            has_side_effects=True, collective_id=1, vmem_limit_bytes=60 << 20
        ),
        cost_estimate=pl.CostEstimate(flops=0, bytes_accessed=300 << 20, transcendentals=0),
    )(*weights, cot, x, lengths)


def backward_kernel(wide, small, large, *refs):
    (
        (cot_in, product_in, left_in, right_in, mid_in, middle_in, normed_in, gate_in, mixed_in, query_pre_in,
         key_pre_in, query_in, key_in, value_in, probs_in, square_in, ends_in, output_w, vg_w, qk_w, left_w, right_w,
         down_w, x_in, _),
        (output_out, gate_out, value_out, query_out, key_out, left_out, right_out, down_out, layer_out, input_grad_out,
         grad_middle_out,
         out_own, out_near, out_far, out_source, grad_own, grad_near, grad_far, branch_out, big_grad, big_near, big_far,
         big_line, big_more),
        (held_tokens, normed, weights, gate, mixed, query, key, value, grad_blended, grad_mixed, vg_grad, qk_grad,
         inner, inner_core, inner_sum, inner_far, inner_col, scale, ends, part_core, part_far, out_core, grad_core, own,
         middle, held, near, far, line, stage, added, filled, small_result, big_result),
        (load_sem, send, recv, line_send, line_recv, big_send, big_recv, big_line_send, big_line_recv, small_send,
         small_recv, stage_sem, result_sem, more_send, more_recv, chunk_sem, big_more_send, big_more_recv, piece_sem),
    ) = split_refs(refs, (25, 24, 34, 19))
    branch = held_tokens
    me, core, z, on_line, flip = place_of(wide)
    extra = list(range(4, wide.bit_length() - 1))
    plane_at = (me // 16) * 4 + me % 4
    others = [on_line(k)[0] for k in (1, 2, 3)] + [flip(b) for b in [0, 1] + extra]
    tokens, features = held_tokens.shape
    quarter, row_len = tokens // 4, tokens // 2
    rb = features // wide
    q = LINE * rb
    h = q // 2
    heads = small // HEAD_DIM
    near_device, far_device = (me, 1 - core), (flip(2), core)
    lower = z % 2 == 0
    widths = [min(small, large - at) for at in range(0, large, small)]
    products = [query, key, value]
    lefts = [gate, mixed, grad_blended]
    rights = [grad_mixed, vg_grad.at[:, pl.ds(0, small)], vg_grad.at[:, pl.ds(small, small)]]

    def remote(source, target, send_sem, recv_sem, device):
        return pltpu.make_async_remote_copy(
            src_ref=source, dst_ref=target, send_sem=send_sem, recv_sem=recv_sem,
            device_id=device, device_id_type=pl.DeviceIdType.MESH,
        )

    def block(m):
        return pl.multiple_of((plane_at ^ m) * q, q)

    def rows(b):
        return pl.ds(b * quarter, quarter)

    def loops(count, body):
        def step(n, carry):
            body(n)
            return carry

        lax.fori_loop(0, count, step, 0)

    pending = {}

    def load(name, source, target):
        copy = pltpu.make_async_copy(source, target, load_sem.at[len(pending)])
        copy.start()
        pending[name] = copy

    def load_cut(name, source, targets):
        for n, target in enumerate(targets):
            load(name + str(n), source.at[:, pl.ds(n * small, widths[n])], target.at[:, pl.ds(0, widths[n])])

    def ready(*names):
        for name in names:
            pending[name].wait()

    def ready_cut(name):
        ready(*(name + str(n) for n in range(len(widths))))

    results = []

    def give(source, target):
        copy = pltpu.make_async_copy(source, target, result_sem.at[len(results)])
        copy.start()
        results.append(copy)
        return len(results) - 1

    def given(n):
        if results[n] is not None:
            results[n].wait()
            results[n] = None

    load("cot", cot_in, held_tokens)
    load_cut("product", product_in, products)
    load_cut("down", down_w, [held.at[n] for n in range(3)])
    load_cut("right", right_in, rights)
    load_cut("left", left_in, lefts)
    load("mid", mid_in, normed)
    load("middle", middle_in, middle)
    load("own", cot_in.at[rows(0)], own)
    load("square", square_in, scale)
    load("ends", ends_in, ends)
    for r in range(2):
        for n in range(heads):
            load("probs%d%d" % (r, n), probs_in.at[r, n], held.at[3 + r, pl.ds(n * row_len, row_len)])
    meet([(other, core) for other in others] + [(me, 1 - core)])


    def rows_at(i, start, size):
        return held.at[i, pl.ds(pl.multiple_of(start, min(size, rb)), size)]

    def step(i, j, start, size, target, bit):
        return remote(rows_at(i, start, size), target, send.at[i, j], recv.at[i, j], (flip(bit), core))

    apart = pl.multiple_of((1 - z // 2) * h, h)
    beside = pl.multiple_of(z // 2 * h + (1 - z % 2) * rb, rb)
    at_z = pl.multiple_of(z * rb, rb)

    def copies(i, j):
        if j == 0:
            return step(i, 0, block(3) + apart, h, near.at[i, 0], 1)
        if j == 1:
            return step(i, 1, block(3) + beside, rb, near.at[i, 1, pl.ds(0, rb)], 0)
        if j == 2:
            return step(i, 2, block(1) + beside, rb, far.at[i, 0, pl.ds(beside, rb)], 0)
        if j == 3:
            return step(i, 3, block(2) + apart, h, far.at[i, 1, pl.ds(apart, h)], 1)
        if j == 4:
            return step(i, 4, block(1) + apart, h, far.at[i, 0, pl.ds(apart, h)], 0)
        if j == 5:
            return step(i, 5, block(2) + beside, rb, far.at[i, 1, pl.ds(beside, rb)], 1)
        if j == 6:
            return step(i, 6, block(3) + at_z, rb, near.at[i, 1, pl.ds(rb, rb)], 0)
        if j == 7:
            return step(i, 7, block(1) + at_z, rb, far.at[i, 0, pl.ds(at_z, rb)], 0)
        return step(i, 8, block(2) + at_z, rb, far.at[i, 1, pl.ds(at_z, rb)], 1)

    def line_copy(i, k):
        device, there = on_line(k)
        return remote(
            rows_at(i, block(0) + there * rb, rb), line.at[i, k - 1],
            line_send.at[i, k - 1], line_recv.at[i, k - 1], (device, core),
        )

    tile = min(64, rb)

    def add(target, start, size, *sources):
        def body(n):
            at = pl.ds(pl.multiple_of(start + n * tile, tile), tile)
            total = target[at].astype(F32)
            for source in sources:
                total = total + source[pl.ds(pl.multiple_of(n * tile, tile), tile)].astype(F32)
            target[at] = total.astype(BF16)

        loops(size // tile, body)

    def begin(i, side, other):
        def fill(m):
            held[i, pl.ds(block(m), q)] = lax.dot_general(
                side[:, pl.ds(block(m), q)], other(), (((0,), (0,)), ((), ())), preferred_element_type=F32
            ).astype(BF16)

        if extra:
            loops(wide // LINE, fill)
            for e in reversed(range(len(extra))):
                size = q << (2 + e)
                half = plane_at >> (2 + e)
                copy = remote(
                    rows_at(i, (half ^ 1) * size, size), branch_more(i, e, size),
                    more_send.at[i, e], more_recv.at[i, e], (flip(extra[e]), core),
                )
                copy.start()
                copy.wait()
                add(held.at[i], half * size, size, branch_more(i, e, size))
            for j in range(4):
                copies(i, j).start()
            if i < LATE:
                begin_own(i)
        else:
            fill(3)
            copies(i, 0).start()
            copies(i, 1).start()
            fill(1)
            copies(i, 2).start()
            fill(2)
            copies(i, 3).start()
            if i < LATE:
                begin_own(i)
            fill(0)

    def branch_more(i, e, size):
        return far.at[i, e, pl.ds(0, size)]

    def fold(i):
        copies(i, 0).wait_recv()
        add(held.at[i], block(1) + apart, h, near.at[i, 0])
        copies(i, 4).start()
        copies(i, 1).wait_recv()
        add(held.at[i], block(2) + beside, rb, near.at[i, 1, pl.ds(0, rb)])
        copies(i, 5).start()

    def begin_own(i):
        copies(i, 6).start()
        copies(i, 7).start()

    def fold_own(i):
        copies(i, 6).wait_recv()
        add(held.at[i], block(2) + at_z, rb, near.at[i, 1, pl.ds(rb, rb)])
        copies(i, 8).start()

    def to_line(i):
        for j in range(2, 6):
            copies(i, j).wait_recv()
        for start, size in ((apart, h), (beside, rb)):
            here = pl.ds(start, size)
            add(held.at[i], block(0) + start, size, far.at[i, 0, here], far.at[i, 1, here])
        for k in (1, 2, 3):
            line_copy(i, k).start()

    def finish(i, out):
        for j in (7, 8):
            copies(i, j).wait_recv()
        here = pl.ds(at_z, rb)
        add(held.at[i], block(0) + at_z, rb, far.at[i, 0, here], far.at[i, 1, here])
        for k in (1, 2, 3):
            line_copy(i, k).wait_recv()
        own_sum = held[i, pl.ds(pl.multiple_of(block(0) + at_z, rb), rb)].astype(F32) + line[i, 1].astype(F32)
        other = line[i, 0].astype(F32) + line[i, 2].astype(F32)
        if small_done:
            given(small_done[-1])
        put(small_result, own_sum, other, small)
        small_done.append(give(small_result, out))

    small_done = []

    def put(target, own, other, cols):
        @pl.when(lower)
        def _():
            target[:, pl.ds(0, cols)] = own
            target[:, pl.ds(cols, cols)] = other

        @pl.when(jnp.logical_not(lower))
        def _():
            target[:, pl.ds(0, cols)] = other
            target[:, pl.ds(cols, cols)] = own


    def big_rows(n, start, size):
        return big_grad.at[n, pl.ds(pl.multiple_of(start, min(size, rb)), size)]

    def big_copy(n, j):
        if j == 0:
            source, target = big_rows(n, block(3), h), big_near.at[n, 0]
        elif j == 1:
            source, target = big_rows(n, block(3) + h, h), big_near.at[n, 1]
        elif j == 2:
            source, target = big_rows(n, block(1) + h, h), big_far.at[n, 0, pl.ds(h, h)]
        elif j == 3:
            source, target = big_rows(n, block(2), h), big_far.at[n, 1, pl.ds(0, h)]
        elif j == 4:
            source, target = big_rows(n, block(1), h), big_far.at[n, 0, pl.ds(0, h)]
        else:
            source, target = big_rows(n, block(2) + h, h), big_far.at[n, 1, pl.ds(h, h)]
        bit = (1, 0, 0, 1, 0, 1)[j]
        return remote(source, target, big_send.at[n, j], big_recv.at[n, j], (flip(bit), core))

    def big_line_copy(n, k):
        device, there = on_line(k)
        return remote(
            big_rows(n, block(0) + there * rb, rb), big_line.at[n, k - 1],
            big_line_send.at[n, k - 1], big_line_recv.at[n, k - 1], (device, core),
        )

    def move(j, source, target):
        copy = pltpu.make_async_copy(source, target, stage_sem.at[j])
        copy.start()
        return copy

    def big_add(n, start, *sources):
        moves = [move(0, big_rows(n, start, h), stage.at[pl.ds(0, h)])]
        for j, source in enumerate(sources):
            moves.append(move(1 + j, source, added.at[pl.ds(j * h, h)]))
        for copy in moves:
            copy.wait()
        add(stage, 0, h, *(added.at[pl.ds(j * h, h)] for j in range(len(sources))))
        move(0, stage.at[pl.ds(0, h)], big_rows(n, start, h)).wait()

    def big_begin(n, side=None, parts=None):
        def fill(m):
            if side is None:
                return
            for c, width in enumerate(widths):
                filled[:, pl.ds(c * small, width)] = lax.dot_general(
                    side[:, pl.ds(block(m), q)], parts[c][:, pl.ds(0, width)], (((0,), (0,)), ((), ())),
                    preferred_element_type=F32,
                ).astype(BF16)
            move(3, filled, big_rows(n, block(m), q)).wait()

        if extra:
            loops(wide // LINE, fill)
            for e in reversed(range(len(extra))):
                size = q << (2 + e)
                half = plane_at >> (2 + e)
                copy = remote(
                    big_rows(n, (half ^ 1) * size, size), big_more.at[n, e, pl.ds(0, size)],
                    big_more_send.at[n, e], big_more_recv.at[n, e], (flip(extra[e]), core),
                )
                copy.start()
                copy.wait()
                loops(
                    size // h,
                    lambda i: big_add(
                        n, half * size + i * h, big_more.at[n, e, pl.ds(pl.multiple_of(i * h, h), h)]
                    ),
                )
            for j in range(4):
                big_copy(n, j).start()
        else:
            fill(3)
            big_copy(n, 0).start()
            big_copy(n, 1).start()
            fill(1)
            big_copy(n, 2).start()
            fill(2)
            big_copy(n, 3).start()
            fill(0)

    def big_fold(n):
        big_copy(n, 0).wait_recv()
        big_add(n, block(1), big_near.at[n, 0])
        big_copy(n, 4).start()
        big_copy(n, 1).wait_recv()
        big_add(n, block(2) + h, big_near.at[n, 1])
        big_copy(n, 5).start()

    def big_to_line(n):
        for j in range(2, 6):
            big_copy(n, j).wait_recv()
        for j in range(2):
            here = pl.ds(j * h, h)
            big_add(n, block(0) + j * h, big_far.at[n, 0, here], big_far.at[n, 1, here])
        for k in (1, 2, 3):
            big_line_copy(n, k).start()

    def big_finish(n, out):
        for k in (1, 2, 3):
            big_line_copy(n, k).wait_recv()
        moves = [move(k, big_line.at[n, k], added.at[pl.ds(k * rb, rb)]) for k in range(3)]
        moves.append(move(3, big_rows(n, block(0) + z * rb, rb), added.at[pl.ds(3 * rb, rb)]))
        for copy in moves:
            copy.wait()
        if results_of_big:
            given(results_of_big[-1])
        got = [added[pl.ds(k * rb, rb)].astype(F32) for k in range(4)]
        put(big_result, got[3] + got[1], got[0] + got[2], large)
        results_of_big.append(give(big_result, out))

    results_of_big = []


    def gate_product(r):
        at = pl.ds(r * row_len, row_len)
        for c, width in enumerate(widths):
            here = pl.ds(0, width)
            total = jnp.dot(held_tokens[at], held[c, :, here], preferred_element_type=F32)
            grad_left = (total * rights[c][at, here].astype(F32)).astype(BF16)
            lefts[c][at, here] = (total * lefts[c][at, here].astype(F32)).astype(BF16)
            rights[c][at, here] = grad_left

    chunk = row_len // 2
    chunks = features // chunk
    wide_cols = 2 * small

    def chunk_copies(n, slot):
        source = pl.ds(pl.multiple_of(n * chunk, chunk), chunk)
        target = pl.ds(pl.multiple_of(slot * chunk, chunk), chunk)
        return [
            pltpu.make_async_copy(
                w.at[source, pl.ds(at, cols)], weights.at[2 * i + j, target, pl.ds(0, cols)], chunk_sem.at[slot, 2 * i + j]
            )
            for i, w in enumerate((left_w, right_w))
            for j, (at, cols) in enumerate(((0, wide_cols), (wide_cols, large - wide_cols)))
        ]

    def mid_part(r):
        at = pl.ds(r * row_len, row_len)
        for copy in chunk_copies(0, 0):
            copy.start()

        def body(n):
            slot = n % 2

            @pl.when(n + 1 < chunks)
            def _():
                for copy in chunk_copies(n + 1, 1 - slot):
                    copy.start()

            for copy in chunk_copies(n, slot):
                copy.wait()
            here = pl.ds(pl.multiple_of(slot * chunk, chunk), chunk)
            total = jnp.zeros((row_len, chunk), F32)
            for i, parts in enumerate((rights, lefts)):
                for c, width in enumerate(widths):
                    w = weights[2 * i + c // 2, here, pl.ds((c % 2) * small, width)]
                    total = total + lax.dot_general(
                        parts[c][at, pl.ds(0, width)], w, (((1,), (1,)), ((), ())), preferred_element_type=F32
                    )
            held_tokens[at, pl.ds(pl.multiple_of(n * chunk, chunk), chunk)] = total.astype(BF16)

        loops(chunks, body)

    def output_part(r):
        at = pl.ds(r * row_len, row_len)

        def body(n):
            here = pl.ds(pl.multiple_of(n * row_len, row_len), row_len)
            total = jnp.zeros((row_len, row_len), F32)
            for c, width in enumerate(widths):
                total = total + lax.dot_general(
                    products[c][at, pl.ds(0, width)], held[c, here, pl.ds(0, width)], (((1,), (1,)), ((), ())),
                    preferred_element_type=F32,
                )
            held_tokens[at, here] = total.astype(BF16)

        loops(features // row_len, body)

    def middle_rows(n):
        at = pl.ds(pl.multiple_of(n * 32, 32), 32)
        grad = held_tokens[at].astype(F32) + part_core[at].astype(F32) + part_far[at].astype(F32)
        values = middle[at]
        s = lax.rsqrt(jnp.mean(values * values, axis=1, keepdims=True) + EPS)
        grad = own[at].astype(F32) + norm_back(values, s, grad)
        middle[at] = grad
        own[at] = grad.astype(BF16)


    def grad_rows(row):
        at = pl.ds(row * row_len, row_len)
        total = jnp.zeros((row_len, small), F32)
        for n in range(4):
            total = total + jnp.dot(
                branch[at, pl.ds(n * row_len, row_len)], weights[n, :, pl.ds(0, small)], preferred_element_type=F32
            )
        grad_blended[at] = total.astype(BF16)
        m = mixed[at].astype(F32)
        g = gate[at].astype(F32)
        scaled = m * scale[at, 0:1]
        vg_grad[at, pl.ds(small, small)] = (total * scaled).astype(BF16)
        grad_mixed[at] = (g * scaled).astype(BF16)
        inner[:, at] = lax.dot_general(
            jnp.ones((8, small), F32), total * g * m, (((1,), (1,)), ((), ())),
            preferred_element_type=F32, precision=lax.Precision.HIGHEST,
        )

    def scale_rows(n):
        at = pl.ds(pl.multiple_of(n * 128, 128), 128)
        scale[at] = lax.rsqrt(scale[at] / features + EPS)

    def mix_rows(n):
        at = pl.ds(pl.multiple_of(n * 128, 128), 128)
        s = scale[at, 0:1]
        value_of = s * (grad_blended[at].astype(F32) * gate[at].astype(F32))
        value_of = value_of - mixed[at].astype(F32) * (s * s * s * (inner_col[at, 0:1] / features))
        grad_mixed[at] = value_of.astype(BF16)

    first_head = (core * 2 + z % 2) * heads

    def attend_back(row):
        at = pl.ds(row * row_len, row_len)

        def place(dim):
            index = lax.broadcasted_iota(jnp.int32, (row_len, row_len), dim) + core * quarter
            return jnp.where(index >= row_len, index - row_len, index).astype(F32)

        def slope(pre):
            s = sigmoid(pre)
            return s * (1.0 + pre * (1.0 - s))

        def body(head):
            cols = pl.ds(pl.multiple_of(head * HEAD_DIM, HEAD_DIM), HEAD_DIM)
            more = pl.ds(pl.multiple_of(small + head * HEAD_DIM, HEAD_DIM), HEAD_DIM)
            got = grad_mixed[at, cols]
            grad_probs = lax.dot_general(
                got, value[at, cols], (((1,), (1,)), ((), ())), preferred_element_type=F32
            )
            to, source = place(0), place(1)
            allowed = (to >= source) & (to < ends[pl.ds(8 * row, 1), :])
            rate = (first_head + head).astype(F32) * (DECAY * HEAD_DIM / features)
            decay = jnp.where(allowed, jnp.exp(-rate * jnp.maximum(to - source, 0.0)), 0.0)
            grad_scores = (grad_probs * decay).astype(BF16)
            probs = held[3 + row, pl.ds(pl.multiple_of(head * row_len, row_len), row_len)]
            vg_grad[at, cols] = lax.dot_general(
                probs, got, (((0,), (0,)), ((), ())), preferred_element_type=F32
            ).astype(BF16)
            grad_query = jnp.dot(grad_scores, key[at, cols], preferred_element_type=F32)
            qk_grad[at, cols] = (grad_query * slope(gate[at, cols].astype(F32))).astype(BF16)
            grad_key = lax.dot_general(
                grad_scores, query[at, cols], (((0,), (0,)), ((), ())), preferred_element_type=F32
            )
            qk_grad[at, more] = (grad_key * slope(mixed[at, cols].astype(F32))).astype(BF16)

        loops(heads, body)

    def load_weights(pair):
        for n in range(2):
            here = pl.ds((2 * pair + n) * row_len, row_len)
            load("vg%d%d" % (pair, n), vg_w.at[here], weights.at[n])
            load("qk%d%d" % (pair, n), qk_w.at[here], weights.at[2 + n])

    def normed_part(pair, row):
        at = pl.ds(row * row_len, row_len)
        for n in range(2):
            total = lax.dot_general(vg_grad[at], weights[n], (((1,), (1,)), ((), ())), preferred_element_type=F32)
            total = total + lax.dot_general(
                qk_grad[at], weights[2 + n], (((1,), (1,)), ((), ())), preferred_element_type=F32
            )
            branch[at, pl.ds((2 * pair + n) * row_len, row_len)] = total.astype(BF16)

    def small_copy(n, source, target, device):
        return remote(source, target, small_send.at[n], small_recv.at[n], device)

    pieces = pieces_of(wide, features)

    def layer_rows(n):
        at = pl.ds(pl.multiple_of(n * 32, 32), 32)
        total = middle[at] + own[at].astype(F32) + part_core[at].astype(F32) + part_far[at].astype(F32)
        own[at] = total.astype(BF16)

    def input_rows(n):
        at = pl.ds(pl.multiple_of(n * 32, 32), 32)
        grad = own[at].astype(F32) + part_core[at].astype(F32) + part_far[at].astype(F32)
        values = part_core[pl.ds(pl.multiple_of(quarter + n * 32, 32), 32)].astype(F32)
        s = lax.rsqrt(jnp.mean(values * values, axis=1, keepdims=True) + EPS)
        middle[at] = middle[at] + norm_back(values, s, grad)

    def put_pieces(row, source, target):
        copies = [
            pltpu.make_async_copy(source.at[:, pl.ds(b, size)], target.at[:, pl.ds(a, size)], piece_sem.at[row, n])
            for n, (a, b, size) in enumerate(pieces)
        ]
        for copy in copies:
            copy.start()
        return copies


    big_begin(0)
    ready("cot")
    ready_cut("product")
    ready_cut("down")
    ready_cut("left")
    ready_cut("right")
    gate_product(1)
    gate_product(0)
    mid_part(1)
    part_diag = small_copy(0, held_tokens.at[rows(3)], part_core.at[rows(1)], near_device)
    part_near = small_copy(1, held_tokens.at[rows(1)], part_core.at[rows(0)], near_device)
    part_pair = small_copy(2, held_tokens.at[rows(2)], part_far, far_device)
    part_diag.start()
    part_diag.wait_recv()
    add(held_tokens, 2 * quarter, quarter, part_core.at[rows(1)])
    part_pair.start()
    big_fold(0)
    mid_part(0)
    part_near.start()
    ready("mid")
    big_begin(1, normed, rights)
    ready("middle", "own")
    part_near.wait_recv()
    part_pair.wait_recv()
    loops(quarter // 32, middle_rows)
    branch_own = move(4, own, branch_out.at[rows(0)])
    branch_near = small_copy(3, own, branch_out.at[rows(1)], near_device)
    branch_far = small_copy(4, own, branch_out.at[rows(2)], far_device)
    branch_pass = small_copy(5, branch_out.at[rows(2)], branch_out.at[rows(3)], near_device)
    branch_far.start()
    branch_near.start()
    middle_given = give(middle, grad_middle_out)
    for n in range(4):
        load("output%d" % n, output_w.at[pl.ds(n * row_len, row_len)], weights.at[n, :, pl.ds(0, small)])
    big_to_line(0)
    big_begin(2, normed, lefts)
    load("gate", gate_in, gate)
    load("mixed", mixed_in, mixed)
    load("normed", normed_in, normed)
    big_fold(1)
    for copy in (part_diag, part_near, part_pair):
        copy.wait_send()
    output_part(1)
    out_diag = small_copy(6, held_tokens.at[rows(3)], out_core, near_device)
    out_diag.start()
    output_part(0)
    out_next = small_copy(7, held_tokens.at[rows(1)], out_near, near_device)
    out_next.start()
    out_mine = move(5, held_tokens.at[rows(0)], out_own)
    out_diag.wait_recv()
    add(held_tokens, 2 * quarter, quarter, out_core)
    out_pair = small_copy(8, out_source, out_far, far_device)
    move(0, held_tokens.at[rows(2)], out_source).wait()
    out_pair.start()
    load("value", value_in, value)
    load("query", query_in, query)
    load("key", key_in, key)
    out_mine.wait()
    out_next.wait_send()
    out_diag.wait_send()
    branch_own.wait()
    branch_near.wait_recv()
    load("branch0", branch_out.at[pl.ds(0, row_len)], branch.at[pl.ds(0, row_len)])
    ready("square")
    loops(tokens // 128, scale_rows)
    branch_far.wait_recv()
    branch_pass.start()
    ready("branch0", "output0", "output1", "output2", "output3", "gate", "mixed")
    grad_rows(0)
    branch_pass.wait_recv()
    load("branch1", branch_out.at[pl.ds(row_len, row_len)], branch.at[pl.ds(row_len, row_len)])
    ready("branch1")
    grad_rows(1)
    core_copy = small_copy(9, inner, inner_core, near_device)
    core_copy.start()
    core_copy.wait_recv()
    for b in range(4):
        inner_sum[:, rows(b)] = inner[:, rows(b)] + inner_core[:, rows(b ^ 1)]
    far_copy = small_copy(10, inner_sum, inner_far, far_device)
    far_copy.start()
    begin(0, branch, lambda: grad_mixed[...])
    far_copy.wait_recv()
    for b in range(4):
        total = inner_sum[:, rows(b)] + inner_far[:, rows(b ^ 2)]
        inner_col[rows(b)] = jnp.broadcast_to(total.T[:, 0:1], (quarter, HEAD_DIM))
    loops(tokens // 128, mix_rows)
    load("query_pre", query_pre_in, gate)
    load("key_pre", key_pre_in, mixed)
    load_weights(0)
    ready("normed")
    begin(1, normed, lambda: vg_grad[:, pl.ds(small, small)])
    big_to_line(1)
    big_fold(2)
    ready("value", "query", "key", "query_pre", "key_pre", "ends")
    for r in range(2):
        ready(*("probs%d%d" % (r, n) for n in range(heads)))
    attend_back(1)
    fold(0)
    fold_own(0)
    attend_back(0)
    begin(2, normed, lambda: vg_grad[:, pl.ds(0, small)])
    fold(1)
    fold_own(1)
    begin(3, normed, lambda: qk_grad[:, pl.ds(0, small)])
    begin(4, normed, lambda: qk_grad[:, pl.ds(small, small)])
    big_to_line(2)
    to_line(0)
    fold(2)
    ready("vg00", "vg01", "qk00", "qk01")
    normed_part(0, 1)
    normed_part(0, 0)
    load_weights(1)
    big_finish(0, down_out)
    to_line(1)
    ready("vg10", "vg11", "qk10", "qk11")
    normed_part(1, 1)
    grad_diag = small_copy(11, branch.at[rows(3)], grad_core, near_device)
    grad_next = small_copy(12, branch.at[rows(1)], grad_near, near_device)
    grad_pair = small_copy(13, branch.at[rows(2)], grad_far, far_device)
    grad_diag.start()
    normed_part(1, 0)
    grad_next.start()
    grad_given = give(branch.at[rows(0)], grad_own)
    grad_diag.wait_recv()
    add(branch, 2 * quarter, quarter, grad_core)
    grad_pair.start()
    fold(3)
    fold(4)
    for i in range(LATE, 5):
        begin_own(i)
    big_finish(1, left_out)
    given(middle_given)
    branch_near.wait_send()
    branch_far.wait_send()
    out_next.wait_recv()
    out_pair.wait_recv()
    load("middle2", middle_in, middle)
    load("out_own", out_own, own)
    load("out_near", out_near, part_core.at[rows(0)])
    load("out_far", out_far, part_far)
    to_line(2)
    ready("middle2", "out_own", "out_near", "out_far")
    loops(quarter // 32, layer_rows)
    layer_pieces = put_pieces(0, own, layer_out)
    load("middle3", grad_middle_out, middle)
    x_copies = [
        pltpu.make_async_copy(x_in.at[:, pl.ds(a, size)], part_core.at[rows(1), pl.ds(b, size)], piece_sem.at[1, n])
        for n, (a, b, size) in enumerate(pieces)
    ]
    for copy in x_copies:
        copy.start()
    finish(0, output_out)
    finish(1, gate_out)
    to_line(3)
    fold_own(2)
    big_finish(2, right_out)
    to_line(4)
    fold_own(3)
    fold_own(4)
    for copy in layer_pieces:
        copy.wait()
    given(grad_given)
    grad_next.wait_recv()
    grad_pair.wait_recv()
    load("grad_own", grad_own, own)
    load("grad_near", grad_near, part_core.at[rows(0)])
    load("grad_far", grad_far, part_far)
    for copy in x_copies:
        copy.wait()
    ready("middle3", "grad_own", "grad_near", "grad_far")
    loops(quarter // 32, input_rows)
    grad_pieces = put_pieces(2, middle, input_grad_out)
    finish(2, value_out)
    finish(3, query_out)
    finish(4, key_out)
    for copy in grad_pieces:
        copy.wait()
    for copy in (branch_pass, out_pair, core_copy, far_copy, grad_diag, grad_next, grad_pair):
        copy.wait_send()
    for i in range(5):
        for j in range(9):
            copies(i, j).wait_send()
        for k in (1, 2, 3):
            line_copy(i, k).wait_send()
    for n in range(3):
        for j in range(6):
            big_copy(n, j).wait_send()
        for k in (1, 2, 3):
            big_line_copy(n, k).wait_send()
    for n in range(len(results)):
        given(n)


def backward(wide, arrays, small, large):
    tokens, features = arrays[0].shape
    quarter, row_len = tokens // 4, tokens // 2
    rb = features // wide
    q = LINE * rb
    extra = max(1, wide.bit_length() - 5)
    anywhere = pl.BlockSpec(memory_space=pl.ANY)
    dma = pltpu.SemaphoreType.DMA
    many = features // 2 if wide > 16 else 16
    far_rows = max(q, many)
    part = (quarter, features)
    outs = [((rb, 2 * small), F32)] * 5 + [((rb, 2 * large), F32)] * 3 + [
        (part, BF16),
        (part, F32),
        (part, F32),
        *[(part, BF16)] * 7,

        ((tokens, features), BF16),
        ((3, features, large), BF16),
        ((3, 2, q // 2, large), BF16),
        ((3, 2, q, large), BF16),
        ((3, 3, rb, large), BF16),
        ((3, extra, many, large), BF16),
    ]
    held = [
        ((tokens, features), BF16),
        ((tokens, features), BF16),
        ((4, row_len, 2 * small), BF16),
        *[((tokens, small), BF16)] * 7,
        ((tokens, 2 * small), BF16),
        ((tokens, 2 * small), BF16),
        *[((8, tokens), F32)] * 4,
        ((tokens, HEAD_DIM), F32),
        ((tokens, HEAD_DIM), F32),
        ((16, row_len), F32),
        ((row_len, features), BF16),
        *[(part, BF16)] * 4,
        (part, F32),
        ((5, features, small), BF16),
        ((5, 2, q // 2, small), BF16),
        ((5, 2, far_rows, small), BF16),
        ((5, 3, rb, small), BF16),
        ((q // 2, large), BF16),
        ((q, large), BF16),
        ((q, large), BF16),
        ((rb, 2 * small), F32),
        ((rb, 2 * large), F32),
    ]
    sems = [
        (60,), (5, 9), (5, 9), (5, 3), (5, 3), (3, 6), (3, 6), (3, 3), (3, 3), (14,), (14,), (6,), (10,), (5, extra),
        (5, extra), (2, 4), (3, extra), (3, extra), (3, len(pieces_of(wide, features))),
    ]
    return pl.pallas_call(
        functools.partial(backward_kernel, wide, small, large),
        out_shape=[jax.ShapeDtypeStruct(s, t) for s, t in outs],
        in_specs=[anywhere] * len(arrays),
        out_specs=[anywhere] * len(outs),
        scratch_shapes=[pltpu.VMEM(s, t) for s, t in held] + [dma(s) for s in sems],
        input_output_aliases={24: 19},
        compiler_params=pltpu.CompilerParams(
            has_side_effects=True, collective_id=2, vmem_limit_bytes=60 << 20
        ),
        cost_estimate=pl.CostEstimate(flops=0, bytes_accessed=300 << 20, transcendentals=0),
    )(*arrays)


def sigmoid(z):
    return 1.0 / (1.0 + jnp.exp(-z))


def on_device(
    layer_input, doc_lengths, w_query, w_key, w_value, w_gate, w_output, w_left, w_right, w_down, cotangent, *, wide
):
    features = layer_input.shape[1]
    cut = len(pieces_of(wide, features)) == 1
    x = to_kept(layer_input, wide) if cut else layer_input
    cot = to_kept(cotangent, wide) if cut else cotangent
    weights = [w_query, w_key, w_value, w_gate, w_output, w_left, w_right, w_down]
    (
        qk_w, vg_w, output_w, left_w, right_w, down_w, normed, cot_all, query_pre, key_pre, gate, queries, keys, values,
        mixed, probs, middle, mid, left, right, product, squares, ends, big_grad,
    ) = forward(wide, weights, cot, x, doc_lengths)
    (
        grad_output, grad_gate, grad_value, grad_query, grad_key, grad_left, grad_right, grad_down, layer_output,
        input_grad, *_
    ) = backward(
        wide,
        [
            cot_all, product, left, right, mid, middle, normed, gate, mixed, query_pre, key_pre, queries, keys, values,
            probs, squares, ends, output_w, vg_w, qk_w, left_w, right_w, down_w, x, big_grad,
        ],
        queries.shape[1],
        left.shape[1],
    )
    results = copied(
        [
            layer_output, input_grad, grad_query, grad_key, grad_value, grad_gate, grad_output, grad_left, grad_right,
            grad_down,
        ]
    )
    if cut:
        return tuple(from_kept(value, wide) for value in results[:2]) + tuple(results[2:])
    return tuple(results)


def copy_kernel(count, *refs):
    sources, targets, held = refs[:count], refs[count : 2 * count], refs[2 * count : 3 * count]
    load_sem, store_sem = refs[3 * count :]
    loads = [pltpu.make_async_copy(sources[i], held[i], load_sem.at[i]) for i in range(count)]
    stores = [pltpu.make_async_copy(held[i], targets[i], store_sem.at[i]) for i in range(count)]
    for copy in loads:
        copy.start()
    for load, store in zip(loads, stores):
        load.wait()
        store.start()
    for copy in stores:
        copy.wait()


def copied(arrays):
    anywhere = pl.BlockSpec(memory_space=pl.ANY)
    count = len(arrays)
    return pl.pallas_call(
        functools.partial(copy_kernel, count),
        out_shape=[jax.ShapeDtypeStruct(a.shape, a.dtype) for a in arrays],
        in_specs=[anywhere] * count,
        out_specs=[anywhere] * count,
        scratch_shapes=[pltpu.VMEM(a.shape, a.dtype) for a in arrays] + [pltpu.SemaphoreType.DMA((count,))] * 2,
        compiler_params=pltpu.CompilerParams(vmem_limit_bytes=60 << 20),
    )(*arrays)


def solution(mesh):
    both, weight = P(("wide", "narrow"), None), P("wide", "narrow")
    wide = mesh.shape["wide"]

    def body(*args):
        return on_device(*args, wide=wide)

    return jax.shard_map(
        body,
        mesh=mesh,
        in_specs=(both, P("wide", None)) + (weight,) * 8 + (both,),
        out_specs=(both, both) + (weight,) * 8,
        check_vma=False,
    )
```
